128 devices in a mesh: lat: 16 (over y, x), blk: 8 (over z, core).
Axes of the slice: x: 4, y: 4, z: 4, core: 2. Of those that a mesh axis runs over, the one named last changes fastest.
Arguments:
- mesh_nodes: bfloat16 [40960, 512], P(('lat', 'blk')), may hold values from -6 to 6
- coarse_nodes: bfloat16 [640, 512], replicated, may hold values from -6 to 6
- edge_latents: bfloat16 [262144, 512], P(('lat', 'blk')), may hold values from -6 to 6
- edge_tiles: int32 [2048, 2, 128], P(('lat', 'blk')), may hold values from 0 to 1023, as said below
- send_lists: int32 [128, 8, 8], P(('lat', 'blk')), may hold values from 0 to 319
- tiles_live: int32 [128], P(('lat', 'blk')), may hold values from 1 to 16, as said below
- edge_in: bfloat16 [3, 512, 512], replicated, may hold values from -0.15625 to 0.15625
- edge_out: bfloat16 [512, 512], replicated, may hold values from -0.25 to 0.25
- edge_gain: float32 [512], replicated, may hold values from 0.1 to 1.9
- node_in: bfloat16 [2, 512, 512], replicated, may hold values from -0.1875 to 0.1875
- node_out: bfloat16 [512, 512], replicated, may hold values from -0.25 to 0.25
- node_gain: float32 [512], replicated, may hold values from 0.1 to 1.9
- grad_nodes: bfloat16 [40960, 512], P(('lat', 'blk')), may hold values from -6 to 6
- grad_coarse: bfloat16 [640, 512], replicated, may hold values from -6 to 6
- grad_edges: bfloat16 [262144, 512], P(('lat', 'blk')), may hold values from -6 to 6
Outputs:
- new_nodes: bfloat16 [40960, 512], P(('lat', 'blk'))
- new_coarse: bfloat16 [640, 512], replicated
- new_edges: bfloat16 [262144, 512], P(('lat', 'blk'))
- nodes_grad: bfloat16 [40960, 512], P(('lat', 'blk'))
- coarse_grad: bfloat16 [640, 512], replicated
- edges_grad: bfloat16 [262144, 512], P(('lat', 'blk'))
- edge_in_grad: bfloat16 [3, 512, 512], replicated
- edge_out_grad: bfloat16 [512, 512], replicated
- edge_gain_grad: float32 [512], replicated
- node_in_grad: bfloat16 [2, 512, 512], replicated
- node_out_grad: bfloat16 [512, 512], replicated
- node_gain_grad: float32 [512], replicated
The draws below stay inside these ranges and needn't reach their ends.
Inputs may be any that keep to these rules, and one draw needn't show every extreme that they name: `edge_tiles`: sender entries lie below 1024, receiver entries below 960. `send_lists`: numbers of nodes within the sending block. `tiles_live`: some block has all 16 tiles live.
All inputs are finite; a program needn't handle non-finite values.
Results may differ from the reference program's by a relative error of at most 0.0095.
Values may be sent and summed in bfloat16 or wider, within the bound.
No kernel may reach another device: no remote copies, remote signals or barrier semaphores. Data moves between devices by JAX's collectives and lax.ppermute only.
A program may use at most 192 MiB of HBM per device.

```python
import jax
import jax.numpy as jnp
from jax import lax

D = 512
NODE_DEV = 320
TILE_DEV = 16
SLOTS = 8
NEIGH = 8
TILE = 128
COARSE = 640
BLOCKS = 128
NODES = 40960
TILES = 2048
EDGES = 262144


def draw_edge_tiles(key, part):
    tile_shape = (TILES, TILE)
    subkeys = jax.random.split(jax.random.fold_in(key, 11), 7)
    sender_kind = jax.random.randint(subkeys[0], tile_shape, 0, 20)
    own_ids = jax.random.randint(subkeys[1], tile_shape, 0, NODE_DEV)
    halo_ids = NODE_DEV + jax.random.randint(subkeys[2], tile_shape, 0, NEIGH * SLOTS)
    coarse_ids = NODE_DEV + NEIGH * SLOTS + jax.random.randint(subkeys[3], tile_shape, 0, COARSE)
    senders = jnp.where(sender_kind < 10, own_ids, jnp.where(sender_kind < 17, halo_ids, coarse_ids))
    receiver_kind = jax.random.randint(subkeys[4], tile_shape, 0, 10)
    target_own = jax.random.randint(subkeys[5], tile_shape, 0, NODE_DEV)
    target_coarse = NODE_DEV + jax.random.randint(subkeys[6], tile_shape, 0, COARSE)
    receivers = jnp.where(receiver_kind < 9, target_own, target_coarse)
    return jnp.stack([senders, receivers], axis=1).astype(jnp.int32)


def draw_tiles_live(key, part):
    subkeys = jax.random.split(jax.random.fold_in(key, 23), 3)
    full_flag = jax.random.randint(subkeys[0], (BLOCKS,), 0, 8) == 0
    chosen = jax.random.randint(subkeys[1], (), 0, BLOCKS)
    partial_count = jax.random.randint(subkeys[2], (BLOCKS,), TILE_DEV // 2, TILE_DEV + 1)
    is_full = full_flag | (jnp.arange(BLOCKS) == chosen)
    return jnp.where(is_full, TILE_DEV, partial_count).astype(jnp.int32)


def plant(result, rng, smallest, largest):
    extent = result.shape
    spot = [jax.random.randint(jax.random.fold_in(rng, axis), (), 0, extent[axis]) for axis in range(len(extent))]
    result = result.at[tuple(spot)].set(smallest)
    longest = extent.index(max(extent))
    spot[longest] = (spot[longest] + 1) % extent[longest]
    return result.at[tuple(spot)].set(largest)


def shard_levels(key, extent, pieces, low, largest):
    def one(dim, parts):
        heights = jax.random.uniform(jax.random.fold_in(jax.random.fold_in(key, 6), dim), (parts,), jnp.float32, low / len(pieces), largest / len(pieces))
        return jnp.repeat(jnp.exp(heights), extent[dim] // parts).reshape((-1,) + (1,) * (len(extent) - dim - 1))

    loudness = one(*pieces[0])
    for cut in pieces[1:]:
        loudness = loudness * one(*cut)
    return loudness


def scatter_about(own_key, dims, deviation, reach, pieces=(), kind=jnp.bfloat16):
    loudness = shard_levels(own_key, dims, pieces, -0.22, 0.18) if pieces else 1.0
    result = jax.random.normal(own_key, dims, jnp.float32) * deviation * loudness
    return jnp.minimum(jnp.maximum(result, -reach), reach).astype(kind)


def setup_inputs(seed: int = 0) -> dict:
    seeds = jax.random.split(jax.random.key(seed), 16)
    return {
        "mesh_nodes": scatter_about(seeds[0], (NODES, D), 1.0, 6.0, ((0, 128),)),
        "coarse_nodes": scatter_about(seeds[1], (COARSE, D), 1.0, 6.0),
        "edge_latents": scatter_about(seeds[2], (EDGES, D), 1.0, 6.0, ((0, 128),)),
        "edge_tiles": draw_edge_tiles(jax.random.fold_in(seeds[15], 71), 0),
        "send_lists": plant(jax.random.randint(seeds[4], (BLOCKS, NEIGH, SLOTS), 0, NODE_DEV), jax.random.fold_in(seeds[4], 1), 0, NODE_DEV - 1).astype(jnp.int32),
        "tiles_live": draw_tiles_live(jax.random.fold_in(seeds[15], 71), 0),
        "edge_in": scatter_about(seeds[6], (3, D, D), (3 * D) ** -0.5, 0.15625),
        "edge_out": scatter_about(seeds[7], (D, D), D ** -0.5, 0.25),
        "edge_gain": jnp.clip(1.0 + 0.18 * jax.random.normal(seeds[8], (D,), jnp.float32), 0.1, 1.9),
        "node_in": scatter_about(seeds[9], (2, D, D), (2 * D) ** -0.5, 0.1875),
        "node_out": scatter_about(seeds[10], (D, D), D ** -0.5, 0.25),
        "node_gain": jnp.clip(1.0 + 0.18 * jax.random.normal(seeds[11], (D,), jnp.float32), 0.1, 1.9),
        "grad_nodes": scatter_about(seeds[12], (NODES, D), 1.0, 6.0, ((0, 128),)),
        "grad_coarse": scatter_about(seeds[13], (COARSE, D), 1.0, 6.0),
        "grad_edges": scatter_about(seeds[14], (EDGES, D), 1.0, 6.0, ((0, 128),)),
    }


EPS = 1e-05

def product(first_op, second_op):
    return jnp.dot(first_op, second_op, preferred_element_type=jnp.float32)

def inner_rows(first_op, second_op):
    return lax.dot_general(first_op, second_op, (((0,), (0,)), ((), ())), preferred_element_type=jnp.float32)

def outer_cols(first_op, second_op):
    return lax.dot_general(first_op, second_op, (((1,), (1,)), ((), ())), preferred_element_type=jnp.float32)

def exact_cols(first_op, second_op):
    return lax.dot_general(first_op, second_op, (((1,), (1,)), ((), ())), precision=lax.Precision.HIGHEST, preferred_element_type=jnp.float32)

def normalize(values):
    centered = values - lax.optimization_barrier(jnp.mean(values, axis=-1, keepdims=True))
    inverse = lax.rsqrt(lax.optimization_barrier(jnp.mean(centered * centered, axis=-1, keepdims=True)) + EPS)
    return (centered * inverse, inverse)

def normalize_back(upstream, normed, inverse):
    return inverse * (upstream - lax.optimization_barrier(jnp.mean(upstream, axis=-1, keepdims=True)) - normed * lax.optimization_barrier(jnp.mean(upstream * normed, axis=-1, keepdims=True)))

def swish_slope(values):
    sigmoid_v = jax.nn.sigmoid(values)
    return sigmoid_v * (1.0 + values * (1.0 - sigmoid_v))

def cycle_moves(neigh_count, block_count):
    near_count = neigh_count // 2 - 1
    near = [position - near_count for position in range(near_count)] + [position + 1 for position in range(near_count)]
    return near + [block_count // 4, block_count // 2]

def edge_forward(edge_rows, sender_part, receiver_part, alive_mask, edge_in, edge_out, edge_gain):
    preact = product(edge_rows, edge_in[0]) + sender_part + receiver_part
    hidden = jax.nn.silu(preact).astype(jnp.bfloat16)
    normed, inverse = normalize(product(hidden, edge_out))
    message = normed * edge_gain[None, :] * alive_mask[:, None]
    updated = (edge_rows.astype(jnp.float32) + message).astype(jnp.bfloat16)
    return (preact, hidden, normed, inverse, message, updated)

def edge_backward(edge_rows, preact, hidden, normed, inverse, alive_mask, message_grad, edge_in, edge_out, edge_gain):
    message_grad = message_grad * alive_mask[:, None]
    gain_grad = lax.optimization_barrier(jnp.sum(message_grad * normed, axis=0))
    out_slope = normalize_back(message_grad * edge_gain[None, :], normed, inverse).astype(jnp.bfloat16)
    out_grad = inner_rows(hidden, out_slope)
    pre_slope = (outer_cols(out_slope, edge_out) * swish_slope(preact)).astype(jnp.bfloat16)
    edge_grad = outer_cols(pre_slope, edge_in[0])
    first_grad = inner_rows(edge_rows, pre_slope)
    return (pre_slope, edge_grad, first_grad, out_grad, gain_grad)

def node_forward(node_rows, aggregate, node_in, node_out, node_gain):
    summed = aggregate.astype(jnp.bfloat16)
    preact = product(node_rows, node_in[0]) + product(summed, node_in[1])
    hidden = jax.nn.silu(preact).astype(jnp.bfloat16)
    normed, inverse = normalize(product(hidden, node_out))
    updated = (node_rows.astype(jnp.float32) + normed * node_gain[None, :]).astype(jnp.bfloat16)
    return (summed, preact, hidden, normed, inverse, updated)

def node_backward(node_rows, summed, preact, hidden, normed, inverse, node_slope, node_in, node_out, node_gain):
    gain_grad = lax.optimization_barrier(jnp.sum(node_slope * normed, axis=0))
    out_slope = normalize_back(node_slope * node_gain[None, :], normed, inverse).astype(jnp.bfloat16)
    out_grad = inner_rows(hidden, out_slope)
    pre_slope = (outer_cols(out_slope, node_out) * swish_slope(preact)).astype(jnp.bfloat16)
    direct = node_slope + outer_cols(pre_slope, node_in[0])
    aggregate_grad = outer_cols(pre_slope, node_in[1])
    in_grad = jnp.stack([inner_rows(node_rows, pre_slope), inner_rows(summed, pre_slope)])
    return (direct, aggregate_grad, in_grad, out_grad, gain_grad)

def reference(mesh_nodes, coarse_nodes, edge_latents, edge_tiles, send_lists, tiles_live, edge_in, edge_out, edge_gain, node_in, node_out, node_gain, grad_nodes, grad_coarse, grad_edges):
    block_count = tiles_live.shape[0]
    fine_count, features = mesh_nodes.shape
    node_dev = fine_count // block_count
    neigh_count = send_lists.shape[1]
    slot_count = send_lists.shape[2]
    halo_count = neigh_count * slot_count
    move_table = jnp.array(cycle_moves(neigh_count, block_count), dtype=jnp.int32)
    all_nodes = jnp.concatenate([mesh_nodes, coarse_nodes], axis=0)
    row_count = all_nodes.shape[0]
    sender_proj = product(all_nodes, edge_in[1])
    receiver_proj = product(all_nodes, edge_in[2])
    tile_dev = edge_tiles.shape[0] // block_count
    tile_width = edge_tiles.shape[2]
    edge_blocks = edge_latents.reshape(block_count, tile_dev * tile_width, features)
    tile_blocks = edge_tiles.reshape(block_count, tile_dev, 2, tile_width)
    slope_blocks = grad_edges.reshape(block_count, tile_dev * tile_width, features)
    block_ids = jnp.arange(block_count, dtype=jnp.int32)

    def endpoints(block, tiles):
        senders = tiles[:, 0, :].reshape(-1)
        receivers = tiles[:, 1, :].reshape(-1)
        offset = block * node_dev
        halo_pos = jnp.clip(senders - node_dev, 0, halo_count - 1).astype(jnp.int32)
        neighbour = (halo_pos // slot_count).astype(jnp.int32)
        moved_by = move_table[neighbour].astype(jnp.int32)
        source = ((block + moved_by) % block_count).astype(jnp.int32)
        listed = send_lists[source, neighbour, halo_pos % slot_count]
        sender_ids = jnp.where(senders < node_dev, offset + senders, jnp.where(senders < node_dev + halo_count, source * node_dev + listed, fine_count + senders - node_dev - halo_count))
        receiver_ids = jnp.where(receivers < node_dev, offset + receivers, fine_count + receivers - node_dev)
        alive_flag = jnp.arange(tile_dev, dtype=jnp.int32) < tiles_live[block]
        alive_mask = jnp.broadcast_to(alive_flag[:, None], (tile_dev, tile_width)).reshape(-1).astype(jnp.float32)
        return (sender_ids.astype(jnp.int32), receiver_ids.astype(jnp.int32), alive_mask)

    def forward_block(aggregate, block_data):
        block, edge_rows, tiles = block_data
        sender_ids, receiver_ids, alive_mask = endpoints(block, tiles)
        results = edge_forward(edge_rows, sender_proj[sender_ids], receiver_proj[receiver_ids], alive_mask, edge_in, edge_out, edge_gain)
        aggregate = aggregate + jax.ops.segment_sum(results[4], receiver_ids, num_segments=row_count)
        return (aggregate, results[5])
    zero_rows = jnp.zeros((row_count, features), jnp.float32)
    aggregate, new_edges = lax.scan(forward_block, zero_rows, (block_ids, edge_blocks, tile_blocks))
    summed, preact, hidden, normed, inverse, updated = node_forward(all_nodes, aggregate, node_in, node_out, node_gain)
    node_slope = jnp.concatenate([grad_nodes, grad_coarse], axis=0).astype(jnp.float32)
    direct, aggregate_grad, node_in_sum, node_out_sum, node_gain_sum = node_backward(all_nodes, summed, preact, hidden, normed, inverse, node_slope, node_in, node_out, node_gain)

    def backward_block(carry, block_data):
        sender_slope, receiver_slope, first_sum, sender_sum, receiver_sum, out_sum, gain_sum = carry
        block, edge_rows, tiles, edge_slope = block_data
        sender_ids, receiver_ids, alive_mask = endpoints(block, tiles)
        preact_e, hidden_e, normed_e, inverse_e, message, updated_e = edge_forward(edge_rows, sender_proj[sender_ids], receiver_proj[receiver_ids], alive_mask, edge_in, edge_out, edge_gain)
        message_grad = edge_slope.astype(jnp.float32) + aggregate_grad[receiver_ids]
        pre_slope, edge_grad, first_grad, out_grad, gain_grad = edge_backward(edge_rows, preact_e, hidden_e, normed_e, inverse_e, alive_mask, message_grad, edge_in, edge_out, edge_gain)
        sender_term = inner_rows(all_nodes[sender_ids], pre_slope)
        receiver_term = inner_rows(all_nodes[receiver_ids], pre_slope)
        wide_slope = lax.optimization_barrier(pre_slope).astype(jnp.float32)
        sender_slope = sender_slope + jax.ops.segment_sum(wide_slope, sender_ids, num_segments=row_count)
        receiver_slope = receiver_slope + jax.ops.segment_sum(wide_slope, receiver_ids, num_segments=row_count)
        carry = (sender_slope, receiver_slope, first_sum + first_grad, sender_sum + sender_term, receiver_sum + receiver_term, out_sum + out_grad, gain_sum + gain_grad)
        return (carry, (edge_slope.astype(jnp.float32) + edge_grad).astype(jnp.bfloat16))
    zero_square = jnp.zeros((features, features), jnp.float32)
    start_carry = (zero_rows, zero_rows, zero_square, zero_square, zero_square, zero_square, jnp.zeros((features,), jnp.float32))
    final_carry, edges_grad = lax.scan(backward_block, start_carry, (block_ids, edge_blocks, tile_blocks, slope_blocks))
    sender_slope, receiver_slope, first_sum, sender_sum, receiver_sum, out_sum, gain_sum = final_carry
    node_total = direct + exact_cols(sender_slope, edge_in[1].astype(jnp.float32)) + exact_cols(receiver_slope, edge_in[2].astype(jnp.float32))
    factor = float(edge_latents.shape[0]) ** (-0.5)
    edge_in_grad = (jnp.stack([first_sum, sender_sum, receiver_sum]) * factor).astype(jnp.bfloat16)
    return (updated[:fine_count], updated[fine_count:], new_edges.reshape(edge_latents.shape), node_total[:fine_count].astype(jnp.bfloat16), node_total[fine_count:].astype(jnp.bfloat16), edges_grad.reshape(edge_latents.shape), edge_in_grad, (out_sum * factor).astype(jnp.bfloat16), gain_sum * factor, (node_in_sum * factor).astype(jnp.bfloat16), (node_out_sum * factor).astype(jnp.bfloat16), node_gain_sum * factor)
```

```python
import functools

import jax
import jax.numpy as jnp
from jax import lax
from jax.experimental import pallas as pl
from jax.experimental.pallas import tpu as pltpu
from jax.sharding import PartitionSpec as P

EPS = 1e-05
AXES = ("lat", "blk")
BF = jnp.bfloat16
F32 = jnp.float32
D = 512
LANES = 128
TB = 256

OWN, HALO, COARSE = 320, 64, 640
ROWS = OWN + HALO + COARSE
FIRST_COARSE = OWN + HALO


def dot(a, b):
    return jnp.dot(a, b, preferred_element_type=F32)


def dot_tn(a, b):
    return lax.dot_general(a, b, (((0,), (0,)), ((), ())), preferred_element_type=F32)


def dot_nt(a, b):
    return lax.dot_general(a, b, (((1,), (1,)), ((), ())), preferred_element_type=F32)


def receiver_row(row):
    return jnp.where(row < OWN, row, row + HALO)


def onehot_tall(row, count, first=0):
    ids = lax.broadcasted_iota(jnp.int32, (count, LANES), 0) + first
    return jnp.where(ids == row, 1.0, 0.0).astype(BF)


def onehot_wide(row, count, first=0):
    column = jnp.broadcast_to(row, (LANES, LANES)).astype(F32).T.astype(jnp.int32)
    lane = lax.broadcasted_iota(jnp.int32, (LANES, LANES), 1) + first
    width = min(count, LANES)
    parts = [
        jnp.where((column - c)[:, :width] == lane[:, :width], 1.0, 0.0).astype(BF)
        for c in range(0, count, LANES)
    ]
    return parts[0] if len(parts) == 1 else jnp.concatenate(parts, axis=1)


def alive_rows(live, step):
    edge = lax.broadcasted_iota(jnp.int32, (TB, 1), 0) + step * TB
    return jnp.where(edge < live * LANES, 1.0, 0.0).astype(F32)


def normalize(values):
    centered = values - jnp.mean(values, axis=-1, keepdims=True)
    inverse = lax.rsqrt(jnp.mean(centered * centered, axis=-1, keepdims=True) + EPS)
    return centered * inverse, inverse


def normalize_back(upstream, normed, inverse):
    return inverse * (
        upstream
        - jnp.mean(upstream, axis=-1, keepdims=True)
        - normed * jnp.mean(upstream * normed, axis=-1, keepdims=True)
    )


def swish(values):
    sig = 1.0 / (1.0 + jnp.exp(-values))
    return (values * sig).astype(BF), sig * (1.0 + values * (1.0 - sig))


def pre_kernel(tiles, mesh_rows, coarse, edges, weights, pre, proj, hot):
    @pl.when(pl.program_id(0) == 0)
    def _():
        for k, w in enumerate((2, 1)):
            base = k * ROWS
            proj[base : base + OWN] = dot(mesh_rows[...], weights[w]).astype(BF)
            proj[base + OWN : base + FIRST_COARSE] = jnp.zeros((HALO, D), BF)
            proj[base + FIRST_COARSE : base + ROWS] = dot(coarse[...], weights[w]).astype(BF)

    for j in range(TB // LANES):
        at = slice(j * LANES, (j + 1) * LANES)
        hot[at, :ROWS] = onehot_wide(receiver_row(tiles[j, 1:2, :]), ROWS)
        hot[at, ROWS:] = onehot_wide(tiles[j, 0:1, :], ROWS)
    pre[...] = dot(hot[...], proj[...]) + dot(edges[...], weights[0])


def forward_kernel(
    live, tiles, pre, edges, halo, w_sender, edge_out, gain,
    new_edges, hidden_o, slope_o, normed_o, inverse_o, own_sum, coarse_sum,
    proj, hot, hot_t, total,
):
    step = pl.program_id(0)

    @pl.when(step == 0)
    def _():
        proj[...] = dot(halo[...], w_sender[...]).astype(BF)
        total[...] = jnp.zeros_like(total)

    for j in range(TB // LANES):
        at = slice(j * LANES, (j + 1) * LANES)
        hot[at, :] = onehot_wide(tiles[j, 0:1, :], HALO, OWN)
        hot_t[:, at] = onehot_tall(receiver_row(tiles[j, 1:2, :]), ROWS)
    preact = pre[...] + dot(hot[...], proj[...])
    hidden, slope = swish(preact)
    hidden_o[...] = hidden
    slope_o[...] = slope.astype(BF)
    normed, inverse = normalize(dot(hidden, edge_out[...]))
    normed_o[...] = normed.astype(BF)
    inverse_o[...] = inverse
    message = normed * gain[...] * alive_rows(live[0], step)
    new_edges[...] = (edges[...].astype(F32) + message).astype(BF)
    total[...] += dot(hot_t[...], message.astype(BF))

    @pl.when(step == pl.num_programs(0) - 1)
    def _():
        own_sum[...] = total[:OWN]
        coarse_sum[...] = total[FIRST_COARSE:]


def node_kernel(
    rows, summed_f, grad, node_in, node_out, gain,
    new_rows, direct, agg_slope, squares, gain_sum,
):
    nodes = rows[...]
    summed = summed_f[...].astype(BF)
    hidden, slope = swish(dot(nodes, node_in[0]) + dot(summed, node_in[1]))
    normed, inverse = normalize(dot(hidden, node_out[...]))
    new_rows[...] = (nodes.astype(F32) + normed * gain[...]).astype(BF)
    grad_f = grad[...].astype(F32)
    gain_sum[...] = jnp.broadcast_to(jnp.sum(grad_f * normed, axis=0, keepdims=True), (16, D))
    out_slope = normalize_back(grad_f * gain[...], normed, inverse).astype(BF)
    pre_slope = (dot_nt(out_slope, node_out[...]) * slope).astype(BF)
    agg_slope[...] = dot_nt(pre_slope, node_in[1]).astype(BF)
    direct[...] = grad_f + dot_nt(pre_slope, node_in[0])
    squares[0:D] = dot_tn(nodes, pre_slope)
    squares[D : 2 * D] = dot_tn(summed, pre_slope)
    squares[2 * D :] = dot_tn(hidden, out_slope)


def backward_kernel(
    live, tiles, grads, edges, hidden, slope, normed, inverse,
    own_slope, coarse_slope, own_direct, mesh_rows, halo, coarse, weights, edge_out, gain,
    edges_grad, sums, halo_back, own_total,
    table, hot, hot_s, hot_r, s_total, r_total, out_sum, first_sum, gain_sum, nodes,
):
    step = pl.program_id(0)

    @pl.when(step == 0)
    def _():
        table[:OWN] = own_slope[...]
        table[OWN:FIRST_COARSE] = jnp.zeros((HALO, D), BF)
        table[FIRST_COARSE:] = coarse_slope[...]
        for ref in (s_total, r_total, out_sum, first_sum, gain_sum):
            ref[...] = jnp.zeros_like(ref)

    for j in range(TB // LANES):
        at = slice(j * LANES, (j + 1) * LANES)
        receivers = receiver_row(tiles[j, 1:2, :])
        hot[at, :] = onehot_wide(receivers, ROWS)
        hot_r[:, at] = onehot_tall(receivers, ROWS)
        hot_s[:, at] = onehot_tall(tiles[j, 0:1, :], ROWS)
    grads_f = grads[...].astype(F32)
    normed_f = normed[...].astype(F32)
    message = (grads_f + dot(hot[...], table[...])) * alive_rows(live[0], step)
    gain_sum[...] += jnp.sum(message * normed_f, axis=0, keepdims=True)
    out_slope = normalize_back(message * gain[...], normed_f, inverse[...]).astype(BF)
    out_sum[...] += dot_tn(hidden[...], out_slope)
    pre_slope = (dot_nt(out_slope, edge_out[...]) * slope[...].astype(F32)).astype(BF)
    edges_grad[...] = (grads_f + dot_nt(pre_slope, weights[0])).astype(BF)
    first_sum[...] += dot_tn(edges[...], pre_slope)
    s_total[...] += dot(hot_s[...], pre_slope)
    r_total[...] += dot(hot_r[...], pre_slope)

    @pl.when(step == pl.num_programs(0) - 1)
    def _():
        nodes[:OWN] = mesh_rows[...]
        nodes[OWN:FIRST_COARSE] = halo[...]
        nodes[FIRST_COARSE:] = coarse[...]
        sent = s_total[...].astype(BF)
        got = r_total[...].astype(BF)
        sums[0:D] = first_sum[...].astype(BF)
        sums[D : 2 * D] = dot_tn(nodes[...], sent).astype(BF)
        sums[2 * D : 3 * D] = dot_tn(nodes[...], got).astype(BF)
        sums[3 * D : 4 * D] = out_sum[...].astype(BF)
        term = dot_nt(sent, weights[1]) + dot_nt(got, weights[2])
        sums[4 * D : 4 * D + COARSE] = term[FIRST_COARSE:].astype(BF)
        sums[4 * D + COARSE :] = jnp.broadcast_to(
            gain_sum[...], (sums.shape[0] - 4 * D - COARSE, D)
        ).astype(BF)
        own_total[...] = own_direct[...] + term[:OWN]
        halo_back[...] = sent[OWN:FIRST_COARSE]


def finish_kernel(lists, returned, own_total, w_sender, out):
    spread = onehot_tall_lists(lists[...])
    gathered = dot(spread, returned[...]).astype(BF)
    out[...] = (own_total[...] + dot_nt(gathered, w_sender[...])).astype(BF)


def onehot_tall_lists(row):
    ids = lax.broadcasted_iota(jnp.int32, (OWN, HALO), 0)
    return jnp.where(ids == row, 1.0, 0.0).astype(BF)


def pick_kernel(lists, mesh_rows, out):
    ids = lax.broadcasted_iota(jnp.int32, (OWN, HALO), 0)
    spread = jnp.where(ids == lists[...], 1.0, 0.0).astype(BF)
    out[...] = dot_tn(spread, mesh_rows[...]).astype(BF)


def whole(shape):
    return pl.BlockSpec(shape, lambda i: (0,) * len(shape))


def tiled(width):
    return pl.BlockSpec((TB, width), lambda i: (i, 0))


TILES = pl.BlockSpec((TB // LANES, 2, LANES), lambda i: (i, 0, 0))
SMEM = pl.BlockSpec(memory_space=pltpu.SMEM)
VM = pl.BlockSpec(memory_space=pltpu.VMEM)


def sds(shape, dtype):
    return jax.ShapeDtypeStruct(shape, dtype)


def params(mib):
    return pltpu.CompilerParams(vmem_limit_bytes=mib << 20)


def cost(gflop, mbytes):
    return pl.CostEstimate(
        flops=int(gflop * 1e9), bytes_accessed=int(mbytes * 1e6), transcendentals=0
    )


SHIFT = {"z": 1, "x": 3, "y": 5}


def ring_pairs(axis, offset):
    shift = SHIFT[axis]

    def target(i):
        p = (i >> shift) & 3
        return (i & ~(3 << shift)) | (((p + offset) % 4) << shift)

    return [(i, target(i)) for i in range(128)]


def position(me, axis):
    return (me >> SHIFT[axis]) & 3


def part(x, index, dim):
    size = x.shape[dim] // 4
    return lax.dynamic_slice_in_dim(x, index * size, size, dim)


def swap_core(x):
    return lax.ppermute(x, AXES, [(i, i ^ 1) for i in range(128)])


def halve(x, me):
    half = x.shape[0] // 2
    core = me & 1
    send = jnp.where(core == 0, x[half:], x[:half]).astype(BF)
    keep = jnp.where(core == 0, x[:half], x[half:])
    return keep.astype(F32) + swap_core(send).astype(F32)


def double(x, me):
    other = swap_core(x)
    first = (me & 1) == 0
    return jnp.concatenate([jnp.where(first, x, other), jnp.where(first, other, x)])


def scatter_sum(x, me, axis, dim):
    p = position(me, axis)
    got = [
        lax.ppermute(part(x, (p + o) % 4, dim).astype(BF), AXES, ring_pairs(axis, o))
        for o in (2, 1, 3)
    ]
    total = part(x, p, dim).astype(F32)
    for g in got:
        total = total + g.astype(F32)
    return total


def exchange_sum(x, axis):
    x = x.astype(BF)
    far, one, three = [lax.ppermute(x, AXES, ring_pairs(axis, o)) for o in (2, 1, 3)]
    x, far, one, three = [v.astype(F32) for v in (x, far, one, three)]
    return (x + far) + (one + three)


def gather(x, me, axis, dim):
    p = position(me, axis)
    pieces = [x] * 4
    for o in (2, 1, 3):
        pieces[o] = lax.ppermute(x, AXES, ring_pairs(axis, o))
    return jnp.concatenate(
        [lax.select_n((p - j) % 4, *pieces) for j in range(4)], axis=dim
    )


def reduce_color(x, me, axes):
    a, b, c = axes
    x = scatter_sum(x, me, a, 0)
    x = scatter_sum(x, me, b, 1)
    x = exchange_sum(x, c).astype(BF)
    return gather(gather(x, me, b, 1), me, a, 0)


def reduce_all(x, me, colors):
    x = halve(x, me)
    n = x.shape[0] // colors
    orders = ("zxy", "xyz", "yzx")
    parts = [
        reduce_color(x[k * n : (k + 1) * n], me, orders[k]) for k in range(colors)
    ]
    return double(jnp.concatenate(parts) if colors > 1 else parts[0], me)


def reduce_coarse(x, me):
    x = halve(x, me)
    x = scatter_sum(x, me, "z", 0)
    x = exchange_sum(x, "x")
    x = exchange_sum(x, "y").astype(BF)
    return double(gather(x, me, "z", 0), me)


MOVES = (-3, -2, -1, 1, 2, 3, 32, 64)


def halo_exchange(x, sign):
    pieces = []
    for k, move in enumerate(MOVES):
        pairs = [(i, (i + sign * move) % 128) for i in range(128)]
        pieces.append(lax.ppermute(x[k * 8 : (k + 1) * 8], AXES, pairs))
    return jnp.concatenate(pieces)


def node_call(rows, summed, grad, node_in, node_out, gain, name):
    n = rows.shape[0]
    return pl.pallas_call(
        node_kernel,
        out_shape=(
            sds((n, D), BF), sds((n, D), F32), sds((n, D), BF),
            sds((3 * D, D), F32), sds((16, D), F32),
        ),
        in_specs=[VM] * 6,
        out_specs=(VM,) * 5,
        compiler_params=params(32),
        cost_estimate=cost(n * 512 * 512 * 2 * 9 / 1e9, 8),
        name=name,
    )(rows, summed, grad, node_in, node_out, gain)


def on_device(
    mesh_nodes, coarse_nodes, edge_latents, edge_tiles, send_lists, tiles_live,
    edge_in, edge_out, edge_gain, node_in, node_out, node_gain,
    grad_nodes, grad_coarse, grad_edges,
):
    me = lax.axis_index(AXES)
    edges = edge_latents.shape[0]
    grid = (edges // TB,)
    lists = send_lists.reshape(1, HALO)
    gain_e = edge_gain.reshape(1, D)
    gain_n = node_gain.reshape(1, D)

    outgoing = pl.pallas_call(
        pick_kernel, out_shape=sds((HALO, D), BF), in_specs=[VM] * 2, out_specs=VM,
        name="pick",
    )(lists, mesh_nodes)
    halo = halo_exchange(outgoing, -1)

    pre = pl.pallas_call(
        pre_kernel,
        grid=grid,
        out_shape=sds((edges, D), F32),
        in_specs=[TILES, whole((OWN, D)), whole((COARSE, D)), tiled(D), whole((3, D, D))],
        out_specs=tiled(D),
        scratch_shapes=[pltpu.VMEM((2 * ROWS, D), BF), pltpu.VMEM((TB, 2 * ROWS), BF)],
        compiler_params=params(32),
        cost_estimate=cost(6.4, 8),
        name="pre",
    )(edge_tiles, mesh_nodes, coarse_nodes, edge_latents, edge_in)

    (new_edges, hidden, slope, normed, inverse, own_sum, coarse_sum) = pl.pallas_call(
        forward_kernel,
        grid=grid,
        out_shape=(
            sds((edges, D), BF), sds((edges, D), BF), sds((edges, D), BF), sds((edges, D), BF),
            sds((edges, 1), F32), sds((OWN, D), F32), sds((COARSE, D), F32),
        ),
        in_specs=[
            SMEM, TILES, tiled(D), tiled(D), whole((HALO, D)), whole((D, D)), whole((D, D)),
            whole((1, D)),
        ],
        out_specs=(
            tiled(D), tiled(D), tiled(D), tiled(D), tiled(1), whole((OWN, D)), whole((COARSE, D)),
        ),
        scratch_shapes=[
            pltpu.VMEM((HALO, D), BF), pltpu.VMEM((TB, HALO), BF), pltpu.VMEM((ROWS, TB), BF),
            pltpu.VMEM((ROWS, D), F32),
        ],
        compiler_params=params(32),
        cost_estimate=cost(4, 16),
        name="forward",
    )(tiles_live, edge_tiles, pre, edge_latents, halo, edge_in[1], edge_out, gain_e)

    coarse_total = reduce_coarse(coarse_sum, me)
    new_nodes, own_direct, own_slope, own_squares, own_gain = node_call(
        mesh_nodes, own_sum, grad_nodes, node_in, node_out, gain_n, "own"
    )
    node_sums = reduce_all(
        jnp.concatenate([own_squares, jnp.broadcast_to(own_gain[:1], (128, D))]), me, 1
    )
    new_coarse, coarse_direct, coarse_slope, extra_squares, extra_gain = node_call(
        coarse_nodes, coarse_total, grad_coarse, node_in, node_out, gain_n, "coarse"
    )

    sum_rows = 4 * D + COARSE + 128
    edges_grad, sums, halo_back, own_total = pl.pallas_call(
        backward_kernel,
        grid=grid,
        out_shape=(
            sds((edges, D), BF), sds((sum_rows, D), BF), sds((HALO, D), BF), sds((OWN, D), F32),
        ),
        in_specs=[
            SMEM, TILES, tiled(D), tiled(D), tiled(D), tiled(D), tiled(D), tiled(1),
            whole((OWN, D)), whole((COARSE, D)), whole((OWN, D)), whole((OWN, D)),
            whole((HALO, D)), whole((COARSE, D)), whole((3, D, D)), whole((D, D)), whole((1, D)),
        ],
        out_specs=(tiled(D), whole((sum_rows, D)), whole((HALO, D)), whole((OWN, D))),
        scratch_shapes=[
            pltpu.VMEM((ROWS, D), BF), pltpu.VMEM((TB, ROWS), BF), pltpu.VMEM((ROWS, TB), BF),
            pltpu.VMEM((ROWS, TB), BF), pltpu.VMEM((ROWS, D), F32), pltpu.VMEM((ROWS, D), F32),
            pltpu.VMEM((D, D), F32), pltpu.VMEM((D, D), F32), pltpu.VMEM((1, D), F32),
            pltpu.VMEM((ROWS, D), BF),
        ],
        compiler_params=params(48),
        cost_estimate=cost(13, 16),
        name="backward",
    )(
        tiles_live, edge_tiles, grad_edges, edge_latents, hidden, slope, normed, inverse,
        own_slope, coarse_slope, own_direct, mesh_nodes, halo, coarse_nodes, edge_in, edge_out,
        gain_e,
    )

    returned = halo_exchange(halo_back, 1)
    edge_sums = reduce_all(sums, me, 2).astype(F32)
    nodes_grad = pl.pallas_call(
        finish_kernel, out_shape=sds((OWN, D), BF), in_specs=[VM] * 4, out_specs=VM,
        name="finish",
    )(lists, returned, own_total, edge_in[1])

    factor = float(edges * 128) ** (-0.5)
    node_sums = node_sums.astype(F32)
    square = 4 * D
    return (
        new_nodes,
        new_coarse,
        new_edges,
        nodes_grad,
        (coarse_direct + edge_sums[square : square + COARSE]).astype(BF),
        edges_grad,
        (edge_sums[: 3 * D] * factor).astype(BF).reshape(3, D, D),
        (edge_sums[3 * D : square] * factor).astype(BF),
        edge_sums[square + COARSE] * factor,
        ((node_sums[: 2 * D] + extra_squares[: 2 * D]) * factor).astype(BF).reshape(2, D, D),
        ((node_sums[2 * D : 3 * D] + extra_squares[2 * D :]) * factor).astype(BF),
        (node_sums[3 * D] + extra_gain[0]) * factor,
    )


def solution(mesh):
    block = P(AXES, None)
    cube = P(AXES, None, None)
    in_specs = (
        block, P(), block, cube, cube, P(AXES), P(), P(), P(), P(), P(), P(), block, P(), block,
    )
    out_specs = (block, P(), block, block, P(), block, P(), P(), P(), P(), P(), P())
    return jax.shard_map(
        on_device, mesh=mesh, in_specs=in_specs, out_specs=out_specs, check_vma=False
    )
```

```python
import functools

import jax
import jax.numpy as jnp
from jax import lax
from jax.experimental import pallas as pl
from jax.experimental.pallas import tpu as pltpu
from jax.sharding import PartitionSpec as P

EPS = 1e-05
AXES = ("lat", "blk")
BF = jnp.bfloat16
F32 = jnp.float32
D = 512
LANES = 128
TB = 256
BIG = 56
COLORS = 2

OWN, HALO, COARSE = 320, 64, 640
ROWS = OWN + HALO + COARSE
FIRST_COARSE = OWN + HALO


def dot(a, b):
    return jnp.dot(a, b, preferred_element_type=F32)


def dot_tn(a, b):
    return lax.dot_general(a, b, (((0,), (0,)), ((), ())), preferred_element_type=F32)


def dot_nt(a, b):
    return lax.dot_general(a, b, (((1,), (1,)), ((), ())), preferred_element_type=F32)


def receiver_row(row):
    return jnp.where(row < OWN, row, row + HALO)


def onehot_tall(row, count, first=0):
    ids = lax.broadcasted_iota(jnp.int32, (count, LANES), 0) + first
    return jnp.where(ids == row, 1.0, 0.0).astype(BF)


def onehot_wide(row, count, first=0):
    column = jnp.broadcast_to(row, (LANES, LANES)).astype(F32).T.astype(jnp.int32)
    lane = lax.broadcasted_iota(jnp.int32, (LANES, LANES), 1) + first
    width = min(count, LANES)
    parts = [
        jnp.where((column - c)[:, :width] == lane[:, :width], 1.0, 0.0).astype(BF)
        for c in range(0, count, LANES)
    ]
    return parts[0] if len(parts) == 1 else jnp.concatenate(parts, axis=1)


def alive_rows(live, step):
    edge = lax.broadcasted_iota(jnp.int32, (TB, 1), 0) + step * TB
    return jnp.where(edge < live * LANES, 1.0, 0.0).astype(F32)


def normalize(values):
    centered = values - jnp.mean(values, axis=-1, keepdims=True)
    inverse = lax.rsqrt(jnp.mean(centered * centered, axis=-1, keepdims=True) + EPS)
    return centered * inverse, inverse


def normalize_back(upstream, normed, inverse):
    return inverse * (
        upstream
        - jnp.mean(upstream, axis=-1, keepdims=True)
        - normed * jnp.mean(upstream * normed, axis=-1, keepdims=True)
    )


def swish(values):
    sig = 1.0 / (1.0 + jnp.exp(-values))
    return (values * sig).astype(BF), sig * (1.0 + values * (1.0 - sig))


def pre_kernel(tiles, mesh_rows, coarse, edges, weights, pre, proj, hot):
    @pl.when(pl.program_id(0) == 0)
    def _():
        for k, w in enumerate((2, 1)):
            base = k * ROWS
            proj[base : base + OWN] = dot(mesh_rows[...], weights[w]).astype(BF)
            proj[base + OWN : base + FIRST_COARSE] = jnp.zeros((HALO, D), BF)
            proj[base + FIRST_COARSE : base + ROWS] = dot(coarse[...], weights[w]).astype(BF)

    for j in range(TB // LANES):
        at = slice(j * LANES, (j + 1) * LANES)
        hot[at, :ROWS] = onehot_wide(receiver_row(tiles[j, 1:2, :]), ROWS)
        hot[at, ROWS:] = onehot_wide(tiles[j, 0:1, :], ROWS)
    pre[...] = dot(hot[...], proj[...]) + dot(edges[...], weights[0])


def forward_kernel(
    live, core_ref, tiles, pre, edges, halo, w_sender, edge_out, gain,
    new_edges, hidden_o, slope_o, normed_o, inverse_o, own_sum, send, keep,
    proj, hot, hot_t, total,
):
    step = pl.program_id(0)

    @pl.when(step == 0)
    def _():
        proj[...] = dot(halo[...], w_sender[...]).astype(BF)
        total[...] = jnp.zeros_like(total)

    for j in range(TB // LANES):
        at = slice(j * LANES, (j + 1) * LANES)
        hot[at, :] = onehot_wide(tiles[j, 0:1, :], HALO, OWN)
        hot_t[:, at] = onehot_tall(receiver_row(tiles[j, 1:2, :]), ROWS)
    preact = pre[...] + dot(hot[...], proj[...])
    hidden, slope = swish(preact)
    hidden_o[...] = hidden
    slope_o[...] = slope.astype(BF)
    normed, inverse = normalize(dot(hidden, edge_out[...]))
    normed_o[...] = normed.astype(BF)
    inverse_o[...] = inverse
    message = normed * gain[...] * alive_rows(live[0], step)
    new_edges[...] = (edges[...].astype(F32) + message).astype(BF)
    total[...] += dot(hot_t[...], message.astype(BF))

    @pl.when(step == pl.num_programs(0) - 1)
    def _():
        own_sum[...] = total[:OWN]
        middle = FIRST_COARSE + COARSE // 2

        @pl.when(core_ref[0] == 0)
        def _():
            keep[...] = total[FIRST_COARSE:middle]
            send[...] = total[middle:].astype(BF)

        @pl.when(core_ref[0] != 0)
        def _():
            keep[...] = total[middle:]
            send[...] = total[FIRST_COARSE:middle].astype(BF)


def node_kernel(
    core_ref, rows, summed_f, grad, node_in, node_out, gain,
    new_rows, direct, agg_slope, gain_sum, *squares,
):
    nodes = rows[...]
    summed = summed_f[...].astype(BF)
    hidden, slope = swish(dot(nodes, node_in[0]) + dot(summed, node_in[1]))
    normed, inverse = normalize(dot(hidden, node_out[...]))
    new_rows[...] = (nodes.astype(F32) + normed * gain[...]).astype(BF)
    grad_f = grad[...].astype(F32)
    gain_sum[...] = jnp.sum(grad_f * normed, axis=0, keepdims=True)
    out_slope = normalize_back(grad_f * gain[...], normed, inverse).astype(BF)
    pre_slope = (dot_nt(out_slope, node_out[...]) * slope).astype(BF)
    agg_slope[...] = dot_nt(pre_slope, node_in[1]).astype(BF)
    direct[...] = grad_f + dot_nt(pre_slope, node_in[0])
    values = (dot_tn(nodes, pre_slope), dot_tn(summed, pre_slope), dot_tn(hidden, out_slope))
    for k, value in enumerate(values):
        if len(squares) == 1:
            squares[0][k * D : (k + 1) * D] = value
        else:
            store_halves(core_ref[0], squares[0], squares[1], k * D, value)


def slope_kernel(
    live, tiles, grads, edges, hidden, slope, normed, inverse,
    own_slope, coarse_slope, w_first, edge_out, gain,
    edges_grad, pre_slope_o, out_sum, first_sum, gain_sum, halo_back,
    table, hot, hot_h, halo_total,
):
    step = pl.program_id(0)

    @pl.when(step == 0)
    def _():
        table[:OWN] = own_slope[...]
        table[OWN:FIRST_COARSE] = jnp.zeros((HALO, D), BF)
        table[FIRST_COARSE:] = coarse_slope[...]
        for ref in (out_sum, first_sum, gain_sum, halo_total):
            ref[...] = jnp.zeros_like(ref)

    for j in range(TB // LANES):
        at = slice(j * LANES, (j + 1) * LANES)
        hot[at, :] = onehot_wide(receiver_row(tiles[j, 1:2, :]), ROWS)
        hot_h[:, at] = onehot_tall(tiles[j, 0:1, :], HALO, OWN)
    grads_f = grads[...].astype(F32)
    normed_f = normed[...].astype(F32)
    message = (grads_f + dot(hot[...], table[...])) * alive_rows(live[0], step)
    gain_sum[...] += jnp.sum(message * normed_f, axis=0, keepdims=True)
    out_slope = normalize_back(message * gain[...], normed_f, inverse[...]).astype(BF)
    out_sum[...] += dot_tn(hidden[...], out_slope)
    pre_slope = (dot_nt(out_slope, edge_out[...]) * slope[...].astype(F32)).astype(BF)
    pre_slope_o[...] = pre_slope
    edges_grad[...] = (grads_f + dot_nt(pre_slope, w_first[...])).astype(BF)
    first_sum[...] += dot_tn(edges[...], pre_slope)
    halo_total[...] += dot(hot_h[...], pre_slope)

    @pl.when(step == pl.num_programs(0) - 1)
    def _():
        halo_back[...] = halo_total[...].astype(BF)


SUM_ROWS = 4 * D + COARSE + LANES
HALF = SUM_ROWS // 2


def store_halves(core, send, keep, first, value):
    last = first + value.shape[0]
    for half in range(2):
        size = keep.shape[0]
        lo, hi = max(first, half * size), min(last, (half + 1) * size)
        if lo >= hi:
            continue
        rows = value[lo - first : hi - first].astype(BF)
        at = slice(lo - half * size, hi - half * size)

        @pl.when(core == half)
        def _():
            keep[at] = rows

        @pl.when(core != half)
        def _():
            send[at] = rows


def scatter_kernel(
    core_ref, tiles, pre_slope, own_direct, mesh_rows, halo, coarse, weights,
    out_sum, first_sum, gain_sum, node_gain_sum,
    send, keep, own_total,
    hot_s, hot_r, s_total, r_total, nodes,
):
    step = pl.program_id(0)

    @pl.when(step == 0)
    def _():
        s_total[...] = jnp.zeros_like(s_total)
        r_total[...] = jnp.zeros_like(r_total)

    for j in range(TB // LANES):
        at = slice(j * LANES, (j + 1) * LANES)
        hot_r[:, at] = onehot_tall(receiver_row(tiles[j, 1:2, :]), ROWS)
        hot_s[:, at] = onehot_tall(tiles[j, 0:1, :], ROWS)
    s_total[...] += dot(hot_s[...], pre_slope[...])
    r_total[...] += dot(hot_r[...], pre_slope[...])

    @pl.when(step == pl.num_programs(0) - 1)
    def _():
        core = core_ref[0]
        nodes[:OWN] = mesh_rows[...]
        nodes[OWN:FIRST_COARSE] = halo[...]
        nodes[FIRST_COARSE:] = coarse[...]
        sent = s_total[...].astype(BF)
        got = r_total[...].astype(BF)
        store_halves(core, send, keep, 0, first_sum[...])
        store_halves(core, send, keep, D, dot_tn(nodes[...], sent))
        store_halves(core, send, keep, 2 * D, dot_tn(nodes[...], got))
        store_halves(core, send, keep, 3 * D, out_sum[...])
        term = dot_nt(sent, weights[1]) + dot_nt(got, weights[2])
        store_halves(core, send, keep, 4 * D, term[FIRST_COARSE:])
        for k, ref in enumerate((gain_sum, node_gain_sum)):
            wide = jnp.broadcast_to(ref[...], (LANES // 2, D))
            store_halves(core, send, keep, 4 * D + COARSE + k * LANES // 2, wide)
        own_total[...] = own_direct[...] + term[:OWN]


def found_rows(mine, other, core, first, count):
    pieces = (mine + other) if core == 0 else (other + mine)
    size = pieces[0].shape[0]
    for c, ref in enumerate(pieces):
        lo, hi = max(first, c * size), min(first + count, (c + 1) * size)
        if lo < hi:
            yield slice(lo - first, hi - first), ref[lo - c * size : hi - c * size].astype(F32)


def assemble_kernel(colors, factor, core_ref, *refs):
    mine, other = refs[:colors], refs[colors : 2 * colors]
    node_mine, node_other, coarse_direct, extra, extra_gain = refs[2 * colors : 2 * colors + 5]
    coarse_grad, in_grad, out_grad, gain_grad, node_in_grad, node_out_grad, node_gain_grad = refs[
        2 * colors + 5 :
    ]

    def fill(core):
        rows = functools.partial(found_rows, mine, other, core)
        for k in range(3):
            for at, v in rows(k * D, D):
                in_grad[k, at] = (v * factor).astype(BF)
        for at, v in rows(3 * D, D):
            out_grad[at] = (v * factor).astype(BF)
        for at, v in rows(4 * D, COARSE):
            coarse_grad[at] = (coarse_direct[at] + v).astype(BF)
        for at, v in rows(4 * D + COARSE, 16):
            gain_grad[...] = v[:1] * factor
        for at, v in rows(4 * D + COARSE + LANES // 2, 16):
            node_gain_grad[...] = (v[:1] + extra_gain[...]) * factor
        rows = functools.partial(found_rows, (node_mine,), (node_other,), core)
        for k in range(3):
            out = node_out_grad if k == 2 else node_in_grad.at[k]
            for at, v in rows(k * D, D):
                more = extra[k * D + at.start : k * D + at.stop]
                out[at] = ((v + more) * factor).astype(BF)

    for core in range(2):

        @pl.when(core_ref[0] == core)
        def _():
            fill(core)


def finish_kernel(lists, returned, own_total, w_sender, out):
    spread = onehot_tall_lists(lists[...])
    gathered = dot(spread, returned[...]).astype(BF)
    out[...] = (own_total[...] + dot_nt(gathered, w_sender[...])).astype(BF)


def onehot_tall_lists(row):
    ids = lax.broadcasted_iota(jnp.int32, (OWN, HALO), 0)
    return jnp.where(ids == row, 1.0, 0.0).astype(BF)


def pick_kernel(lists, mesh_rows, out):
    ids = lax.broadcasted_iota(jnp.int32, (OWN, HALO), 0)
    spread = jnp.where(ids == lists[...], 1.0, 0.0).astype(BF)
    out[...] = dot_tn(spread, mesh_rows[...]).astype(BF)


def whole(shape):
    return pl.BlockSpec(shape, lambda i: (0,) * len(shape))


def tiled(width):
    return pl.BlockSpec((TB, width), lambda i: (i, 0))


TILES = pl.BlockSpec((TB // LANES, 2, LANES), lambda i: (i, 0, 0))
SMEM = pl.BlockSpec(memory_space=pltpu.SMEM)
VM = pl.BlockSpec(memory_space=pltpu.VMEM)


def sds(shape, dtype):
    return jax.ShapeDtypeStruct(shape, dtype)


def params(mib):
    return pltpu.CompilerParams(vmem_limit_bytes=mib << 20)


def cost(gflop, mbytes):
    return pl.CostEstimate(
        flops=int(gflop * 1e9), bytes_accessed=int(mbytes * 1e6), transcendentals=0
    )


SHIFT = {"z": 1, "x": 3, "y": 5}


def ring_pairs(axis, offset):
    shift = SHIFT[axis]

    def target(i):
        p = (i >> shift) & 3
        return (i & ~(3 << shift)) | (((p + offset) % 4) << shift)

    return [(i, target(i)) for i in range(128)]


def position(me, axis):
    return (me >> SHIFT[axis]) & 3


def part(x, index, dim):
    size = x.shape[dim] // 4
    return lax.dynamic_slice_in_dim(x, index * size, size, dim)


def swap_core(x):
    return lax.ppermute(x, AXES, [(i, i ^ 1) for i in range(128)])


def double(x, me):
    other = swap_core(x)
    first = (me & 1) == 0
    return jnp.concatenate([jnp.where(first, x, other), jnp.where(first, other, x)])


def scatter_sum(x, me, axis, dim):
    p = position(me, axis)
    got = [
        lax.ppermute(part(x, (p + o) % 4, dim).astype(BF), AXES, ring_pairs(axis, o))
        for o in (2, 1, 3)
    ]
    total = part(x, p, dim).astype(F32)
    for g in got:
        total = total + g.astype(F32)
    return total


def exchange_sum(x, axis):
    x = x.astype(BF)
    far, one, three = [lax.ppermute(x, AXES, ring_pairs(axis, o)) for o in (2, 1, 3)]
    x, far, one, three = [v.astype(F32) for v in (x, far, one, three)]
    return (x + far) + (one + three)


def gather(x, me, axis, dim):
    p = position(me, axis)
    pieces = [x] * 4
    for o in (2, 1, 3):
        pieces[o] = lax.ppermute(x, AXES, ring_pairs(axis, o))
    return jnp.concatenate(
        [lax.select_n((p - j) % 4, *pieces) for j in range(4)], axis=dim
    )


def reduce_color(x, me, axes):
    a, b, c = axes
    x = scatter_sum(x, me, a, 0)
    x = scatter_sum(x, me, b, 1)
    x = exchange_sum(x, c).astype(BF)
    return gather(gather(x, me, b, 1), me, a, 0)


def reduce_all(send, keep, me, colors):
    other = swap_core(send)
    n = HALF // colors
    orders = ("zxy", "xyz", "yzx")
    mine = []
    for k in range(colors):
        at = slice(k * n, (k + 1) * n)
        x = keep[at].astype(F32) + other[at].astype(F32)
        mine.append(reduce_color(x, me, orders[k]))
    return mine, [swap_core(x) for x in mine]


MOVES = (-3, -2, -1, 1, 2, 3, 32, 64)


def halo_exchange(x, sign):
    pieces = []
    for k, move in enumerate(MOVES):
        pairs = [(i, (i + sign * move) % 128) for i in range(128)]
        pieces.append(lax.ppermute(x[k * 8 : (k + 1) * 8], AXES, pairs))
    return jnp.concatenate(pieces)


def node_call(core, rows, summed, grad, node_in, node_out, gain, name):
    n = rows.shape[0]
    if name == "own":
        squares = (sds((3 * D // 2, D), BF),) * 2
    else:
        squares = (sds((3 * D, D), F32),)
    return pl.pallas_call(
        node_kernel,
        out_shape=(
            sds((n, D), BF), sds((n, D), F32), sds((n, D), BF), sds((1, D), F32), *squares,
        ),
        in_specs=[SMEM] + [VM] * 6,
        out_specs=(VM,) * (4 + len(squares)),
        compiler_params=params(BIG),
        cost_estimate=cost(n * 512 * 512 * 2 * 9 / 1e9, 8),
        name=name,
    )(core, rows, summed, grad, node_in, node_out, gain)


def tie(*values):
    return lax.optimization_barrier(values)


def on_device(
    mesh_nodes, coarse_nodes, edge_latents, edge_tiles, send_lists, tiles_live,
    edge_in, edge_out, edge_gain, node_in, node_out, node_gain,
    grad_nodes, grad_coarse, grad_edges,
):
    me = lax.axis_index(AXES)
    edges = edge_latents.shape[0]
    grid = (edges // TB,)
    lists = send_lists.reshape(1, HALO)
    gain_e = edge_gain.reshape(1, D)
    gain_n = node_gain.reshape(1, D)

    outgoing = pl.pallas_call(
        pick_kernel, out_shape=sds((HALO, D), BF), in_specs=[VM] * 2, out_specs=VM,
        name="pick",
    )(lists, mesh_nodes)
    halo = halo_exchange(outgoing, -1)

    pre = pl.pallas_call(
        pre_kernel,
        grid=grid,
        out_shape=sds((edges, D), F32),
        in_specs=[TILES, whole((OWN, D)), whole((COARSE, D)), tiled(D), whole((3, D, D))],
        out_specs=tiled(D),
        scratch_shapes=[pltpu.VMEM((2 * ROWS, D), BF), pltpu.VMEM((TB, 2 * ROWS), BF)],
        compiler_params=params(BIG),
        cost_estimate=cost(6.4, 8),
        name="pre",
    )(edge_tiles, mesh_nodes, coarse_nodes, edge_latents, edge_in)

    core = (me & 1).reshape(1)
    half = COARSE // 2
    (new_edges, hidden, slope, normed, inverse, own_sum, c_send, c_keep) = pl.pallas_call(
        forward_kernel,
        grid=grid,
        out_shape=(
            sds((edges, D), BF), sds((edges, D), BF), sds((edges, D), BF), sds((edges, D), BF),
            sds((edges, 1), F32), sds((OWN, D), F32), sds((half, D), BF), sds((half, D), F32),
        ),
        in_specs=[
            SMEM, SMEM, TILES, tiled(D), tiled(D), whole((HALO, D)), whole((D, D)), whole((D, D)),
            whole((1, D)),
        ],
        out_specs=(
            tiled(D), tiled(D), tiled(D), tiled(D), tiled(1), whole((OWN, D)), whole((half, D)),
            whole((half, D)),
        ),
        scratch_shapes=[
            pltpu.VMEM((HALO, D), BF), pltpu.VMEM((TB, HALO), BF), pltpu.VMEM((ROWS, TB), BF),
            pltpu.VMEM((ROWS, D), F32),
        ],
        compiler_params=params(BIG),
        cost_estimate=cost(4, 16),
        name="forward",
    )(tiles_live, core, edge_tiles, pre, edge_latents, halo, edge_in[1], edge_out, gain_e)

    new_nodes, own_direct, own_slope, own_gain, n_send, n_keep = node_call(
        core, mesh_nodes, own_sum, grad_nodes, node_in, node_out, gain_n, "own"
    )
    c = c_keep + swap_core(c_send).astype(F32)
    c, n_send = tie(scatter_sum(c, me, "z", 0), n_send)
    n = n_keep.astype(F32) + swap_core(n_send).astype(F32)
    c, n = tie(exchange_sum(c, "x"), n)
    n = scatter_sum(n, me, "y", 0)
    c, n = tie(exchange_sum(c, "y").astype(BF), n)
    n = scatter_sum(n, me, "x", 1)
    c, n = tie(gather(c, me, "z", 0), n)
    n = exchange_sum(n, "z").astype(BF)
    coarse_total, n = tie(double(c, me), n)
    n = gather(n, me, "x", 1)
    new_coarse, coarse_direct, coarse_slope, extra_gain, extra_squares = node_call(
        core, coarse_nodes, coarse_total, grad_coarse, node_in, node_out, gain_n, "coarse"
    )
    coarse_slope, n = tie(coarse_slope, n)
    n = gather(n, me, "y", 0)

    edges_grad, pre_slope, out_sum, first_sum, gain_sum, halo_back = pl.pallas_call(
        slope_kernel,
        grid=grid,
        out_shape=(
            sds((edges, D), BF), sds((edges, D), BF), sds((D, D), F32), sds((D, D), F32),
            sds((1, D), F32), sds((HALO, D), BF),
        ),
        in_specs=[
            SMEM, TILES, tiled(D), tiled(D), tiled(D), tiled(D), tiled(D), tiled(1),
            whole((OWN, D)), whole((COARSE, D)), whole((D, D)), whole((D, D)), whole((1, D)),
        ],
        out_specs=(
            tiled(D), tiled(D), whole((D, D)), whole((D, D)), whole((1, D)), whole((HALO, D)),
        ),
        scratch_shapes=[
            pltpu.VMEM((ROWS, D), BF), pltpu.VMEM((TB, ROWS), BF), pltpu.VMEM((HALO, TB), BF),
            pltpu.VMEM((HALO, D), F32),
        ],
        compiler_params=params(BIG),
        cost_estimate=cost(7, 16),
        name="slope",
    )(
        tiles_live, edge_tiles, grad_edges, edge_latents, hidden, slope, normed, inverse,
        own_slope, coarse_slope, edge_in[0], edge_out, gain_e,
    )
    pre_slope, n = tie(pre_slope, n)
    n_other = swap_core(n)
    returned = halo_exchange(halo_back, 1)

    s_send, s_keep, own_total = pl.pallas_call(
        scatter_kernel,
        grid=grid,
        out_shape=(sds((HALF, D), BF), sds((HALF, D), BF), sds((OWN, D), F32)),
        in_specs=[
            SMEM, TILES, tiled(D), whole((OWN, D)), whole((OWN, D)), whole((HALO, D)),
            whole((COARSE, D)), whole((3, D, D)), whole((D, D)), whole((D, D)), whole((1, D)),
            whole((1, D)),
        ],
        out_specs=(whole((HALF, D)), whole((HALF, D)), whole((OWN, D))),
        scratch_shapes=[
            pltpu.VMEM((ROWS, TB), BF), pltpu.VMEM((ROWS, TB), BF), pltpu.VMEM((ROWS, D), F32),
            pltpu.VMEM((ROWS, D), F32), pltpu.VMEM((ROWS, D), BF),
        ],
        compiler_params=params(BIG),
        cost_estimate=cost(7, 8),
        name="scatter",
    )(
        core, edge_tiles, pre_slope, own_direct, mesh_nodes, halo, coarse_nodes, edge_in,
        out_sum, first_sum, gain_sum, own_gain,
    )

    s_send, n_other, returned = tie(s_send, n_other, returned)
    mine, other = reduce_all(s_send, s_keep, me, COLORS)
    nodes_grad = pl.pallas_call(
        finish_kernel, out_shape=sds((OWN, D), BF), in_specs=[VM] * 4, out_specs=VM,
        name="finish",
    )(lists, returned, own_total, edge_in[1])

    factor = float(edges * 128) ** (-0.5)
    (coarse_grad, in_grad, out_grad, gain_grad, node_in_grad, node_out_grad, node_gain_grad) = (
        pl.pallas_call(
            functools.partial(assemble_kernel, COLORS, factor),
            out_shape=(
                sds((COARSE, D), BF), sds((3, D, D), BF), sds((D, D), BF), sds((1, D), F32),
                sds((2, D, D), BF), sds((D, D), BF), sds((1, D), F32),
            ),
            in_specs=[SMEM] + [VM] * (2 * COLORS + 5),
            out_specs=(VM,) * 7,
            compiler_params=params(BIG),
            name="assemble",
        )(core, *mine, *other, n, n_other, coarse_direct, extra_squares, extra_gain)
    )
    return (
        new_nodes, new_coarse, new_edges, nodes_grad, coarse_grad, edges_grad, in_grad, out_grad,
        gain_grad.reshape(D), node_in_grad, node_out_grad, node_gain_grad.reshape(D),
    )


def solution(mesh):
    block = P(AXES, None)
    cube = P(AXES, None, None)
    in_specs = (
        block, P(), block, cube, cube, P(AXES), P(), P(), P(), P(), P(), P(), block, P(), block,
    )
    out_specs = (block, P(), block, block, P(), block, P(), P(), P(), P(), P(), P())
    return jax.shard_map(
        on_device, mesh=mesh, in_specs=in_specs, out_specs=out_specs, check_vma=False
    )
```

```python
import functools

import jax
import jax.numpy as jnp
from jax import lax
from jax.experimental import pallas as pl
from jax.experimental.pallas import tpu as pltpu
from jax.sharding import PartitionSpec as P

EPS = 1e-05
AXES = ("lat", "blk")
BF = jnp.bfloat16
F32 = jnp.float32
D = 512
LANES = 128
TB = 256
BIG = 32
COLORS = 2

OWN, HALO, COARSE = 320, 64, 640
ROWS = OWN + HALO + COARSE
MOVES = (-3, -2, -1, 1, 2, 3, 32, 64)
SUM_ROWS = 7 * D + COARSE + LANES
HALF = SUM_ROWS // 2
GAINS = 4 * D + COARSE
SQUARES = GAINS + LANES
FIRST_COARSE = OWN + HALO


def dot(a, b):
    return jnp.dot(a, b, preferred_element_type=F32)


def dot_tn(a, b):
    return lax.dot_general(a, b, (((0,), (0,)), ((), ())), preferred_element_type=F32)


def dot_nt(a, b):
    return lax.dot_general(a, b, (((1,), (1,)), ((), ())), preferred_element_type=F32)


def receiver_row(row):
    return jnp.where(row < OWN, row, row + HALO)


def onehot_tall(row, count, first=0):
    ids = lax.broadcasted_iota(jnp.int32, (count, LANES), 0) + first
    return jnp.where(ids == row, 1.0, 0.0).astype(BF)


def onehot_wide(row, count, first=0):
    column = jnp.broadcast_to(row, (LANES, LANES)).astype(F32).T.astype(jnp.int32)
    lane = lax.broadcasted_iota(jnp.int32, (LANES, LANES), 1) + first
    width = min(count, LANES)
    parts = [
        jnp.where((column - c)[:, :width] == lane[:, :width], 1.0, 0.0).astype(BF)
        for c in range(0, count, LANES)
    ]
    return parts[0] if len(parts) == 1 else jnp.concatenate(parts, axis=1)


def alive_rows(live, step):
    edge = lax.broadcasted_iota(jnp.int32, (TB, 1), 0) + step * TB
    return jnp.where(edge < live * LANES, 1.0, 0.0).astype(F32)


def normalize(values):
    centered = values - jnp.mean(values, axis=-1, keepdims=True)
    inverse = lax.rsqrt(jnp.mean(centered * centered, axis=-1, keepdims=True) + EPS)
    return centered * inverse, inverse


def normalize_back(upstream, normed, inverse):
    return inverse * (
        upstream
        - jnp.mean(upstream, axis=-1, keepdims=True)
        - normed * jnp.mean(upstream * normed, axis=-1, keepdims=True)
    )


def swish(values):
    sig = 1.0 / (1.0 + jnp.exp(-values))
    return (values * sig).astype(BF), sig * (1.0 + values * (1.0 - sig))


def pre_kernel(tiles, mesh_rows, coarse, edges, weights, pre, proj, hot):
    @pl.when(pl.program_id(0) == 0)
    def _():
        for k, w in enumerate((2, 1)):
            base = k * ROWS
            proj[base : base + OWN] = dot(mesh_rows[...], weights[w]).astype(BF)
            proj[base + OWN : base + FIRST_COARSE] = jnp.zeros((HALO, D), BF)
            proj[base + FIRST_COARSE : base + ROWS] = dot(coarse[...], weights[w]).astype(BF)

    for j in range(TB // LANES):
        at = slice(j * LANES, (j + 1) * LANES)
        hot[at, :ROWS] = onehot_wide(receiver_row(tiles[j, 1:2, :]), ROWS)
        hot[at, ROWS:] = onehot_wide(tiles[j, 0:1, :], ROWS)
    pre[...] = dot(hot[...], proj[...]) + dot(edges[...], weights[0])


def forward_kernel(
    live, me_ref, tiles, pre, edges, arrived, w_sender, edge_out, gain,
    new_edges, hidden_o, slope_o, normed_o, inverse_o, own_sum, send, keep, halo_o,
    halo, proj, hot, hot_t, total,
):
    step = pl.program_id(0)

    @pl.when(step == 0)
    def _():
        for k, move in enumerate(MOVES):
            halo[k * 8 : (k + 1) * 8] = arrived[peer(me_ref, move)].astype(F32)
        halo_o[...] = halo[...].astype(BF)
        proj[...] = dot(halo[...].astype(BF), w_sender[...]).astype(BF)
        total[...] = jnp.zeros_like(total)

    for j in range(TB // LANES):
        at = slice(j * LANES, (j + 1) * LANES)
        hot[at, :] = onehot_wide(tiles[j, 0:1, :], HALO, OWN)
        hot_t[:, at] = onehot_tall(receiver_row(tiles[j, 1:2, :]), ROWS)
    preact = pre[...] + dot(hot[...], proj[...])
    hidden, slope = swish(preact)
    hidden_o[...] = hidden
    slope_o[...] = slope.astype(BF)
    normed, inverse = normalize(dot(hidden, edge_out[...]))
    normed_o[...] = normed.astype(BF)
    inverse_o[...] = inverse
    message = normed * gain[...] * alive_rows(live[0], step)
    new_edges[...] = (edges[...].astype(F32) + message).astype(BF)
    total[...] += dot(hot_t[...], message.astype(BF))

    @pl.when(step == pl.num_programs(0) - 1)
    def _():
        own_sum[...] = total[:OWN]
        middle = FIRST_COARSE + COARSE // 2

        @pl.when(me_ref[0] % 2 == 0)
        def _():
            keep[...] = total[FIRST_COARSE:middle]
            send[...] = total[middle:].astype(BF)

        @pl.when(me_ref[0] % 2 != 0)
        def _():
            keep[...] = total[middle:]
            send[...] = total[FIRST_COARSE:middle].astype(BF)


def node_kernel(
    rows, summed_f, grad, node_in, node_out, gain,
    new_rows, direct, agg_slope, gain_sum, squares,
):
    nodes = rows[...]
    summed = summed_f[...].astype(BF)
    hidden, slope = swish(dot(nodes, node_in[0]) + dot(summed, node_in[1]))
    normed, inverse = normalize(dot(hidden, node_out[...]))
    new_rows[...] = (nodes.astype(F32) + normed * gain[...]).astype(BF)
    grad_f = grad[...].astype(F32)
    gain_sum[...] = jnp.sum(grad_f * normed, axis=0, keepdims=True)
    out_slope = normalize_back(grad_f * gain[...], normed, inverse).astype(BF)
    pre_slope = (dot_nt(out_slope, node_out[...]) * slope).astype(BF)
    agg_slope[...] = dot_nt(pre_slope, node_in[1]).astype(BF)
    direct[...] = grad_f + dot_nt(pre_slope, node_in[0])
    values = (dot_tn(nodes, pre_slope), dot_tn(summed, pre_slope), dot_tn(hidden, out_slope))
    for k, value in enumerate(values):
        squares[k * D : (k + 1) * D] = value.astype(squares.dtype)


def slope_kernel(
    live, me_ref, tiles, grads, edges, hidden, slope, normed, inverse,
    own_slope, coarse_slope, w_first, edge_out, gain,
    edges_grad, pre_slope_o, out_sum, first_sum, gain_sum, halo_back,
    table, hot, hot_h, halo_total,
):
    step = pl.program_id(0)

    @pl.when(step == 0)
    def _():
        table[:OWN] = own_slope[...]
        table[OWN:FIRST_COARSE] = jnp.zeros((HALO, D), BF)
        table[FIRST_COARSE:] = coarse_slope[...]
        for ref in (out_sum, first_sum, gain_sum, halo_total):
            ref[...] = jnp.zeros_like(ref)

    for j in range(TB // LANES):
        at = slice(j * LANES, (j + 1) * LANES)
        hot[at, :] = onehot_wide(receiver_row(tiles[j, 1:2, :]), ROWS)
        hot_h[:, at] = onehot_tall(tiles[j, 0:1, :], HALO, OWN)
    grads_f = grads[...].astype(F32)
    normed_f = normed[...].astype(F32)
    message = (grads_f + dot(hot[...], table[...])) * alive_rows(live[0], step)
    gain_sum[...] += jnp.sum(message * normed_f, axis=0, keepdims=True)
    out_slope = normalize_back(message * gain[...], normed_f, inverse[...]).astype(BF)
    out_sum[...] += dot_tn(hidden[...], out_slope)
    pre_slope = (dot_nt(out_slope, edge_out[...]) * slope[...].astype(F32)).astype(BF)
    pre_slope_o[...] = pre_slope
    edges_grad[...] = (grads_f + dot_nt(pre_slope, w_first[...])).astype(BF)
    first_sum[...] += dot_tn(edges[...], pre_slope)
    halo_total[...] += dot(hot_h[...], pre_slope)

    @pl.when(step == pl.num_programs(0) - 1)
    def _():
        halo_back[...] = jnp.zeros_like(halo_back)
        for k, move in enumerate(MOVES):
            halo_back[peer(me_ref, move)] = halo_total[k * 8 : (k + 1) * 8].astype(BF)


def store_halves(core, send, keep, first, value):
    last = first + value.shape[0]
    for half in range(2):
        size = keep.shape[0]
        lo, hi = max(first, half * size), min(last, (half + 1) * size)
        if lo >= hi:
            continue
        rows = value[lo - first : hi - first].astype(BF)
        at = slice(lo - half * size, hi - half * size)

        @pl.when(core == half)
        def _():
            keep[at] = rows

        @pl.when(core != half)
        def _():
            send[at] = rows


def scatter_kernel(
    me_ref, tiles, pre_slope, own_direct, mesh_rows, halo, coarse, weights,
    out_sum, first_sum, gain_sum, node_squares, node_gain_sum,
    send, keep, own_total,
    hot_s, hot_r, s_total, r_total, nodes,
):
    step = pl.program_id(0)

    @pl.when(step == 0)
    def _():
        s_total[...] = jnp.zeros_like(s_total)
        r_total[...] = jnp.zeros_like(r_total)

    for j in range(TB // LANES):
        at = slice(j * LANES, (j + 1) * LANES)
        hot_r[:, at] = onehot_tall(receiver_row(tiles[j, 1:2, :]), ROWS)
        hot_s[:, at] = onehot_tall(tiles[j, 0:1, :], ROWS)
    s_total[...] += dot(hot_s[...], pre_slope[...])
    r_total[...] += dot(hot_r[...], pre_slope[...])

    @pl.when(step == pl.num_programs(0) - 1)
    def _():
        core = lax.rem(me_ref[0], 2)
        nodes[:OWN] = mesh_rows[...]
        nodes[OWN:FIRST_COARSE] = halo[...]
        nodes[FIRST_COARSE:] = coarse[...]
        sent = s_total[...].astype(BF)
        got = r_total[...].astype(BF)
        store_halves(core, send, keep, 0, first_sum[...])
        store_halves(core, send, keep, D, dot_tn(nodes[...], sent))
        store_halves(core, send, keep, 2 * D, dot_tn(nodes[...], got))
        store_halves(core, send, keep, 3 * D, out_sum[...])
        term = dot_nt(sent, weights[1]) + dot_nt(got, weights[2])
        store_halves(core, send, keep, 4 * D, term[FIRST_COARSE:])
        for k, ref in enumerate((gain_sum, node_gain_sum)):
            wide = jnp.broadcast_to(ref[...], (LANES // 2, D))
            store_halves(core, send, keep, GAINS + k * LANES // 2, wide)
        store_halves(core, send, keep, SQUARES, node_squares[...])
        own_total[...] = own_direct[...] + term[:OWN]


def found_rows(mine, other, core, first, count):
    pieces = (mine + other) if core == 0 else (other + mine)
    size = pieces[0].shape[0]
    for c, ref in enumerate(pieces):
        lo, hi = max(first, c * size), min(first + count, (c + 1) * size)
        if lo < hi:
            yield slice(lo - first, hi - first), ref[lo - c * size : hi - c * size].astype(F32)


def assemble_kernel(colors, factor, me_ref, *refs):
    mine, other = refs[:colors], refs[colors : 2 * colors]
    coarse_direct, extra, extra_gain = refs[2 * colors : 2 * colors + 3]
    coarse_grad, in_grad, out_grad, gain_grad, node_in_grad, node_out_grad, node_gain_grad = refs[
        2 * colors + 3 :
    ]

    def fill(core):
        rows = functools.partial(found_rows, mine, other, core)
        for k in range(3):
            for at, v in rows(k * D, D):
                in_grad[k, at] = (v * factor).astype(BF)
        for at, v in rows(3 * D, D):
            out_grad[at] = (v * factor).astype(BF)
        for at, v in rows(4 * D, COARSE):
            coarse_grad[at] = (coarse_direct[at] + v).astype(BF)
        for at, v in rows(GAINS, 16):
            gain_grad[...] = v[:1] * factor
        for at, v in rows(GAINS + LANES // 2, 16):
            node_gain_grad[...] = (v[:1] + extra_gain[...]) * factor
        for k in range(3):
            out = node_out_grad if k == 2 else node_in_grad.at[k]
            for at, v in rows(SQUARES + k * D, D):
                more = extra[k * D + at.start : k * D + at.stop]
                out[at] = ((v + more) * factor).astype(BF)

    for core in range(2):

        @pl.when(lax.rem(me_ref[0], 2) == core)
        def _():
            fill(core)


def finish_kernel(me_ref, lists, arrived, own_total, w_sender, out, returned):
    for k, move in enumerate(MOVES):
        returned[k * 8 : (k + 1) * 8] = arrived[peer(me_ref, -move)].astype(F32)
    gathered = dot(onehot_tall_lists(lists[...]), returned[...].astype(BF)).astype(BF)
    out[...] = (own_total[...] + dot_nt(gathered, w_sender[...])).astype(BF)


def onehot_tall_lists(row):
    ids = lax.broadcasted_iota(jnp.int32, (OWN, HALO), 0)
    return jnp.where(ids == row, 1.0, 0.0).astype(BF)


def peer(me_ref, offset):
    return lax.rem(me_ref[0] + (offset + 128), 128)


def pick_kernel(me_ref, lists, mesh_rows, out):
    picked = dot_tn(onehot_tall_lists(lists[...]), mesh_rows[...])
    out[...] = jnp.zeros_like(out)
    for k, move in enumerate(MOVES):
        out[peer(me_ref, -move)] = picked[k * 8 : (k + 1) * 8].astype(BF)


def whole(shape):
    return pl.BlockSpec(shape, lambda i: (0,) * len(shape))


def tiled(width):
    return pl.BlockSpec((TB, width), lambda i: (i, 0))


TILES = pl.BlockSpec((TB // LANES, 2, LANES), lambda i: (i, 0, 0))
SMEM = pl.BlockSpec(memory_space=pltpu.SMEM)
VM = pl.BlockSpec(memory_space=pltpu.VMEM)


def sds(shape, dtype):
    return jax.ShapeDtypeStruct(shape, dtype)


def params(mib):
    return pltpu.CompilerParams(vmem_limit_bytes=mib << 20)


def cost(gflop, mbytes):
    return pl.CostEstimate(
        flops=int(gflop * 1e9), bytes_accessed=int(mbytes * 1e6), transcendentals=0
    )


SHIFT = {"z": 1, "x": 3, "y": 5}


def ring_pairs(axis, offset):
    shift = SHIFT[axis]

    def target(i):
        p = (i >> shift) & 3
        return (i & ~(3 << shift)) | (((p + offset) % 4) << shift)

    return [(i, target(i)) for i in range(128)]


def position(me, axis):
    return (me >> SHIFT[axis]) & 3


def part(x, index, dim):
    size = x.shape[dim] // 4
    return lax.dynamic_slice_in_dim(x, index * size, size, dim)


def swap_core(x):
    return lax.ppermute(x, AXES, [(i, i ^ 1) for i in range(128)])


def double(x, me):
    other = swap_core(x)
    first = (me & 1) == 0
    return jnp.concatenate([jnp.where(first, x, other), jnp.where(first, other, x)])


def scatter_sum(x, me, axis, dim):
    p = position(me, axis)
    got = [
        lax.ppermute(part(x, (p + o) % 4, dim).astype(BF), AXES, ring_pairs(axis, o))
        for o in (2, 1, 3)
    ]
    total = part(x, p, dim).astype(F32)
    for g in got:
        total = total + g.astype(F32)
    return total


def exchange_sum(x, axis):
    x = x.astype(BF)
    far, one, three = [lax.ppermute(x, AXES, ring_pairs(axis, o)) for o in (2, 1, 3)]
    x, far, one, three = [v.astype(F32) for v in (x, far, one, three)]
    return (x + far) + (one + three)


def gather(x, me, axis, dim):
    p = position(me, axis)
    pieces = [x] * 4
    for o in (2, 1, 3):
        pieces[o] = lax.ppermute(x, AXES, ring_pairs(axis, o))
    return jnp.concatenate(
        [lax.select_n((p - j) % 4, *pieces) for j in range(4)], axis=dim
    )


def reduce_color(x, me, axes):
    a, b, c = axes
    x = scatter_sum(x, me, a, 0)
    x = scatter_sum(x, me, b, 1)
    x = exchange_sum(x, c).astype(BF)
    return gather(gather(x, me, b, 1), me, a, 0)


def reduce_all(send, keep, me, colors):
    other = swap_core(send)
    n = HALF // colors
    orders = ("zxy", "xyz", "yzx")
    mine = []
    for k in range(colors):
        at = slice(k * n, (k + 1) * n)
        x = keep[at].astype(F32) + other[at].astype(F32)
        mine.append(reduce_color(x, me, orders[k]))
    return mine, [swap_core(x) for x in mine]


def all_to_all(x):
    return lax.all_to_all(x, AXES, split_axis=0, concat_axis=0, tiled=True)


def node_call(rows, summed, grad, node_in, node_out, gain, name, kind):
    n = rows.shape[0]
    return pl.pallas_call(
        node_kernel,
        out_shape=(
            sds((n, D), BF), sds((n, D), F32), sds((n, D), BF), sds((1, D), F32),
            sds((3 * D, D), kind),
        ),
        in_specs=[VM] * 6,
        out_specs=(VM,) * 5,
        compiler_params=params(24),
        cost_estimate=cost(n * 512 * 512 * 2 * 9 / 1e9, 8),
        name=name,
    )(rows, summed, grad, node_in, node_out, gain)


def tie(*values):
    return lax.optimization_barrier(values)


def on_device(
    mesh_nodes, coarse_nodes, edge_latents, edge_tiles, send_lists, tiles_live,
    edge_in, edge_out, edge_gain, node_in, node_out, node_gain,
    grad_nodes, grad_coarse, grad_edges,
):
    me = lax.axis_index(AXES)
    edges = edge_latents.shape[0]
    grid = (edges // TB,)
    lists = send_lists.reshape(1, HALO)
    gain_e = edge_gain.reshape(1, D)
    gain_n = node_gain.reshape(1, D)

    here = me.reshape(1)
    sent = pl.pallas_call(
        pick_kernel, out_shape=sds((128, 8, D), BF), in_specs=[SMEM, VM, VM], out_specs=VM,
        name="pick",
    )(here, lists, mesh_nodes)
    arrived = all_to_all(sent)

    pre = pl.pallas_call(
        pre_kernel,
        grid=grid,
        out_shape=sds((edges, D), F32),
        in_specs=[TILES, whole((OWN, D)), whole((COARSE, D)), tiled(D), whole((3, D, D))],
        out_specs=tiled(D),
        scratch_shapes=[pltpu.VMEM((2 * ROWS, D), BF), pltpu.VMEM((TB, 2 * ROWS), BF)],
        compiler_params=params(BIG),
        cost_estimate=cost(6.4, 8),
        name="pre",
    )(edge_tiles, mesh_nodes, coarse_nodes, edge_latents, edge_in)

    half = COARSE // 2
    (new_edges, hidden, slope, normed, inverse, own_sum, c_send, c_keep, halo) = pl.pallas_call(
        forward_kernel,
        grid=grid,
        out_shape=(
            sds((edges, D), BF), sds((edges, D), BF), sds((edges, D), BF), sds((edges, D), BF),
            sds((edges, 1), F32), sds((OWN, D), F32), sds((half, D), BF), sds((half, D), F32),
            sds((HALO, D), BF),
        ),
        in_specs=[
            SMEM, SMEM, TILES, tiled(D), tiled(D), whole((128, 8, D)), whole((D, D)),
            whole((D, D)), whole((1, D)),
        ],
        out_specs=(
            tiled(D), tiled(D), tiled(D), tiled(D), tiled(1), whole((OWN, D)), whole((half, D)),
            whole((half, D)), whole((HALO, D)),
        ),
        scratch_shapes=[
            pltpu.VMEM((HALO, D), F32), pltpu.VMEM((HALO, D), BF), pltpu.VMEM((TB, HALO), BF),
            pltpu.VMEM((ROWS, TB), BF), pltpu.VMEM((ROWS, D), F32),
        ],
        compiler_params=params(BIG),
        cost_estimate=cost(4, 16),
        name="forward",
    )(tiles_live, here, edge_tiles, pre, edge_latents, arrived, edge_in[1], edge_out, gain_e)

    new_nodes, own_direct, own_slope, own_gain, own_squares = node_call(
        mesh_nodes, own_sum, grad_nodes, node_in, node_out, gain_n, "own", BF
    )
    c = c_keep + swap_core(c_send).astype(F32)
    c = scatter_sum(c, me, "z", 0)
    c = exchange_sum(c, "x")
    c = exchange_sum(c, "y").astype(BF)
    coarse_total = double(gather(c, me, "z", 0), me)
    new_coarse, coarse_direct, coarse_slope, extra_gain, extra_squares = node_call(
        coarse_nodes, coarse_total, grad_coarse, node_in, node_out, gain_n, "coarse", F32
    )

    edges_grad, pre_slope, out_sum, first_sum, gain_sum, halo_back = pl.pallas_call(
        slope_kernel,
        grid=grid,
        out_shape=(
            sds((edges, D), BF), sds((edges, D), BF), sds((D, D), F32), sds((D, D), F32),
            sds((1, D), F32), sds((128, 8, D), BF),
        ),
        in_specs=[
            SMEM, SMEM, TILES, tiled(D), tiled(D), tiled(D), tiled(D), tiled(D), tiled(1),
            whole((OWN, D)), whole((COARSE, D)), whole((D, D)), whole((D, D)), whole((1, D)),
        ],
        out_specs=(
            tiled(D), tiled(D), whole((D, D)), whole((D, D)), whole((1, D)),
            whole((128, 8, D)),
        ),
        scratch_shapes=[
            pltpu.VMEM((ROWS, D), BF), pltpu.VMEM((TB, ROWS), BF), pltpu.VMEM((HALO, TB), BF),
            pltpu.VMEM((HALO, D), F32),
        ],
        compiler_params=params(BIG),
        cost_estimate=cost(7, 16),
        name="slope",
    )(
        tiles_live, here, edge_tiles, grad_edges, edge_latents, hidden, slope, normed, inverse,
        own_slope, coarse_slope, edge_in[0], edge_out, gain_e,
    )
    returned = all_to_all(halo_back)

    s_send, s_keep, own_total = pl.pallas_call(
        scatter_kernel,
        grid=grid,
        out_shape=(sds((HALF, D), BF), sds((HALF, D), BF), sds((OWN, D), F32)),
        in_specs=[
            SMEM, TILES, tiled(D), whole((OWN, D)), whole((OWN, D)), whole((HALO, D)),
            whole((COARSE, D)), whole((3, D, D)), whole((D, D)), whole((D, D)), whole((1, D)),
            whole((3 * D, D)), whole((1, D)),
        ],
        out_specs=(whole((HALF, D)), whole((HALF, D)), whole((OWN, D))),
        scratch_shapes=[
            pltpu.VMEM((ROWS, TB), BF), pltpu.VMEM((ROWS, TB), BF), pltpu.VMEM((ROWS, D), F32),
            pltpu.VMEM((ROWS, D), F32), pltpu.VMEM((ROWS, D), BF),
        ],
        compiler_params=params(BIG),
        cost_estimate=cost(7, 8),
        name="scatter",
    )(
        here, edge_tiles, pre_slope, own_direct, mesh_nodes, halo, coarse_nodes, edge_in,
        out_sum, first_sum, gain_sum, own_squares, own_gain,
    )

    s_send, returned = tie(s_send, returned)
    mine, other = reduce_all(s_send, s_keep, me, COLORS)
    nodes_grad = pl.pallas_call(
        finish_kernel, out_shape=sds((OWN, D), BF), in_specs=[SMEM] + [VM] * 4, out_specs=VM,
        scratch_shapes=[pltpu.VMEM((HALO, D), F32)], name="finish",
    )(here, lists, returned, own_total, edge_in[1])

    factor = float(edges * 128) ** (-0.5)
    (coarse_grad, in_grad, out_grad, gain_grad, node_in_grad, node_out_grad, node_gain_grad) = (
        pl.pallas_call(
            functools.partial(assemble_kernel, COLORS, factor),
            out_shape=(
                sds((COARSE, D), BF), sds((3, D, D), BF), sds((D, D), BF), sds((1, D), F32),
                sds((2, D, D), BF), sds((D, D), BF), sds((1, D), F32),
            ),
            in_specs=[SMEM] + [VM] * (2 * COLORS + 3),
            out_specs=(VM,) * 7,
            compiler_params=params(24),
            name="assemble",
        )(here, *mine, *other, coarse_direct, extra_squares, extra_gain)
    )
    return (
        new_nodes, new_coarse, new_edges, nodes_grad, coarse_grad, edges_grad, in_grad, out_grad,
        gain_grad.reshape(D), node_in_grad, node_out_grad, node_gain_grad.reshape(D),
    )


def solution(mesh):
    block = P(AXES, None)
    cube = P(AXES, None, None)
    in_specs = (
        block, P(), block, cube, cube, P(AXES), P(), P(), P(), P(), P(), P(), block, P(), block,
    )
    out_specs = (block, P(), block, block, P(), block, P(), P(), P(), P(), P(), P())
    return jax.shard_map(
        on_device, mesh=mesh, in_specs=in_specs, out_specs=out_specs, check_vma=False
    )
```

```python
import functools

import jax
import jax.numpy as jnp
from jax import lax
from jax.experimental import pallas as pl
from jax.experimental.pallas import tpu as pltpu
from jax.sharding import PartitionSpec as P

EPS = 1e-05
AXES = ("lat", "blk")
BF = jnp.bfloat16
F32 = jnp.float32
D = 512
LANES = 128
TB = 256
BIG = 16

OWN, HALO, COARSE = 320, 64, 640
ROWS = OWN + HALO + COARSE
MOVES = (-3, -2, -1, 1, 2, 3, 32, 64)
EARLY = 5 * D
LATE = 2 * D + COARSE + LANES
GAINS = 2 * D + COARSE
FIRST_COARSE = OWN + HALO


def dot(a, b):
    return jnp.dot(a, b, preferred_element_type=F32)


def dot_tn(a, b):
    return lax.dot_general(a, b, (((0,), (0,)), ((), ())), preferred_element_type=F32)


def dot_nt(a, b):
    return lax.dot_general(a, b, (((1,), (1,)), ((), ())), preferred_element_type=F32)


def receiver_row(row):
    return jnp.where(row < OWN, row, row + HALO)


def onehot_tall(row, count, first=0):
    ids = lax.broadcasted_iota(jnp.int32, (count, LANES), 0) + first
    return jnp.where(ids == row, 1.0, 0.0).astype(BF)


def onehot_wide(row, count, first=0):
    column = jnp.broadcast_to(row, (LANES, LANES)).astype(F32).T.astype(jnp.int32)
    lane = lax.broadcasted_iota(jnp.int32, (LANES, LANES), 1) + first
    width = min(count, LANES)
    parts = [
        jnp.where((column - c)[:, :width] == lane[:, :width], 1.0, 0.0).astype(BF)
        for c in range(0, count, LANES)
    ]
    return parts[0] if len(parts) == 1 else jnp.concatenate(parts, axis=1)


def alive_rows(live, step):
    edge = lax.broadcasted_iota(jnp.int32, (TB, 1), 0) + step * TB
    return jnp.where(edge < live * LANES, 1.0, 0.0).astype(F32)


def normalize(values):
    centered = values - jnp.mean(values, axis=-1, keepdims=True)
    inverse = lax.rsqrt(jnp.mean(centered * centered, axis=-1, keepdims=True) + EPS)
    return centered * inverse, inverse


def normalize_back(upstream, normed, inverse):
    return inverse * (
        upstream
        - jnp.mean(upstream, axis=-1, keepdims=True)
        - normed * jnp.mean(upstream * normed, axis=-1, keepdims=True)
    )


def swish(values):
    sig = 1.0 / (1.0 + jnp.exp(-values))
    return (values * sig).astype(BF), sig * (1.0 + values * (1.0 - sig))


def pre_kernel(tiles, mesh_rows, coarse, edges, weights, pre, proj, hot):
    @pl.when(pl.program_id(0) == 0)
    def _():
        for k, w in enumerate((2, 1)):
            base = k * ROWS
            proj[base : base + OWN] = dot(mesh_rows[...], weights[w]).astype(BF)
            proj[base + OWN : base + FIRST_COARSE] = jnp.zeros((HALO, D), BF)
            proj[base + FIRST_COARSE : base + ROWS] = dot(coarse[...], weights[w]).astype(BF)

    for j in range(TB // LANES):
        at = slice(j * LANES, (j + 1) * LANES)
        hot[at, :ROWS] = onehot_wide(receiver_row(tiles[j, 1:2, :]), ROWS)
        hot[at, ROWS:] = onehot_wide(tiles[j, 0:1, :], ROWS)
    pre[...] = dot(hot[...], proj[...]) + dot(edges[...], weights[0])


def forward_kernel(
    live, me_ref, tiles, pre, edges, halo, w_sender, edge_out, gain,
    new_edges, hidden_o, slope_o, normed_o, inverse_o, own_sum, send, keep,
    proj, hot, hot_t, total,
):
    step = pl.program_id(0)

    @pl.when(step == 0)
    def _():
        proj[...] = dot(halo[...], w_sender[...]).astype(BF)
        total[...] = jnp.zeros_like(total)

    for j in range(TB // LANES):
        at = slice(j * LANES, (j + 1) * LANES)
        hot[at, :] = onehot_wide(tiles[j, 0:1, :], HALO, OWN)
        hot_t[:, at] = onehot_tall(receiver_row(tiles[j, 1:2, :]), ROWS)
    preact = pre[...] + dot(hot[...], proj[...])
    hidden, slope = swish(preact)
    hidden_o[...] = hidden
    slope_o[...] = slope.astype(BF)
    normed, inverse = normalize(dot(hidden, edge_out[...]))
    normed_o[...] = normed.astype(BF)
    inverse_o[...] = inverse
    message = normed * gain[...] * alive_rows(live[0], step)
    new_edges[...] = (edges[...].astype(F32) + message).astype(BF)
    total[...] += dot(hot_t[...], message.astype(BF))

    @pl.when(step == pl.num_programs(0) - 1)
    def _():
        own_sum[...] = total[:OWN]
        middle = FIRST_COARSE + COARSE // 2

        @pl.when(me_ref[0] % 2 == 0)
        def _():
            keep[...] = total[FIRST_COARSE:middle]
            send[...] = total[middle:].astype(BF)

        @pl.when(me_ref[0] % 2 != 0)
        def _():
            keep[...] = total[middle:]
            send[...] = total[FIRST_COARSE:middle].astype(BF)


def node_kernel(
    rows, summed_f, grad, node_in, node_out, gain,
    new_rows, direct, agg_slope, gain_sum, squares,
):
    nodes = rows[...]
    summed = summed_f[...].astype(BF)
    hidden, slope = swish(dot(nodes, node_in[0]) + dot(summed, node_in[1]))
    normed, inverse = normalize(dot(hidden, node_out[...]))
    new_rows[...] = (nodes.astype(F32) + normed * gain[...]).astype(BF)
    grad_f = grad[...].astype(F32)
    gain_sum[...] = jnp.sum(grad_f * normed, axis=0, keepdims=True)
    out_slope = normalize_back(grad_f * gain[...], normed, inverse).astype(BF)
    pre_slope = (dot_nt(out_slope, node_out[...]) * slope).astype(BF)
    agg_slope[...] = dot_nt(pre_slope, node_in[1]).astype(BF)
    direct[...] = grad_f + dot_nt(pre_slope, node_in[0])
    values = (dot_tn(nodes, pre_slope), dot_tn(summed, pre_slope), dot_tn(hidden, out_slope))
    for k, value in enumerate(values):
        squares[k * D : (k + 1) * D] = value.astype(squares.dtype)


def slope_kernel(
    live, me_ref, tiles, grads, edges, hidden, slope, normed, inverse,
    own_slope, coarse_slope, w_first, edge_out, gain, node_squares,
    edges_grad, pre_slope_o, gain_sum, send, keep, even,
    table, hot, hot_h, halo_total, out_sum, first_sum,
):
    step = pl.program_id(0)

    @pl.when(step == 0)
    def _():
        table[:OWN] = own_slope[...]
        table[OWN:FIRST_COARSE] = jnp.zeros((HALO, D), BF)
        table[FIRST_COARSE:] = coarse_slope[...]
        for ref in (out_sum, first_sum, gain_sum, halo_total):
            ref[...] = jnp.zeros_like(ref)

    for j in range(TB // LANES):
        at = slice(j * LANES, (j + 1) * LANES)
        hot[at, :] = onehot_wide(receiver_row(tiles[j, 1:2, :]), ROWS)
        hot_h[:, at] = onehot_tall(tiles[j, 0:1, :], HALO, OWN)
    grads_f = grads[...].astype(F32)
    normed_f = normed[...].astype(F32)
    message = (grads_f + dot(hot[...], table[...])) * alive_rows(live[0], step)
    gain_sum[...] += jnp.sum(message * normed_f, axis=0, keepdims=True)
    out_slope = normalize_back(message * gain[...], normed_f, inverse[...]).astype(BF)
    out_sum[...] += dot_tn(hidden[...], out_slope)
    pre_slope = (dot_nt(out_slope, edge_out[...]) * slope[...].astype(F32)).astype(BF)
    pre_slope_o[...] = pre_slope
    edges_grad[...] = (grads_f + dot_nt(pre_slope, w_first[...])).astype(BF)
    first_sum[...] += dot_tn(edges[...], pre_slope)
    halo_total[...] += dot(hot_h[...], pre_slope)

    @pl.when(step == pl.num_programs(0) - 1)
    def _():
        core = lax.rem(me_ref[0], 2)
        store_halves(core, send, keep, 0, first_sum[...])
        store_halves(core, send, keep, D, out_sum[...])
        store_halves(core, send, keep, 2 * D, node_squares[...])
        orders = piece_order(1)
        send[EARLY // 2 :] = pieces(halo_total[...], orders[0])
        even[...] = pieces(halo_total[...], orders[1])


def store_halves(core, send, keep, first, value):
    last = first + value.shape[0]
    for half in range(2):
        size = keep.shape[0]
        lo, hi = max(first, half * size), min(last, (half + 1) * size)
        if lo >= hi:
            continue
        rows = value[lo - first : hi - first].astype(BF)
        at = slice(lo - half * size, hi - half * size)

        @pl.when(core == half)
        def _():
            keep[at] = rows

        @pl.when(core != half)
        def _():
            send[at] = rows


def scatter_kernel(
    me_ref, tiles, pre_slope, own_direct, mesh_rows, halo, coarse, weights,
    gain_sum, node_gain_sum,
    send, keep, own_total,
    hot_s, hot_r, s_total, r_total, nodes,
):
    step = pl.program_id(0)

    @pl.when(step == 0)
    def _():
        s_total[...] = jnp.zeros_like(s_total)
        r_total[...] = jnp.zeros_like(r_total)

    for j in range(TB // LANES):
        at = slice(j * LANES, (j + 1) * LANES)
        hot_r[:, at] = onehot_tall(receiver_row(tiles[j, 1:2, :]), ROWS)
        hot_s[:, at] = onehot_tall(tiles[j, 0:1, :], ROWS)
    s_total[...] += dot(hot_s[...], pre_slope[...])
    r_total[...] += dot(hot_r[...], pre_slope[...])

    @pl.when(step == pl.num_programs(0) - 1)
    def _():
        core = lax.rem(me_ref[0], 2)
        nodes[:OWN] = mesh_rows[...]
        nodes[OWN:FIRST_COARSE] = halo[...]
        nodes[FIRST_COARSE:] = coarse[...]
        sent = s_total[...].astype(BF)
        got = r_total[...].astype(BF)
        store_halves(core, send, keep, 0, dot_tn(nodes[...], sent))
        store_halves(core, send, keep, D, dot_tn(nodes[...], got))
        term = dot_nt(sent, weights[1]) + dot_nt(got, weights[2])
        store_halves(core, send, keep, 2 * D, term[FIRST_COARSE:])
        for k, ref in enumerate((gain_sum, node_gain_sum)):
            wide = jnp.broadcast_to(ref[...], (LANES // 2, D))
            store_halves(core, send, keep, GAINS + k * LANES // 2, wide)
        own_total[...] = own_direct[...] + term[:OWN]


def found_rows(mine, other, core, first, count):
    pieces = (mine + other) if core == 0 else (other + mine)
    size = pieces[0].shape[0]
    for c, ref in enumerate(pieces):
        lo, hi = max(first, c * size), min(first + count, (c + 1) * size)
        if lo < hi:
            yield slice(lo - first, hi - first), ref[lo - c * size : hi - c * size].astype(F32)


def assemble_kernel(
    factor, me_ref, early_mine, early_other, late_mine, late_other, coarse_direct, extra,
    extra_gain,
    coarse_grad, in_grad, out_grad, gain_grad, node_in_grad, node_out_grad, node_gain_grad,
):
    def fill(core):
        early = functools.partial(found_rows, (early_mine,), (early_other,), core)
        late = functools.partial(found_rows, (late_mine,), (late_other,), core)
        for at, v in early(0, D):
            in_grad[0, at] = (v * factor).astype(BF)
        for at, v in early(D, D):
            out_grad[at] = (v * factor).astype(BF)
        for k in range(3):
            out = node_out_grad if k == 2 else node_in_grad.at[k]
            for at, v in early((2 + k) * D, D):
                more = extra[k * D + at.start : k * D + at.stop]
                out[at] = ((v + more) * factor).astype(BF)
        for k in range(2):
            for at, v in late(k * D, D):
                in_grad[k + 1, at] = (v * factor).astype(BF)
        for at, v in late(2 * D, COARSE):
            coarse_grad[at] = (coarse_direct[at] + v).astype(BF)
        for at, v in late(GAINS, 16):
            gain_grad[...] = v[:1] * factor
        for at, v in late(GAINS + LANES // 2, 16):
            node_gain_grad[...] = (v[:1] + extra_gain[...]) * factor

    for core in range(2):

        @pl.when(lax.rem(me_ref[0], 2) == core)
        def _():
            fill(core)


def piece_order(sign):
    odd = [MOVES.index(sign * offset) for offset in (-3, -1, 1, 3)]
    even = [MOVES.index(sign * offset) for offset in (-2, 2, sign * 32, sign * 64)]
    return odd, even


def pieces(value, order):
    return jnp.concatenate([value[k * 8 : (k + 1) * 8] for k in order]).astype(BF)


def onehot_tall_lists(row):
    ids = lax.broadcasted_iota(jnp.int32, (OWN, HALO), 0)
    return jnp.where(ids == row, 1.0, 0.0).astype(BF)


def finish_kernel(lists, returned, own_total, w_sender, out):
    gathered = dot(onehot_tall_lists(lists[...]), returned[...]).astype(BF)
    out[...] = (own_total[...] + dot_nt(gathered, w_sender[...])).astype(BF)


def pick_kernel(lists, mesh_rows, odd, even):
    picked = dot_tn(onehot_tall_lists(lists[...]), mesh_rows[...])
    orders = piece_order(-1)
    odd[...] = pieces(picked, orders[0])
    even[...] = pieces(picked, orders[1])


def whole(shape):
    return pl.BlockSpec(shape, lambda i: (0,) * len(shape))


def tiled(width):
    return pl.BlockSpec((TB, width), lambda i: (i, 0))


TILES = pl.BlockSpec((TB // LANES, 2, LANES), lambda i: (i, 0, 0))
SMEM = pl.BlockSpec(memory_space=pltpu.SMEM)
VM = pl.BlockSpec(memory_space=pltpu.VMEM)


def sds(shape, dtype):
    return jax.ShapeDtypeStruct(shape, dtype)


def params(mib):
    return pltpu.CompilerParams(vmem_limit_bytes=mib << 20)


def cost(gflop, mbytes):
    return pl.CostEstimate(
        flops=int(gflop * 1e9), bytes_accessed=int(mbytes * 1e6), transcendentals=0
    )


SHIFT = {"z": 1, "x": 3, "y": 5}


def ring_pairs(axis, offset):
    shift = SHIFT[axis]

    def target(i):
        p = (i >> shift) & 3
        return (i & ~(3 << shift)) | (((p + offset) % 4) << shift)

    return [(i, target(i)) for i in range(128)]


def position(me, axis):
    return (me >> SHIFT[axis]) & 3


def part(x, index, dim):
    size = x.shape[dim] // 4
    return lax.dynamic_slice_in_dim(x, index * size, size, dim)


def swap_core(x):
    return lax.ppermute(x, AXES, [(i, i ^ 1) for i in range(128)])


def double(x, me):
    other = swap_core(x)
    first = (me & 1) == 0
    return jnp.concatenate([jnp.where(first, x, other), jnp.where(first, other, x)])


def scatter_sum(x, me, axis, dim):
    p = position(me, axis)
    got = [
        lax.ppermute(part(x, (p + o) % 4, dim).astype(BF), AXES, ring_pairs(axis, o))
        for o in (2, 1, 3)
    ]
    total = part(x, p, dim).astype(F32)
    for g in got:
        total = total + g.astype(F32)
    return total


def exchange_sum(x, axis):
    x = x.astype(BF)
    far, one, three = [lax.ppermute(x, AXES, ring_pairs(axis, o)) for o in (2, 1, 3)]
    x, far, one, three = [v.astype(F32) for v in (x, far, one, three)]
    return (x + far) + (one + three)


def gather(x, me, axis, dim):
    p = position(me, axis)
    pieces = [x] * 4
    for o in (2, 1, 3):
        pieces[o] = lax.ppermute(x, AXES, ring_pairs(axis, o))
    return jnp.concatenate(
        [lax.select_n((p - j) % 4, *pieces) for j in range(4)], axis=dim
    )


def shift(x, offset):
    return lax.ppermute(x, AXES, [(i, (i + offset) % 128) for i in range(128)])


def far_route(even, sign):
    return tuple(shift(even[8 * k : 8 * k + 8], sign * far) for k, far in ((2, 32), (3, 64)))


def near_route(even, swapped, far, me, sign):
    low = (me & 1) == 0
    minus2, plus2 = [even[8 * k : 8 * k + 8] for k in range(2)]
    minus3, minus1, plus1, plus3 = [swapped[8 * k : 8 * k + 8] for k in range(4)]
    up = shift(jnp.concatenate([plus2, jnp.where(low, plus1, plus3)]), 2)
    down = shift(jnp.concatenate([minus2, jnp.where(low, minus3, minus1)]), -2)
    pairs = [(i, (i + (4 if i % 2 == 0 else -4)) % 128) for i in range(128)]
    skip = lax.ppermute(jnp.where(low, plus3, minus3), AXES, pairs)
    here = jnp.where(low, minus1, plus1)
    got = {
        2: up[:8],
        -2: down[:8],
        1: jnp.where(low, up[8:], here),
        3: jnp.where(low, skip, up[8:]),
        -3: jnp.where(low, down[8:], skip),
        -1: jnp.where(low, here, down[8:]),
        sign * 32: far[0],
        sign * 64: far[1],
    }
    return jnp.concatenate([got[sign * move] for move in MOVES])


def node_call(rows, summed, grad, node_in, node_out, gain, name, kind):
    n = rows.shape[0]
    return pl.pallas_call(
        node_kernel,
        out_shape=(
            sds((n, D), BF), sds((n, D), F32), sds((n, D), BF), sds((1, D), F32),
            sds((3 * D, D), kind),
        ),
        in_specs=[VM] * 6,
        out_specs=(VM,) * 5,
        compiler_params=params(24),
        cost_estimate=cost(n * 512 * 512 * 2 * 9 / 1e9, 8),
        name=name,
    )(rows, summed, grad, node_in, node_out, gain)


def tie(*values):
    return lax.optimization_barrier(values)


def on_device(
    mesh_nodes, coarse_nodes, edge_latents, edge_tiles, send_lists, tiles_live,
    edge_in, edge_out, edge_gain, node_in, node_out, node_gain,
    grad_nodes, grad_coarse, grad_edges,
):
    me = lax.axis_index(AXES)
    edges = edge_latents.shape[0]
    grid = (edges // TB,)
    lists = send_lists.reshape(1, HALO)
    gain_e = edge_gain.reshape(1, D)
    gain_n = node_gain.reshape(1, D)

    here = me.reshape(1)
    odd, even = pl.pallas_call(
        pick_kernel, out_shape=(sds((HALO // 2, D), BF),) * 2, in_specs=[VM, VM],
        out_specs=(VM, VM), name="pick",
    )(lists, mesh_nodes)
    far = far_route(even, -1)
    swapped, tiles_after = tie(swap_core(odd), edge_tiles)
    halo = near_route(even, swapped, far, me, -1)

    pre = pl.pallas_call(
        pre_kernel,
        grid=grid,
        out_shape=sds((edges, D), F32),
        in_specs=[TILES, whole((OWN, D)), whole((COARSE, D)), tiled(D), whole((3, D, D))],
        out_specs=tiled(D),
        scratch_shapes=[pltpu.VMEM((2 * ROWS, D), BF), pltpu.VMEM((TB, 2 * ROWS), BF)],
        compiler_params=params(BIG),
        cost_estimate=cost(6.4, 8),
        name="pre",
    )(tiles_after, mesh_nodes, coarse_nodes, edge_latents, edge_in)

    half = COARSE // 2
    (new_edges, hidden, slope, normed, inverse, own_sum, c_send, c_keep) = pl.pallas_call(
        forward_kernel,
        grid=grid,
        out_shape=(
            sds((edges, D), BF), sds((edges, D), BF), sds((edges, D), BF), sds((edges, D), BF),
            sds((edges, 1), F32), sds((OWN, D), F32), sds((half, D), BF), sds((half, D), F32),
        ),
        in_specs=[
            SMEM, SMEM, TILES, tiled(D), tiled(D), whole((HALO, D)), whole((D, D)),
            whole((D, D)), whole((1, D)),
        ],
        out_specs=(
            tiled(D), tiled(D), tiled(D), tiled(D), tiled(1), whole((OWN, D)), whole((half, D)),
            whole((half, D)),
        ),
        scratch_shapes=[
            pltpu.VMEM((HALO, D), BF), pltpu.VMEM((TB, HALO), BF),
            pltpu.VMEM((ROWS, TB), BF), pltpu.VMEM((ROWS, D), F32),
        ],
        compiler_params=params(BIG),
        cost_estimate=cost(4, 16),
        name="forward",
    )(tiles_live, here, edge_tiles, pre, edge_latents, halo, edge_in[1], edge_out, gain_e)

    new_nodes, own_direct, own_slope, own_gain, own_squares = node_call(
        mesh_nodes, own_sum, grad_nodes, node_in, node_out, gain_n, "own", BF
    )
    c = c_keep + swap_core(c_send).astype(F32)
    c = scatter_sum(c, me, "z", 0)
    c = exchange_sum(c, "x")
    c = exchange_sum(c, "y").astype(BF)
    coarse_total = double(gather(c, me, "z", 0), me)
    new_coarse, coarse_direct, coarse_slope, extra_gain, extra_squares = node_call(
        coarse_nodes, coarse_total, grad_coarse, node_in, node_out, gain_n, "coarse", F32
    )

    edges_grad, pre_slope, gain_sum, e_send, e_keep, even = pl.pallas_call(
        slope_kernel,
        grid=grid,
        out_shape=(
            sds((edges, D), BF), sds((edges, D), BF), sds((1, D), F32),
            sds((EARLY // 2 + HALO // 2, D), BF), sds((EARLY // 2, D), BF),
            sds((HALO // 2, D), BF),
        ),
        in_specs=[
            SMEM, SMEM, TILES, tiled(D), tiled(D), tiled(D), tiled(D), tiled(D), tiled(1),
            whole((OWN, D)), whole((COARSE, D)), whole((D, D)), whole((D, D)), whole((1, D)),
            whole((3 * D, D)),
        ],
        out_specs=(
            tiled(D), tiled(D), whole((1, D)), whole((EARLY // 2 + HALO // 2, D)),
            whole((EARLY // 2, D)), whole((HALO // 2, D)),
        ),
        scratch_shapes=[
            pltpu.VMEM((ROWS, D), BF), pltpu.VMEM((TB, ROWS), BF), pltpu.VMEM((HALO, TB), BF),
            pltpu.VMEM((HALO, D), F32), pltpu.VMEM((D, D), F32), pltpu.VMEM((D, D), F32),
        ],
        compiler_params=params(BIG + 8),
        cost_estimate=cost(7, 16),
        name="slope",
    )(
        tiles_live, here, edge_tiles, grad_edges, edge_latents, hidden, slope, normed, inverse,
        own_slope, coarse_slope, edge_in[0], edge_out, gain_e, own_squares,
    )
    swapped = swap_core(e_send)
    early = e_keep.astype(F32) + swapped[: EARLY // 2].astype(F32)
    pre_slope, early, back = tie(pre_slope, early, swapped[EARLY // 2 :])
    early = scatter_sum(early, me, "z", 0)
    far = far_route(even, 1)

    l_send, l_keep, own_total = pl.pallas_call(
        scatter_kernel,
        grid=grid,
        out_shape=(sds((LATE // 2, D), BF), sds((LATE // 2, D), BF), sds((OWN, D), F32)),
        in_specs=[
            SMEM, TILES, tiled(D), whole((OWN, D)), whole((OWN, D)), whole((HALO, D)),
            whole((COARSE, D)), whole((3, D, D)), whole((1, D)), whole((1, D)),
        ],
        out_specs=(whole((LATE // 2, D)), whole((LATE // 2, D)), whole((OWN, D))),
        scratch_shapes=[
            pltpu.VMEM((ROWS, TB), BF), pltpu.VMEM((ROWS, TB), BF), pltpu.VMEM((ROWS, D), F32),
            pltpu.VMEM((ROWS, D), F32), pltpu.VMEM((ROWS, D), BF),
        ],
        compiler_params=params(BIG + 8),
        cost_estimate=cost(7, 8),
        name="scatter",
    )(
        here, edge_tiles, pre_slope, own_direct, mesh_nodes, halo, coarse_nodes, edge_in,
        gain_sum, own_gain,
    )

    l_send, l_keep, back, far, early = tie(l_send, l_keep, back, far, early)
    late = l_keep.astype(F32) + swap_core(l_send).astype(F32)
    late, early = tie(late, early)
    returned = near_route(even, back, far, me, 1)
    late, returned = tie(scatter_sum(late, me, "x", 0), returned)
    early = exchange_sum(scatter_sum(early, me, "x", 1), "y").astype(BF)
    late = exchange_sum(scatter_sum(late, me, "y", 1), "z").astype(BF)
    early = gather(gather(early, me, "x", 1), me, "z", 0)
    late = gather(gather(late, me, "y", 1), me, "x", 0)
    nodes_grad = pl.pallas_call(
        finish_kernel, out_shape=sds((OWN, D), BF), in_specs=[VM] * 4, out_specs=VM,
        name="finish",
    )(lists, returned, own_total, edge_in[1])

    factor = float(edges * 128) ** (-0.5)
    (coarse_grad, in_grad, out_grad, gain_grad, node_in_grad, node_out_grad, node_gain_grad) = (
        pl.pallas_call(
            functools.partial(assemble_kernel, factor),
            out_shape=(
                sds((COARSE, D), BF), sds((3, D, D), BF), sds((D, D), BF), sds((1, D), F32),
                sds((2, D, D), BF), sds((D, D), BF), sds((1, D), F32),
            ),
            in_specs=[SMEM] + [VM] * 7,
            out_specs=(VM,) * 7,
            compiler_params=params(24),
            name="assemble",
        )(
            here, early, swap_core(early), late, swap_core(late), coarse_direct, extra_squares,
            extra_gain,
        )
    )
    return (
        new_nodes, new_coarse, new_edges, nodes_grad, coarse_grad, edges_grad, in_grad, out_grad,
        gain_grad.reshape(D), node_in_grad, node_out_grad, node_gain_grad.reshape(D),
    )


def solution(mesh):
    block = P(AXES, None)
    cube = P(AXES, None, None)
    in_specs = (
        block, P(), block, cube, cube, P(AXES), P(), P(), P(), P(), P(), P(), block, P(), block,
    )
    out_specs = (block, P(), block, block, P(), block, P(), P(), P(), P(), P(), P())
    return jax.shard_map(
        on_device, mesh=mesh, in_specs=in_specs, out_specs=out_specs, check_vma=False
    )
```

```python
import functools

import jax
import jax.numpy as jnp
from jax import lax
from jax.experimental import pallas as pl
from jax.experimental.pallas import tpu as pltpu
from jax.sharding import PartitionSpec as P

EPS = 1e-05
AXES = ("lat", "blk")
BF = jnp.bfloat16
F32 = jnp.float32
D = 512
LANES = 128
TB = 512
BIG = 24

OWN, HALO, COARSE = 320, 64, 640
ROWS = OWN + HALO + COARSE
MOVES = (-3, -2, -1, 1, 2, 3, 32, 64)
EARLY = 5 * D
LATE = 2 * D + COARSE + LANES
GAINS = 2 * D + COARSE
FIRST_COARSE = OWN + HALO


def dot(a, b):
    return jnp.dot(a, b, preferred_element_type=F32)


def dot_tn(a, b):
    return lax.dot_general(a, b, (((0,), (0,)), ((), ())), preferred_element_type=F32)


def dot_nt(a, b):
    return lax.dot_general(a, b, (((1,), (1,)), ((), ())), preferred_element_type=F32)


def receiver_row(row):
    return jnp.where(row < OWN, row, row + HALO)


def onehot_tall(row, count, first=0):
    ids = lax.broadcasted_iota(jnp.int32, (count, LANES), 0) + first
    return jnp.where(ids == row, 1.0, 0.0).astype(BF)


def onehot_wide(row, count, first=0):
    column = jnp.broadcast_to(row, (LANES, LANES)).astype(F32).T.astype(jnp.int32)
    lane = lax.broadcasted_iota(jnp.int32, (LANES, LANES), 1) + first
    width = min(count, LANES)
    parts = [
        jnp.where((column - c)[:, :width] == lane[:, :width], 1.0, 0.0).astype(BF)
        for c in range(0, count, LANES)
    ]
    return parts[0] if len(parts) == 1 else jnp.concatenate(parts, axis=1)


def alive_rows(live, step):
    edge = lax.broadcasted_iota(jnp.int32, (TB, 1), 0) + step * TB
    return jnp.where(edge < live * LANES, 1.0, 0.0).astype(F32)


def normalize(values):
    centered = values - jnp.mean(values, axis=-1, keepdims=True)
    inverse = lax.rsqrt(jnp.mean(centered * centered, axis=-1, keepdims=True) + EPS)
    return centered * inverse, inverse


def normalize_back(upstream, normed, inverse):
    return inverse * (
        upstream
        - jnp.mean(upstream, axis=-1, keepdims=True)
        - normed * jnp.mean(upstream * normed, axis=-1, keepdims=True)
    )


def swish(values):
    sig = 1.0 / (1.0 + jnp.exp(-values))
    return (values * sig).astype(BF), sig * (1.0 + values * (1.0 - sig))


def pre_kernel(tiles, mesh_rows, coarse, edges, weights, pre, proj, hot):
    @pl.when(pl.program_id(0) == 0)
    def _():
        for k, w in enumerate((2, 1)):
            base = k * ROWS
            proj[base : base + OWN] = dot(mesh_rows[...], weights[w]).astype(BF)
            proj[base + OWN : base + FIRST_COARSE] = jnp.zeros((HALO, D), BF)
            proj[base + FIRST_COARSE : base + ROWS] = dot(coarse[...], weights[w]).astype(BF)

    for j in range(TB // LANES):
        at = slice(j * LANES, (j + 1) * LANES)
        hot[at, :ROWS] = onehot_wide(receiver_row(tiles[j, 1:2, :]), ROWS)
        hot[at, ROWS:] = onehot_wide(tiles[j, 0:1, :], ROWS)
    pre[...] = dot(hot[...], proj[...]) + dot(edges[...], weights[0])


def forward_kernel(
    live, me_ref, tiles, pre, edges, halo, w_sender, edge_out, gain,
    new_edges, hidden_o, slope_o, normed_o, inverse_o, own_sum, send, keep,
    proj, hot, hot_t, total,
):
    step = pl.program_id(0)

    @pl.when(step == 0)
    def _():
        proj[...] = dot(halo[...], w_sender[...]).astype(BF)
        total[...] = jnp.zeros_like(total)

    for j in range(TB // LANES):
        at = slice(j * LANES, (j + 1) * LANES)
        hot[at, :] = onehot_wide(tiles[j, 0:1, :], HALO, OWN)
        hot_t[:, at] = onehot_tall(receiver_row(tiles[j, 1:2, :]), ROWS)
    preact = pre[...] + dot(hot[...], proj[...])
    hidden, slope = swish(preact)
    hidden_o[...] = hidden
    slope_o[...] = slope.astype(BF)
    normed, inverse = normalize(dot(hidden, edge_out[...]))
    normed_o[...] = normed.astype(BF)
    inverse_o[...] = inverse
    message = normed * gain[...] * alive_rows(live[0], step)
    new_edges[...] = (edges[...].astype(F32) + message).astype(BF)
    total[...] += dot(hot_t[...], message.astype(BF))

    @pl.when(step == pl.num_programs(0) - 1)
    def _():
        own_sum[...] = total[:OWN]
        middle = FIRST_COARSE + COARSE // 2

        @pl.when(me_ref[0] % 2 == 0)
        def _():
            keep[...] = total[FIRST_COARSE:middle]
            send[...] = total[middle:].astype(BF)

        @pl.when(me_ref[0] % 2 != 0)
        def _():
            keep[...] = total[middle:]
            send[...] = total[FIRST_COARSE:middle].astype(BF)


def node_kernel(
    rows, summed_f, grad, node_in, node_out, gain,
    new_rows, direct, agg_slope, gain_sum, squares,
):
    nodes = rows[...]
    summed = summed_f[...].astype(BF)
    hidden, slope = swish(dot(nodes, node_in[0]) + dot(summed, node_in[1]))
    normed, inverse = normalize(dot(hidden, node_out[...]))
    new_rows[...] = (nodes.astype(F32) + normed * gain[...]).astype(BF)
    grad_f = grad[...].astype(F32)
    gain_sum[...] = jnp.sum(grad_f * normed, axis=0, keepdims=True)
    out_slope = normalize_back(grad_f * gain[...], normed, inverse).astype(BF)
    pre_slope = (dot_nt(out_slope, node_out[...]) * slope).astype(BF)
    agg_slope[...] = dot_nt(pre_slope, node_in[1]).astype(BF)
    direct[...] = grad_f + dot_nt(pre_slope, node_in[0])
    values = (dot_tn(nodes, pre_slope), dot_tn(summed, pre_slope), dot_tn(hidden, out_slope))
    for k, value in enumerate(values):
        squares[k * D : (k + 1) * D] = value.astype(squares.dtype)


def slope_kernel(
    live, me_ref, tiles, grads, edges, hidden, slope, normed, inverse,
    own_slope, coarse_slope, w_first, edge_out, gain, node_squares,
    edges_grad, pre_slope_o, gain_sum, send, keep, even,
    table, hot, hot_h, halo_total, out_sum, first_sum,
):
    step = pl.program_id(0)

    @pl.when(step == 0)
    def _():
        table[:OWN] = own_slope[...]
        table[OWN:FIRST_COARSE] = jnp.zeros((HALO, D), BF)
        table[FIRST_COARSE:] = coarse_slope[...]
        for ref in (out_sum, first_sum, gain_sum, halo_total):
            ref[...] = jnp.zeros_like(ref)

    for j in range(TB // LANES):
        at = slice(j * LANES, (j + 1) * LANES)
        hot[at, :] = onehot_wide(receiver_row(tiles[j, 1:2, :]), ROWS)
        hot_h[:, at] = onehot_tall(tiles[j, 0:1, :], HALO, OWN)
    grads_f = grads[...].astype(F32)
    normed_f = normed[...].astype(F32)
    message = (grads_f + dot(hot[...], table[...])) * alive_rows(live[0], step)
    gain_sum[...] += jnp.sum(message * normed_f, axis=0, keepdims=True)
    out_slope = normalize_back(message * gain[...], normed_f, inverse[...]).astype(BF)
    out_sum[...] += dot_tn(hidden[...], out_slope)
    pre_slope = (dot_nt(out_slope, edge_out[...]) * slope[...].astype(F32)).astype(BF)
    pre_slope_o[...] = pre_slope
    edges_grad[...] = (grads_f + dot_nt(pre_slope, w_first[...])).astype(BF)
    first_sum[...] += dot_tn(edges[...], pre_slope)
    halo_total[...] += dot(hot_h[...], pre_slope)

    @pl.when(step == pl.num_programs(0) - 1)
    def _():
        core = lax.rem(me_ref[0], 2)
        store_halves(core, send, keep, 0, first_sum[...])
        store_halves(core, send, keep, D, out_sum[...])
        store_halves(core, send, keep, 2 * D, node_squares[...])
        orders = piece_order(1)
        send[EARLY // 2 :] = pieces(halo_total[...], orders[0])
        even[...] = pieces(halo_total[...], orders[1])


def store_halves(core, send, keep, first, value):
    last = first + value.shape[0]
    for half in range(2):
        size = keep.shape[0]
        lo, hi = max(first, half * size), min(last, (half + 1) * size)
        if lo >= hi:
            continue
        rows = value[lo - first : hi - first].astype(BF)
        at = slice(lo - half * size, hi - half * size)

        @pl.when(core == half)
        def _():
            keep[at] = rows

        @pl.when(core != half)
        def _():
            send[at] = rows


def scatter_kernel(
    me_ref, tiles, pre_slope, own_direct, mesh_rows, halo, coarse, weights,
    gain_sum, node_gain_sum,
    send, keep, own_total,
    hot_s, hot_r, s_total, r_total, nodes,
):
    step = pl.program_id(0)

    @pl.when(step == 0)
    def _():
        s_total[...] = jnp.zeros_like(s_total)
        r_total[...] = jnp.zeros_like(r_total)

    for j in range(TB // LANES):
        at = slice(j * LANES, (j + 1) * LANES)
        hot_r[:, at] = onehot_tall(receiver_row(tiles[j, 1:2, :]), ROWS)
        hot_s[:, at] = onehot_tall(tiles[j, 0:1, :], ROWS)
    s_total[...] += dot(hot_s[...], pre_slope[...])
    r_total[...] += dot(hot_r[...], pre_slope[...])

    @pl.when(step == pl.num_programs(0) - 1)
    def _():
        core = lax.rem(me_ref[0], 2)
        nodes[:OWN] = mesh_rows[...]
        nodes[OWN:FIRST_COARSE] = halo[...]
        nodes[FIRST_COARSE:] = coarse[...]
        sent = s_total[...].astype(BF)
        got = r_total[...].astype(BF)
        store_halves(core, send, keep, 0, dot_tn(nodes[...], sent))
        store_halves(core, send, keep, D, dot_tn(nodes[...], got))
        term = dot_nt(sent, weights[1]) + dot_nt(got, weights[2])
        store_halves(core, send, keep, 2 * D, term[FIRST_COARSE:])
        for k, ref in enumerate((gain_sum, node_gain_sum)):
            wide = jnp.broadcast_to(ref[...], (LANES // 2, D))
            store_halves(core, send, keep, GAINS + k * LANES // 2, wide)
        own_total[...] = own_direct[...] + term[:OWN]


def found_rows(mine, other, core, first, count):
    pieces = (mine + other) if core == 0 else (other + mine)
    size = pieces[0].shape[0]
    for c, ref in enumerate(pieces):
        lo, hi = max(first, c * size), min(first + count, (c + 1) * size)
        if lo < hi:
            yield slice(lo - first, hi - first), ref[lo - c * size : hi - c * size].astype(F32)


def early_kernel(
    factor, me_ref, mine, other, extra, first_grad, out_grad, node_in_grad, node_out_grad
):
    def fill(core):
        early = functools.partial(found_rows, (mine,), (other,), core)
        for at, v in early(0, D):
            first_grad[at] = (v * factor).astype(BF)
        for at, v in early(D, D):
            out_grad[at] = (v * factor).astype(BF)
        for k in range(3):
            out = node_out_grad if k == 2 else node_in_grad.at[k]
            for at, v in early((2 + k) * D, D):
                more = extra[k * D + at.start : k * D + at.stop]
                out[at] = ((v + more) * factor).astype(BF)

    by_core(me_ref, fill)


def late_kernel(
    factor, me_ref, mine, other, first_grad, coarse_direct, extra_gain,
    coarse_grad, in_grad, gain_grad, node_gain_grad,
):
    in_grad[0] = first_grad[...]

    def fill(core):
        late = functools.partial(found_rows, (mine,), (other,), core)
        for k in range(2):
            for at, v in late(k * D, D):
                in_grad[k + 1, at] = (v * factor).astype(BF)
        for at, v in late(2 * D, COARSE):
            coarse_grad[at] = (coarse_direct[at] + v).astype(BF)
        for at, v in late(GAINS, 16):
            gain_grad[...] = v[:1] * factor
        for at, v in late(GAINS + LANES // 2, 16):
            node_gain_grad[...] = (v[:1] + extra_gain[...]) * factor

    by_core(me_ref, fill)


def by_core(me_ref, fill):
    for core in range(2):

        @pl.when(lax.rem(me_ref[0], 2) == core)
        def _():
            fill(core)


def piece_order(sign):
    odd = [MOVES.index(sign * offset) for offset in (-3, -1, 1, 3)]
    even = [MOVES.index(sign * offset) for offset in (-2, 2, sign * 32, sign * 64)]
    return odd, even


def pieces(value, order):
    return jnp.concatenate([value[k * 8 : (k + 1) * 8] for k in order]).astype(BF)


def onehot_tall_lists(row):
    ids = lax.broadcasted_iota(jnp.int32, (OWN, HALO), 0)
    return jnp.where(ids == row, 1.0, 0.0).astype(BF)


def finish_kernel(lists, returned, own_total, w_sender, out):
    gathered = dot(onehot_tall_lists(lists[...]), returned[...]).astype(BF)
    out[...] = (own_total[...] + dot_nt(gathered, w_sender[...])).astype(BF)


def pick_kernel(lists, mesh_rows, odd, even):
    picked = dot_tn(onehot_tall_lists(lists[...]), mesh_rows[...])
    orders = piece_order(-1)
    odd[...] = pieces(picked, orders[0])
    even[...] = pieces(picked, orders[1])


def whole(shape):
    return pl.BlockSpec(shape, lambda i: (0,) * len(shape))


def tiled(width):
    return pl.BlockSpec((TB, width), lambda i: (i, 0))


TILES = pl.BlockSpec((TB // LANES, 2, LANES), lambda i: (i, 0, 0))
SMEM = pl.BlockSpec(memory_space=pltpu.SMEM)
VM = pl.BlockSpec(memory_space=pltpu.VMEM)


def sds(shape, dtype):
    return jax.ShapeDtypeStruct(shape, dtype)


def far_out(shape, dtype):
    return pltpu.HBM(shape, dtype)


def params(mib):
    return pltpu.CompilerParams(vmem_limit_bytes=mib << 20)


def cost(gflop, mbytes):
    return pl.CostEstimate(
        flops=int(gflop * 1e9), bytes_accessed=int(mbytes * 1e6), transcendentals=0
    )


SHIFT = {"z": 1, "x": 3, "y": 5}


def ring_pairs(axis, offset):
    shift = SHIFT[axis]

    def target(i):
        p = (i >> shift) & 3
        return (i & ~(3 << shift)) | (((p + offset) % 4) << shift)

    return [(i, target(i)) for i in range(128)]


def position(me, axis):
    return (me >> SHIFT[axis]) & 3


def part(x, index, dim):
    size = x.shape[dim] // 4
    return lax.dynamic_slice_in_dim(x, index * size, size, dim)


def swap_core(x):
    return lax.ppermute(x, AXES, [(i, i ^ 1) for i in range(128)])


def double(x, me):
    other = swap_core(x)
    first = (me & 1) == 0
    return jnp.concatenate([jnp.where(first, x, other), jnp.where(first, other, x)])


def scatter_sum(x, me, axis, dim):
    p = position(me, axis)
    got = [
        lax.ppermute(part(x, (p + o) % 4, dim).astype(BF), AXES, ring_pairs(axis, o))
        for o in (2, 1, 3)
    ]
    total = part(x, p, dim).astype(F32)
    for g in got:
        total = total + g.astype(F32)
    return total


def exchange_sum(x, axis):
    x = x.astype(BF)
    far, one, three = [lax.ppermute(x, AXES, ring_pairs(axis, o)) for o in (2, 1, 3)]
    x, far, one, three = [v.astype(F32) for v in (x, far, one, three)]
    return (x + far) + (one + three)


def gather(x, me, axis, dim):
    p = position(me, axis)
    pieces = [x] * 4
    for o in (2, 1, 3):
        pieces[o] = lax.ppermute(x, AXES, ring_pairs(axis, o))
    return jnp.concatenate(
        [lax.select_n((p - j) % 4, *pieces) for j in range(4)], axis=dim
    )


def shift(x, offset):
    return lax.ppermute(x, AXES, [(i, (i + offset) % 128) for i in range(128)])


def far_route(even, sign):
    return tuple(shift(even[8 * k : 8 * k + 8], sign * far) for k, far in ((2, 32), (3, 64)))


def near_route(even, swapped, far, me, sign):
    low = (me & 1) == 0
    minus2, plus2 = [even[8 * k : 8 * k + 8] for k in range(2)]
    minus3, minus1, plus1, plus3 = [swapped[8 * k : 8 * k + 8] for k in range(4)]
    up = shift(jnp.concatenate([plus2, jnp.where(low, plus1, plus3)]), 2)
    down = shift(jnp.concatenate([minus2, jnp.where(low, minus3, minus1)]), -2)
    pairs = [(i, (i + (4 if i % 2 == 0 else -4)) % 128) for i in range(128)]
    skip = lax.ppermute(jnp.where(low, plus3, minus3), AXES, pairs)
    here = jnp.where(low, minus1, plus1)
    got = {
        2: up[:8],
        -2: down[:8],
        1: jnp.where(low, up[8:], here),
        3: jnp.where(low, skip, up[8:]),
        -3: jnp.where(low, down[8:], skip),
        -1: jnp.where(low, here, down[8:]),
        sign * 32: far[0],
        sign * 64: far[1],
    }
    return jnp.concatenate([got[sign * move] for move in MOVES])


def node_call(rows, summed, grad, node_in, node_out, gain, name, kind):
    n = rows.shape[0]
    return pl.pallas_call(
        node_kernel,
        out_shape=(
            sds((n, D), BF), sds((n, D), F32), sds((n, D), BF), sds((1, D), F32),
            sds((3 * D, D), kind),
        ),
        in_specs=[VM] * 6,
        out_specs=(VM,) * 5,
        compiler_params=params(24),
        cost_estimate=cost(n * 512 * 512 * 2 * 9 / 1e9, 8),
        name=name,
    )(rows, summed, grad, node_in, node_out, gain)


def tie(*values):
    return lax.optimization_barrier(values)


def on_device(
    mesh_nodes, coarse_nodes, edge_latents, edge_tiles, send_lists, tiles_live,
    edge_in, edge_out, edge_gain, node_in, node_out, node_gain,
    grad_nodes, grad_coarse, grad_edges,
):
    me = lax.axis_index(AXES)
    edges = edge_latents.shape[0]
    grid = (edges // TB,)
    lists = send_lists.reshape(1, HALO)
    gain_e = edge_gain.reshape(1, D)
    gain_n = node_gain.reshape(1, D)

    here = me.reshape(1)
    odd, even = pl.pallas_call(
        pick_kernel, out_shape=(sds((HALO // 2, D), BF),) * 2, in_specs=[VM, VM],
        out_specs=(VM, VM), name="pick",
    )(lists, mesh_nodes)
    far = far_route(even, -1)
    swapped, tiles_after = tie(swap_core(odd), edge_tiles)
    halo = near_route(even, swapped, far, me, -1)

    pre = pl.pallas_call(
        pre_kernel,
        grid=grid,
        out_shape=sds((edges, D), F32),
        in_specs=[TILES, whole((OWN, D)), whole((COARSE, D)), tiled(D), whole((3, D, D))],
        out_specs=tiled(D),
        scratch_shapes=[pltpu.VMEM((2 * ROWS, D), BF), pltpu.VMEM((TB, 2 * ROWS), BF)],
        compiler_params=params(BIG),
        cost_estimate=cost(6.4, 8),
        name="pre",
    )(tiles_after, mesh_nodes, coarse_nodes, edge_latents, edge_in)

    half = COARSE // 2
    (new_edges, hidden, slope, normed, inverse, own_sum, c_send, c_keep) = pl.pallas_call(
        forward_kernel,
        grid=grid,
        out_shape=(
            far_out((edges, D), BF), far_out((edges, D), BF), far_out((edges, D), BF),
            far_out((edges, D), BF), far_out((edges, 1), F32), sds((OWN, D), F32), sds((half, D), BF), sds((half, D), F32),
        ),
        in_specs=[
            SMEM, SMEM, TILES, tiled(D), tiled(D), whole((HALO, D)), whole((D, D)),
            whole((D, D)), whole((1, D)),
        ],
        out_specs=(
            tiled(D), tiled(D), tiled(D), tiled(D), tiled(1), whole((OWN, D)), whole((half, D)),
            whole((half, D)),
        ),
        scratch_shapes=[
            pltpu.VMEM((HALO, D), BF), pltpu.VMEM((TB, HALO), BF),
            pltpu.VMEM((ROWS, TB), BF), pltpu.VMEM((ROWS, D), F32),
        ],
        compiler_params=params(BIG),
        cost_estimate=cost(4, 16),
        name="forward",
    )(tiles_live, here, edge_tiles, pre, edge_latents, halo, edge_in[1], edge_out, gain_e)

    new_nodes, own_direct, own_slope, own_gain, own_squares = node_call(
        mesh_nodes, own_sum, grad_nodes, node_in, node_out, gain_n, "own", BF
    )
    c = c_keep + swap_core(c_send).astype(F32)
    c, own_gain = tie(scatter_sum(c, me, "z", 0), own_gain)
    c = exchange_sum(c, "x")
    c = exchange_sum(c, "y").astype(BF)
    coarse_total = double(gather(c, me, "z", 0), me)
    new_coarse, coarse_direct, coarse_slope, extra_gain, extra_squares = node_call(
        coarse_nodes, coarse_total, grad_coarse, node_in, node_out, gain_n, "coarse", F32
    )

    edges_grad, pre_slope, gain_sum, e_send, e_keep, even = pl.pallas_call(
        slope_kernel,
        grid=grid,
        out_shape=(
            far_out((edges, D), BF), far_out((edges, D), BF), sds((1, D), F32),
            sds((EARLY // 2 + HALO // 2, D), BF), sds((EARLY // 2, D), BF),
            sds((HALO // 2, D), BF),
        ),
        in_specs=[
            SMEM, SMEM, TILES, tiled(D), tiled(D), tiled(D), tiled(D), tiled(D), tiled(1),
            whole((OWN, D)), whole((COARSE, D)), whole((D, D)), whole((D, D)), whole((1, D)),
            whole((3 * D, D)),
        ],
        out_specs=(
            tiled(D), tiled(D), whole((1, D)), whole((EARLY // 2 + HALO // 2, D)),
            whole((EARLY // 2, D)), whole((HALO // 2, D)),
        ),
        scratch_shapes=[
            pltpu.VMEM((ROWS, D), BF), pltpu.VMEM((TB, ROWS), BF), pltpu.VMEM((HALO, TB), BF),
            pltpu.VMEM((HALO, D), F32), pltpu.VMEM((D, D), F32), pltpu.VMEM((D, D), F32),
        ],
        compiler_params=params(BIG + 8),
        cost_estimate=cost(7, 16),
        name="slope",
    )(
        tiles_live, here, edge_tiles, grad_edges, edge_latents, hidden, slope, normed, inverse,
        own_slope, coarse_slope, edge_in[0], edge_out, gain_e, own_squares,
    )
    swapped = swap_core(e_send)
    early = (e_keep.astype(F32) + swapped[: EARLY // 2].astype(F32)).astype(BF)
    pre_slope, early, back = tie(pre_slope, early, swapped[EARLY // 2 :])
    early = scatter_sum(early, me, "z", 0)
    far = far_route(even, 1)

    l_send, l_keep, own_total = pl.pallas_call(
        scatter_kernel,
        grid=grid,
        out_shape=(sds((LATE // 2, D), BF), sds((LATE // 2, D), BF), sds((OWN, D), F32)),
        in_specs=[
            SMEM, TILES, tiled(D), whole((OWN, D)), whole((OWN, D)), whole((HALO, D)),
            whole((COARSE, D)), whole((3, D, D)), whole((1, D)), whole((1, D)),
        ],
        out_specs=(whole((LATE // 2, D)), whole((LATE // 2, D)), whole((OWN, D))),
        scratch_shapes=[
            pltpu.VMEM((ROWS, TB), BF), pltpu.VMEM((ROWS, TB), BF), pltpu.VMEM((ROWS, D), F32),
            pltpu.VMEM((ROWS, D), F32), pltpu.VMEM((ROWS, D), BF),
        ],
        compiler_params=params(BIG + 8),
        cost_estimate=cost(7, 8),
        name="scatter",
    )(
        here, edge_tiles, pre_slope, own_direct, mesh_nodes, halo, coarse_nodes, edge_in,
        gain_sum, own_gain,
    )

    l_send, l_keep, back, far, early = tie(l_send, l_keep, back, far, early)
    late = (l_keep.astype(F32) + swap_core(l_send).astype(F32)).astype(BF)
    late, early = tie(late, early)
    returned = near_route(even, back, far, me, 1)
    late, returned = tie(scatter_sum(late, me, "x", 0), returned)
    nodes_grad = pl.pallas_call(
        finish_kernel, out_shape=sds((OWN, D), BF), in_specs=[VM] * 4, out_specs=VM,
        name="finish",
    )(lists, returned, own_total, edge_in[1])
    early = exchange_sum(scatter_sum(early, me, "x", 1), "y").astype(BF)
    late = exchange_sum(scatter_sum(late, me, "y", 1), "z").astype(BF)
    early = gather(gather(early, me, "x", 1), me, "z", 0)
    late = gather(gather(late, me, "y", 1), me, "x", 0)

    factor = float(edges * 128) ** (-0.5)
    square = sds((D, D), BF)
    first_grad, out_grad, node_in_grad, node_out_grad = pl.pallas_call(
        functools.partial(early_kernel, factor),
        out_shape=(square, square, sds((2, D, D), BF), square),
        in_specs=[SMEM] + [VM] * 3,
        out_specs=(VM,) * 4,
        compiler_params=params(BIG),
        name="early",
    )(here, early, swap_core(early), extra_squares)
    coarse_grad, in_grad, gain_grad, node_gain_grad = pl.pallas_call(
        functools.partial(late_kernel, factor),
        out_shape=(sds((COARSE, D), BF), sds((3, D, D), BF), sds((1, D), F32), sds((1, D), F32)),
        in_specs=[SMEM] + [VM] * 5,
        out_specs=(VM,) * 4,
        compiler_params=params(BIG),
        name="late",
    )(here, late, swap_core(late), first_grad, coarse_direct, extra_gain)
    return (
        new_nodes, new_coarse, new_edges, nodes_grad, coarse_grad, edges_grad, in_grad, out_grad,
        gain_grad.reshape(D), node_in_grad, node_out_grad, node_gain_grad.reshape(D),
    )


def solution(mesh):
    block = P(AXES, None)
    cube = P(AXES, None, None)
    in_specs = (
        block, P(), block, cube, cube, P(AXES), P(), P(), P(), P(), P(), P(), block, P(), block,
    )
    out_specs = (block, P(), block, block, P(), block, P(), P(), P(), P(), P(), P())
    return jax.shard_map(
        on_device, mesh=mesh, in_specs=in_specs, out_specs=out_specs, check_vma=False
    )
```

```python
import functools

import jax
import jax.numpy as jnp
from jax import lax
from jax.experimental import pallas as pl
from jax.experimental.pallas import tpu as pltpu
from jax.sharding import PartitionSpec as P

EPS = 1e-05
AXES = ("lat", "blk")
BF = jnp.bfloat16
F32 = jnp.float32
D = 512
LANES = 128
TB = 512
BIG = 24

OWN, HALO, COARSE = 320, 64, 640
ROWS = OWN + HALO + COARSE
MOVES = (-3, -2, -1, 1, 2, 3, 32, 64)
EARLY = 5 * D
LATE = 2 * D + COARSE + LANES
GAINS = 2 * D + COARSE
FIRST_COARSE = OWN + HALO


def dot(a, b):
    return jnp.dot(a, b, preferred_element_type=F32)


def dot_tn(a, b):
    return lax.dot_general(a, b, (((0,), (0,)), ((), ())), preferred_element_type=F32)


def dot_nt(a, b):
    return lax.dot_general(a, b, (((1,), (1,)), ((), ())), preferred_element_type=F32)


def receiver_row(row):
    return jnp.where(row < OWN, row, row + HALO)


def onehot_tall(row, count, first=0):
    ids = lax.broadcasted_iota(jnp.int32, (count, LANES), 0) + first
    return jnp.where(ids == row, 1.0, 0.0).astype(BF)


def onehot_wide(row, count, first=0):
    column = jnp.broadcast_to(row, (LANES, LANES)).astype(F32).T.astype(jnp.int32)
    lane = lax.broadcasted_iota(jnp.int32, (LANES, LANES), 1) + first
    width = min(count, LANES)
    parts = [
        jnp.where((column - c)[:, :width] == lane[:, :width], 1.0, 0.0).astype(BF)
        for c in range(0, count, LANES)
    ]
    return parts[0] if len(parts) == 1 else jnp.concatenate(parts, axis=1)


def alive_rows(live, step):
    edge = lax.broadcasted_iota(jnp.int32, (TB, 1), 0) + step * TB
    return jnp.where(edge < live * LANES, 1.0, 0.0).astype(F32)


def normalize(values):
    centered = values - jnp.mean(values, axis=-1, keepdims=True)
    inverse = lax.rsqrt(jnp.mean(centered * centered, axis=-1, keepdims=True) + EPS)
    return centered * inverse, inverse


def normalize_back(upstream, normed, inverse):
    return inverse * (
        upstream
        - jnp.mean(upstream, axis=-1, keepdims=True)
        - normed * jnp.mean(upstream * normed, axis=-1, keepdims=True)
    )


def swish(values):
    sig = 1.0 / (1.0 + jnp.exp(-values))
    return (values * sig).astype(BF), sig * (1.0 + values * (1.0 - sig))


def pre_kernel(tiles, mesh_rows, coarse, edges, weights, pre, proj, hot):
    @pl.when(pl.program_id(0) == 0)
    def _():
        for k, w in enumerate((2, 1)):
            base = k * ROWS
            proj[base : base + OWN] = dot(mesh_rows[...], weights[w]).astype(BF)
            proj[base + OWN : base + FIRST_COARSE] = jnp.zeros((HALO, D), BF)
            proj[base + FIRST_COARSE : base + ROWS] = dot(coarse[...], weights[w]).astype(BF)

    for j in range(TB // LANES):
        at = slice(j * LANES, (j + 1) * LANES)
        hot[at, :ROWS] = onehot_wide(receiver_row(tiles[j, 1:2, :]), ROWS)
        hot[at, ROWS:] = onehot_wide(tiles[j, 0:1, :], ROWS)
    pre[...] = dot(hot[...], proj[...]) + dot(edges[...], weights[0])


def forward_kernel(
    live, me_ref, tiles, pre, edges, halo, w_sender, edge_out, gain,
    new_edges, hidden_o, slope_o, normed_o, inverse_o, own_sum, send, keep,
    proj, hot, hot_t, total,
):
    step = pl.program_id(0)

    @pl.when(step == 0)
    def _():
        proj[...] = dot(halo[...], w_sender[...]).astype(BF)
        total[...] = jnp.zeros_like(total)

    for j in range(TB // LANES):
        at = slice(j * LANES, (j + 1) * LANES)
        hot[at, :] = onehot_wide(tiles[j, 0:1, :], HALO, OWN)
        hot_t[:, at] = onehot_tall(receiver_row(tiles[j, 1:2, :]), ROWS)
    preact = pre[...] + dot(hot[...], proj[...])
    hidden, slope = swish(preact)
    hidden_o[...] = hidden
    slope_o[...] = slope.astype(BF)
    normed, inverse = normalize(dot(hidden, edge_out[...]))
    normed_o[...] = normed.astype(BF)
    inverse_o[...] = inverse
    message = normed * gain[...] * alive_rows(live[0], step)
    new_edges[...] = (edges[...].astype(F32) + message).astype(BF)
    total[...] += dot(hot_t[...], message.astype(BF))

    @pl.when(step == pl.num_programs(0) - 1)
    def _():
        own_sum[...] = total[:OWN]
        middle = FIRST_COARSE + COARSE // 2

        @pl.when(me_ref[0] % 2 == 0)
        def _():
            keep[...] = total[FIRST_COARSE:middle]
            send[...] = total[middle:].astype(BF)

        @pl.when(me_ref[0] % 2 != 0)
        def _():
            keep[...] = total[middle:]
            send[...] = total[FIRST_COARSE:middle].astype(BF)


def node_kernel(
    rows, summed_f, grad, node_in, node_out, gain,
    new_rows, direct, agg_slope, gain_sum, squares,
):
    nodes = rows[...]
    summed = summed_f[...].astype(BF)
    hidden, slope = swish(dot(nodes, node_in[0]) + dot(summed, node_in[1]))
    normed, inverse = normalize(dot(hidden, node_out[...]))
    new_rows[...] = (nodes.astype(F32) + normed * gain[...]).astype(BF)
    grad_f = grad[...].astype(F32)
    gain_sum[...] = jnp.sum(grad_f * normed, axis=0, keepdims=True)
    out_slope = normalize_back(grad_f * gain[...], normed, inverse).astype(BF)
    pre_slope = (dot_nt(out_slope, node_out[...]) * slope).astype(BF)
    agg_slope[...] = dot_nt(pre_slope, node_in[1]).astype(BF)
    direct[...] = grad_f + dot_nt(pre_slope, node_in[0])
    values = (dot_tn(nodes, pre_slope), dot_tn(summed, pre_slope), dot_tn(hidden, out_slope))
    for k, value in enumerate(values):
        squares[k * D : (k + 1) * D] = value.astype(squares.dtype)


def coarse_kernel(rows, summed, grad, node_in, node_out, gain, agg_slope):
    hidden, slope = swish(dot(rows[...], node_in[0]) + dot(summed[...], node_in[1]))
    normed, inverse = normalize(dot(hidden, node_out[...]))
    upstream = grad[...].astype(F32) * gain[...]
    out_slope = normalize_back(upstream, normed, inverse).astype(BF)
    pre_slope = (dot_nt(out_slope, node_out[...]) * slope).astype(BF)
    agg_slope[...] = dot_nt(pre_slope, node_in[1]).astype(BF)


def slope_kernel(
    live, me_ref, tiles, grads, edges, hidden, slope, normed, inverse,
    own_slope, coarse_slope, w_first, edge_out, gain, node_squares,
    edges_grad, pre_slope_o, gain_sum, send, keep, even,
    table, hot, hot_h, halo_total, out_sum, first_sum,
):
    step = pl.program_id(0)

    @pl.when(step == 0)
    def _():
        table[:OWN] = own_slope[...]
        table[OWN:FIRST_COARSE] = jnp.zeros((HALO, D), BF)
        table[FIRST_COARSE:] = coarse_slope[...]
        for ref in (out_sum, first_sum, gain_sum, halo_total):
            ref[...] = jnp.zeros_like(ref)

    for j in range(TB // LANES):
        at = slice(j * LANES, (j + 1) * LANES)
        hot[at, :] = onehot_wide(receiver_row(tiles[j, 1:2, :]), ROWS)
        hot_h[:, at] = onehot_tall(tiles[j, 0:1, :], HALO, OWN)
    grads_f = grads[...].astype(F32)
    normed_f = normed[...].astype(F32)
    message = (grads_f + dot(hot[...], table[...])) * alive_rows(live[0], step)
    gain_sum[...] += jnp.sum(message * normed_f, axis=0, keepdims=True)
    out_slope = normalize_back(message * gain[...], normed_f, inverse[...]).astype(BF)
    out_sum[...] += dot_tn(hidden[...], out_slope)
    pre_slope = (dot_nt(out_slope, edge_out[...]) * slope[...].astype(F32)).astype(BF)
    pre_slope_o[...] = pre_slope
    edges_grad[...] = (grads_f + dot_nt(pre_slope, w_first[...])).astype(BF)
    first_sum[...] += dot_tn(edges[...], pre_slope)
    halo_total[...] += dot(hot_h[...], pre_slope)

    @pl.when(step == pl.num_programs(0) - 1)
    def _():
        core = lax.rem(me_ref[0], 2)
        store_halves(core, send, keep, 0, first_sum[...])
        store_halves(core, send, keep, D, out_sum[...])
        store_halves(core, send, keep, 2 * D, node_squares[...])
        orders = piece_order(1)
        send[EARLY // 2 :] = pieces(halo_total[...], orders[0])
        even[...] = pieces(halo_total[...], orders[1])


def store_halves(core, send, keep, first, value):
    last = first + value.shape[0]
    for half in range(2):
        size = keep.shape[0]
        lo, hi = max(first, half * size), min(last, (half + 1) * size)
        if lo >= hi:
            continue
        rows = value[lo - first : hi - first].astype(BF)
        at = slice(lo - half * size, hi - half * size)

        @pl.when(core == half)
        def _():
            keep[at] = rows

        @pl.when(core != half)
        def _():
            send[at] = rows


def scatter_kernel(
    me_ref, tiles, pre_slope, own_direct, mesh_rows, halo, coarse, weights,
    gain_sum, node_gain_sum,
    send, keep, own_total,
    hot_s, hot_r, s_total, r_total, nodes,
):
    step = pl.program_id(0)

    @pl.when(step == 0)
    def _():
        s_total[...] = jnp.zeros_like(s_total)
        r_total[...] = jnp.zeros_like(r_total)

    for j in range(TB // LANES):
        at = slice(j * LANES, (j + 1) * LANES)
        hot_r[:, at] = onehot_tall(receiver_row(tiles[j, 1:2, :]), ROWS)
        hot_s[:, at] = onehot_tall(tiles[j, 0:1, :], ROWS)
    s_total[...] += dot(hot_s[...], pre_slope[...])
    r_total[...] += dot(hot_r[...], pre_slope[...])

    @pl.when(step == pl.num_programs(0) - 1)
    def _():
        core = lax.rem(me_ref[0], 2)
        nodes[:OWN] = mesh_rows[...]
        nodes[OWN:FIRST_COARSE] = halo[...]
        nodes[FIRST_COARSE:] = coarse[...]
        sent = s_total[...].astype(BF)
        got = r_total[...].astype(BF)
        store_halves(core, send, keep, 0, dot_tn(nodes[...], sent))
        store_halves(core, send, keep, D, dot_tn(nodes[...], got))
        term = dot_nt(sent, weights[1]) + dot_nt(got, weights[2])
        store_halves(core, send, keep, 2 * D, term[FIRST_COARSE:])
        for k, ref in enumerate((gain_sum, node_gain_sum)):
            wide = jnp.broadcast_to(ref[...], (LANES // 2, D))
            store_halves(core, send, keep, GAINS + k * LANES // 2, wide)
        own_total[...] = own_direct[...] + term[:OWN]


def found_rows(mine, other, core, first, count):
    pieces = (mine + other) if core == 0 else (other + mine)
    size = pieces[0].shape[0]
    for c, ref in enumerate(pieces):
        lo, hi = max(first, c * size), min(first + count, (c + 1) * size)
        if lo < hi:
            yield slice(lo - first, hi - first), ref[lo - c * size : hi - c * size].astype(F32)


def early_kernel(
    factor, me_ref, mine, other, extra, first_grad, out_grad, node_in_grad, node_out_grad
):
    def fill(core):
        early = functools.partial(found_rows, (mine,), (other,), core)
        for at, v in early(0, D):
            first_grad[at] = (v * factor).astype(BF)
        for at, v in early(D, D):
            out_grad[at] = (v * factor).astype(BF)
        for k in range(3):
            out = node_out_grad if k == 2 else node_in_grad.at[k]
            for at, v in early((2 + k) * D, D):
                more = extra[k * D + at.start : k * D + at.stop]
                out[at] = ((v + more) * factor).astype(BF)

    by_core(me_ref, fill)


def late_kernel(
    factor, me_ref, mine, other, first_grad, coarse_direct, extra_gain,
    coarse_grad, in_grad, gain_grad, node_gain_grad,
):
    in_grad[0] = first_grad[...]

    def fill(core):
        late = functools.partial(found_rows, (mine,), (other,), core)
        for k in range(2):
            for at, v in late(k * D, D):
                in_grad[k + 1, at] = (v * factor).astype(BF)
        for at, v in late(2 * D, COARSE):
            coarse_grad[at] = (coarse_direct[at] + v).astype(BF)
        for at, v in late(GAINS, 16):
            gain_grad[...] = v[:1] * factor
        for at, v in late(GAINS + LANES // 2, 16):
            node_gain_grad[...] = (v[:1] + extra_gain[...]) * factor

    by_core(me_ref, fill)


def by_core(me_ref, fill):
    for core in range(2):

        @pl.when(lax.rem(me_ref[0], 2) == core)
        def _():
            fill(core)


def piece_order(sign):
    odd = [MOVES.index(sign * offset) for offset in (-3, -1, 1, 3)]
    even = [MOVES.index(sign * offset) for offset in (-2, 2, sign * 32, sign * 64)]
    return odd, even


def pieces(value, order):
    return jnp.concatenate([value[k * 8 : (k + 1) * 8] for k in order]).astype(BF)


def onehot_lists(lists):
    lane = lax.broadcasted_iota(jnp.int32, (8, HALO), 1)
    entry = jnp.zeros((8, HALO), jnp.int32)
    for j in range(8):
        entry += jnp.where(lane % 8 == j, lists[0][:, j : j + 1], 0)
    mine = lax.broadcasted_iota(jnp.int32, (8, HALO), 0) == lane // 8
    row = jnp.sum(jnp.where(mine, entry, 0), axis=0, keepdims=True)
    ids = lax.broadcasted_iota(jnp.int32, (OWN, HALO), 0)
    return jnp.where(ids == row, 1.0, 0.0).astype(BF)


def finish_kernel(lists, returned, own_total, w_sender, out):
    gathered = dot(onehot_lists(lists[...]), returned[...]).astype(BF)
    out[...] = (own_total[...] + dot_nt(gathered, w_sender[...])).astype(BF)


def pick_kernel(lists, mesh_rows, odd, even):
    picked = dot_tn(onehot_lists(lists[...]), mesh_rows[...])
    orders = piece_order(-1)
    odd[...] = pieces(picked, orders[0])
    even[...] = pieces(picked, orders[1])


def whole(shape):
    return pl.BlockSpec(shape, lambda i: (0,) * len(shape))


def tiled(width):
    return pl.BlockSpec((TB, width), lambda i: (i, 0))


TILES = pl.BlockSpec((TB // LANES, 2, LANES), lambda i: (i, 0, 0))
SMEM = pl.BlockSpec(memory_space=pltpu.SMEM)
VM = pl.BlockSpec(memory_space=pltpu.VMEM)


def sds(shape, dtype):
    return jax.ShapeDtypeStruct(shape, dtype)


def far_out(shape, dtype):
    return pltpu.HBM(shape, dtype)


def params(mib):
    return pltpu.CompilerParams(vmem_limit_bytes=mib << 20)


def cost(gflop, mbytes):
    return pl.CostEstimate(
        flops=int(gflop * 1e9), bytes_accessed=int(mbytes * 1e6), transcendentals=0
    )


SHIFT = {"z": 1, "x": 3, "y": 5}


def ring_pairs(axis, offset):
    shift = SHIFT[axis]

    def target(i):
        p = (i >> shift) & 3
        return (i & ~(3 << shift)) | (((p + offset) % 4) << shift)

    return [(i, target(i)) for i in range(128)]


def position(me, axis):
    return (me >> SHIFT[axis]) & 3


def part(x, index, dim):
    size = x.shape[dim] // 4
    return lax.dynamic_slice_in_dim(x, index * size, size, dim)


def swap_core(x):
    return lax.ppermute(x, AXES, [(i, i ^ 1) for i in range(128)])


def double(x, me):
    other = swap_core(x)
    first = (me & 1) == 0
    return jnp.concatenate([jnp.where(first, x, other), jnp.where(first, other, x)])


def scatter_sum(x, me, axis, dim):
    p = position(me, axis)
    got = [
        lax.ppermute(part(x, (p + o) % 4, dim).astype(BF), AXES, ring_pairs(axis, o))
        for o in (2, 1, 3)
    ]
    total = part(x, p, dim).astype(F32)
    for g in got:
        total = total + g.astype(F32)
    return total


def exchange_sum(x, axis):
    x = x.astype(BF)
    far, one, three = [lax.ppermute(x, AXES, ring_pairs(axis, o)) for o in (2, 1, 3)]
    x, far, one, three = [v.astype(F32) for v in (x, far, one, three)]
    return (x + far) + (one + three)


def gather(x, me, axis, dim):
    p = position(me, axis)
    pieces = [x] * 4
    for o in (2, 1, 3):
        pieces[o] = lax.ppermute(x, AXES, ring_pairs(axis, o))
    return jnp.concatenate(
        [lax.select_n((p - j) % 4, *pieces) for j in range(4)], axis=dim
    )


def shift(x, offset):
    return lax.ppermute(x, AXES, [(i, (i + offset) % 128) for i in range(128)])


def far_route(even, sign):
    return tuple(shift(even[8 * k : 8 * k + 8], sign * far) for k, far in ((2, 32), (3, 64)))


def near_shifts(even, swapped, me):
    low = (me & 1) == 0
    minus2, plus2 = [even[8 * k : 8 * k + 8] for k in range(2)]
    minus3, minus1, plus1, plus3 = [swapped[8 * k : 8 * k + 8] for k in range(4)]
    up = shift(jnp.concatenate([plus2, jnp.where(low, plus1, plus3)]), 2)
    down = shift(jnp.concatenate([minus2, jnp.where(low, minus3, minus1)]), -2)
    return up, down


def near_route(even, swapped, up, down, far, me, sign):
    low = (me & 1) == 0
    minus3, minus1, plus1, plus3 = [swapped[8 * k : 8 * k + 8] for k in range(4)]
    pairs = [(i, (i + (4 if i % 2 == 0 else -4)) % 128) for i in range(128)]
    skip = lax.ppermute(jnp.where(low, plus3, minus3), AXES, pairs)
    here = jnp.where(low, minus1, plus1)
    got = {
        2: up[:8],
        -2: down[:8],
        1: jnp.where(low, up[8:], here),
        3: jnp.where(low, skip, up[8:]),
        -3: jnp.where(low, down[8:], skip),
        -1: jnp.where(low, here, down[8:]),
        sign * 32: far[0],
        sign * 64: far[1],
    }
    return jnp.concatenate([got[sign * move] for move in MOVES])


def node_call(rows, summed, grad, node_in, node_out, gain, name, kind):
    n = rows.shape[0]
    return pl.pallas_call(
        node_kernel,
        out_shape=(
            sds((n, D), BF), sds((n, D), F32), sds((n, D), BF), sds((1, D), F32),
            sds((3 * D, D), kind),
        ),
        in_specs=[VM] * 6,
        out_specs=(VM,) * 5,
        compiler_params=params(16),
        cost_estimate=cost(n * 512 * 512 * 2 * 9 / 1e9, 8),
        name=name,
    )(rows, summed, grad, node_in, node_out, gain)


def tie(*values):
    return lax.optimization_barrier(values)


def on_device(
    mesh_nodes, coarse_nodes, edge_latents, edge_tiles, send_lists, tiles_live,
    edge_in, edge_out, edge_gain, node_in, node_out, node_gain,
    grad_nodes, grad_coarse, grad_edges,
):
    me = lax.axis_index(AXES)
    edges = edge_latents.shape[0]
    grid = (edges // TB,)
    lists = send_lists
    gain_e = edge_gain.reshape(1, D)
    gain_n = node_gain.reshape(1, D)

    here = me.reshape(1)
    odd, even = pl.pallas_call(
        pick_kernel, out_shape=(sds((HALO // 2, D), BF),) * 2, in_specs=[VM, VM],
        out_specs=(VM, VM), name="pick",
    )(lists, mesh_nodes)
    far = far_route(even, -1)
    swapped, tiles_after = tie(swap_core(odd), edge_tiles)
    halo = near_route(even, swapped, *near_shifts(even, swapped, me), far, me, -1)

    pre = pl.pallas_call(
        pre_kernel,
        grid=grid,
        out_shape=sds((edges, D), F32),
        in_specs=[TILES, whole((OWN, D)), whole((COARSE, D)), tiled(D), whole((3, D, D))],
        out_specs=tiled(D),
        scratch_shapes=[pltpu.VMEM((2 * ROWS, D), BF), pltpu.VMEM((TB, 2 * ROWS), BF)],
        compiler_params=params(BIG),
        cost_estimate=cost(6.4, 8),
        name="pre",
    )(tiles_after, mesh_nodes, coarse_nodes, edge_latents, edge_in)

    half = COARSE // 2
    (new_edges, hidden, slope, normed, inverse, own_sum, c_send, c_keep) = pl.pallas_call(
        forward_kernel,
        grid=grid,
        out_shape=(
            far_out((edges, D), BF), far_out((edges, D), BF), far_out((edges, D), BF),
            far_out((edges, D), BF), far_out((edges, 1), F32), sds((OWN, D), F32), sds((half, D), BF), sds((half, D), F32),
        ),
        in_specs=[
            SMEM, SMEM, TILES, tiled(D), tiled(D), whole((HALO, D)), whole((D, D)),
            whole((D, D)), whole((1, D)),
        ],
        out_specs=(
            tiled(D), tiled(D), tiled(D), tiled(D), tiled(1), whole((OWN, D)), whole((half, D)),
            whole((half, D)),
        ),
        scratch_shapes=[
            pltpu.VMEM((HALO, D), BF), pltpu.VMEM((TB, HALO), BF),
            pltpu.VMEM((ROWS, TB), BF), pltpu.VMEM((ROWS, D), F32),
        ],
        compiler_params=params(BIG),
        cost_estimate=cost(4, 16),
        name="forward",
    )(tiles_live, here, edge_tiles, pre, edge_latents, halo, edge_in[1], edge_out, gain_e)

    new_nodes, own_direct, own_slope, own_gain, own_squares = node_call(
        mesh_nodes, own_sum, grad_nodes, node_in, node_out, gain_n, "own", BF
    )
    c = c_keep + swap_core(c_send).astype(F32)
    c, own_gain = tie(scatter_sum(c, me, "z", 0), own_gain)
    c = exchange_sum(c, "x")
    c = exchange_sum(c, "y").astype(BF)
    coarse_total = double(gather(c, me, "z", 0), me)
    coarse_slope = pl.pallas_call(
        coarse_kernel,
        out_shape=sds((COARSE, D), BF),
        in_specs=[VM] * 6,
        out_specs=VM,
        compiler_params=params(16),
        cost_estimate=cost(2, 6),
        name="coarse",
    )(coarse_nodes, coarse_total, grad_coarse, node_in, node_out, gain_n)

    edges_grad, pre_slope, gain_sum, e_send, e_keep, even = pl.pallas_call(
        slope_kernel,
        grid=grid,
        out_shape=(
            far_out((edges, D), BF), far_out((edges, D), BF), sds((1, D), F32),
            sds((EARLY // 2 + HALO // 2, D), BF), sds((EARLY // 2, D), BF),
            sds((HALO // 2, D), BF),
        ),
        in_specs=[
            SMEM, SMEM, TILES, tiled(D), tiled(D), tiled(D), tiled(D), tiled(D), tiled(1),
            whole((OWN, D)), whole((COARSE, D)), whole((D, D)), whole((D, D)), whole((1, D)),
            whole((3 * D, D)),
        ],
        out_specs=(
            tiled(D), tiled(D), whole((1, D)), whole((EARLY // 2 + HALO // 2, D)),
            whole((EARLY // 2, D)), whole((HALO // 2, D)),
        ),
        scratch_shapes=[
            pltpu.VMEM((ROWS, D), BF), pltpu.VMEM((TB, ROWS), BF), pltpu.VMEM((HALO, TB), BF),
            pltpu.VMEM((HALO, D), F32), pltpu.VMEM((D, D), F32), pltpu.VMEM((D, D), F32),
        ],
        compiler_params=params(54),
        cost_estimate=cost(7, 16),
        name="slope",
    )(
        tiles_live, here, edge_tiles, grad_edges, edge_latents, hidden, slope, normed, inverse,
        own_slope, coarse_slope, edge_in[0], edge_out, gain_e, own_squares,
    )
    swapped = swap_core(e_send)
    early = (e_keep.astype(F32) + swapped[: EARLY // 2].astype(F32)).astype(BF)
    pre_slope, early, back = tie(pre_slope, early, swapped[EARLY // 2 :])
    early = scatter_sum(early, me, "z", 0)
    far = far_route(even, 1)

    l_send, l_keep, own_total = pl.pallas_call(
        scatter_kernel,
        grid=grid,
        out_shape=(sds((LATE // 2, D), BF), sds((LATE // 2, D), BF), sds((OWN, D), F32)),
        in_specs=[
            SMEM, TILES, tiled(D), whole((OWN, D)), whole((OWN, D)), whole((HALO, D)),
            whole((COARSE, D)), whole((3, D, D)), whole((1, D)), whole((1, D)),
        ],
        out_specs=(whole((LATE // 2, D)), whole((LATE // 2, D)), whole((OWN, D))),
        scratch_shapes=[
            pltpu.VMEM((ROWS, TB), BF), pltpu.VMEM((ROWS, TB), BF), pltpu.VMEM((ROWS, D), F32),
            pltpu.VMEM((ROWS, D), F32), pltpu.VMEM((ROWS, D), BF),
        ],
        compiler_params=params(BIG + 8),
        cost_estimate=cost(7, 8),
        name="scatter",
    )(
        here, edge_tiles, pre_slope, own_direct, mesh_nodes, halo, coarse_nodes, edge_in,
        gain_sum, own_gain,
    )

    new_coarse, coarse_direct, _, extra_gain, extra_squares = node_call(
        coarse_nodes, tie(coarse_total, l_keep)[0], grad_coarse, node_in, node_out, gain_n,
        "rest", F32,
    )
    l_send, l_keep, back, far, early, coarse_direct = tie(
        l_send, l_keep, back, far, early, coarse_direct
    )
    late = (l_keep.astype(F32) + swap_core(l_send).astype(F32)).astype(BF)
    late, early = tie(late, early)
    returned = near_route(even, back, *near_shifts(even, back, me), far, me, 1)
    late, returned = tie(scatter_sum(late, me, "x", 0), returned)
    nodes_grad = pl.pallas_call(
        finish_kernel, out_shape=sds((OWN, D), BF), in_specs=[VM] * 4, out_specs=VM,
        name="finish",
    )(lists, returned, own_total, edge_in[1])
    early = exchange_sum(scatter_sum(early, me, "x", 1), "y").astype(BF)
    late = exchange_sum(scatter_sum(late, me, "y", 1), "z").astype(BF)
    late, nodes_grad = tie(late, nodes_grad)
    early = gather(gather(early, me, "x", 1), me, "z", 0)
    late = gather(gather(late, me, "y", 1), me, "x", 0)

    factor = float(edges * 128) ** (-0.5)
    square = sds((D, D), BF)
    first_grad, out_grad, node_in_grad, node_out_grad = pl.pallas_call(
        functools.partial(early_kernel, factor),
        out_shape=(square, square, sds((2, D, D), BF), square),
        in_specs=[SMEM] + [VM] * 3,
        out_specs=(VM,) * 4,
        compiler_params=params(BIG),
        name="early",
    )(here, early, swap_core(early), extra_squares)
    coarse_grad, in_grad, gain_grad, node_gain_grad = pl.pallas_call(
        functools.partial(late_kernel, factor),
        out_shape=(sds((COARSE, D), BF), sds((3, D, D), BF), sds((1, D), F32), sds((1, D), F32)),
        in_specs=[SMEM] + [VM] * 5,
        out_specs=(VM,) * 4,
        compiler_params=params(BIG),
        name="late",
    )(here, late, swap_core(late), first_grad, coarse_direct, extra_gain)
    return (
        new_nodes, new_coarse, new_edges, nodes_grad, coarse_grad, edges_grad, in_grad, out_grad,
        gain_grad.reshape(D), node_in_grad, node_out_grad, node_gain_grad.reshape(D),
    )


def solution(mesh):
    block = P(AXES, None)
    cube = P(AXES, None, None)
    in_specs = (
        block, P(), block, cube, cube, P(AXES), P(), P(), P(), P(), P(), P(), block, P(), block,
    )
    out_specs = (block, P(), block, block, P(), block, P(), P(), P(), P(), P(), P())
    return jax.shard_map(
        on_device, mesh=mesh, in_specs=in_specs, out_specs=out_specs, check_vma=False
    )
```

```python
import functools

import jax
import jax.numpy as jnp
from jax import lax
from jax.experimental import pallas as pl
from jax.experimental.pallas import tpu as pltpu
from jax.sharding import PartitionSpec as P

EPS = 1e-05
AXES = ("lat", "blk")
BF = jnp.bfloat16
F32 = jnp.float32
D = 512
LANES = 128
TB = 512
BIG = 24

OWN, HALO, COARSE = 320, 64, 640
ROWS = OWN + HALO + COARSE
MOVES = (-3, -2, -1, 1, 2, 3, 32, 64)
EARLY = 5 * D
LATE = 2 * D + COARSE + LANES
GAINS = 2 * D + COARSE
FIRST_COARSE = OWN + HALO


def dot(a, b):
    return jnp.dot(a, b, preferred_element_type=F32)


def dot_tn(a, b):
    return lax.dot_general(a, b, (((0,), (0,)), ((), ())), preferred_element_type=F32)


def dot_nt(a, b):
    return lax.dot_general(a, b, (((1,), (1,)), ((), ())), preferred_element_type=F32)


def receiver_row(row):
    return jnp.where(row < OWN, row, row + HALO)


def onehot_tall(row, count, first=0):
    ids = lax.broadcasted_iota(jnp.int32, (count, LANES), 0) + first
    return jnp.where(ids == row, 1.0, 0.0).astype(BF)


def onehot_wide(row, count, first=0):
    column = jnp.broadcast_to(row, (LANES, LANES)).astype(F32).T.astype(jnp.int32)
    lane = lax.broadcasted_iota(jnp.int32, (LANES, LANES), 1) + first
    width = min(count, LANES)
    parts = [
        jnp.where((column - c)[:, :width] == lane[:, :width], 1.0, 0.0).astype(BF)
        for c in range(0, count, LANES)
    ]
    return parts[0] if len(parts) == 1 else jnp.concatenate(parts, axis=1)


def alive_rows(live, step):
    edge = lax.broadcasted_iota(jnp.int32, (TB, 1), 0) + step * TB
    return jnp.where(edge < live * LANES, 1.0, 0.0).astype(F32)


def normalize(values):
    centered = values - jnp.mean(values, axis=-1, keepdims=True)
    inverse = lax.rsqrt(jnp.mean(centered * centered, axis=-1, keepdims=True) + EPS)
    return centered * inverse, inverse


def normalize_back(upstream, normed, inverse):
    return inverse * (
        upstream
        - jnp.mean(upstream, axis=-1, keepdims=True)
        - normed * jnp.mean(upstream * normed, axis=-1, keepdims=True)
    )


def swish(values):
    sig = 1.0 / (1.0 + jnp.exp(-values))
    return (values * sig).astype(BF), sig * (1.0 + values * (1.0 - sig))


def pre_kernel(tiles, mesh_rows, coarse, edges, weights, pre, proj, hot):
    @pl.when(pl.program_id(0) == 0)
    def _():
        for k, w in enumerate((2, 1)):
            base = k * ROWS
            proj[base : base + OWN] = dot(mesh_rows[...], weights[w]).astype(BF)
            proj[base + OWN : base + FIRST_COARSE] = jnp.zeros((HALO, D), BF)
            proj[base + FIRST_COARSE : base + ROWS] = dot(coarse[...], weights[w]).astype(BF)

    for j in range(TB // LANES):
        at = slice(j * LANES, (j + 1) * LANES)
        hot[at, :ROWS] = onehot_wide(receiver_row(tiles[j, 1:2, :]), ROWS)
        hot[at, ROWS:] = onehot_wide(tiles[j, 0:1, :], ROWS)
    pre[...] = dot(hot[...], proj[...]) + dot(edges[...], weights[0])


def forward_kernel(
    live, me_ref, tiles, pre, edges, halo, w_sender, edge_out, gain,
    new_edges, hidden_o, slope_o, normed_o, inverse_o, own_sum, send, keep,
    proj, hot, hot_t, total,
):
    step = pl.program_id(0)

    @pl.when(step == 0)
    def _():
        proj[...] = dot(halo[...], w_sender[...]).astype(BF)
        total[...] = jnp.zeros_like(total)

    for j in range(TB // LANES):
        at = slice(j * LANES, (j + 1) * LANES)
        hot[at, :] = onehot_wide(tiles[j, 0:1, :], HALO, OWN)
        hot_t[:, at] = onehot_tall(receiver_row(tiles[j, 1:2, :]), ROWS)
    preact = pre[...] + dot(hot[...], proj[...])
    hidden, slope = swish(preact)
    hidden_o[...] = hidden
    slope_o[...] = slope.astype(BF)
    normed, inverse = normalize(dot(hidden, edge_out[...]))
    normed_o[...] = normed.astype(BF)
    inverse_o[...] = inverse
    message = normed * gain[...] * alive_rows(live[0], step)
    new_edges[...] = (edges[...].astype(F32) + message).astype(BF)
    total[...] += dot(hot_t[...], message.astype(BF))

    @pl.when(step == pl.num_programs(0) - 1)
    def _():
        own_sum[...] = total[:OWN]
        middle = FIRST_COARSE + COARSE // 2

        @pl.when(me_ref[0] % 2 == 0)
        def _():
            keep[...] = total[FIRST_COARSE:middle]
            send[...] = total[middle:].astype(BF)

        @pl.when(me_ref[0] % 2 != 0)
        def _():
            keep[...] = total[middle:]
            send[...] = total[FIRST_COARSE:middle].astype(BF)


def node_kernel(
    rows, summed_f, grad, node_in, node_out, gain,
    new_rows, direct, agg_slope, gain_sum, squares,
):
    nodes = rows[...]
    summed = summed_f[...].astype(BF)
    hidden, slope = swish(dot(nodes, node_in[0]) + dot(summed, node_in[1]))
    normed, inverse = normalize(dot(hidden, node_out[...]))
    new_rows[...] = (nodes.astype(F32) + normed * gain[...]).astype(BF)
    grad_f = grad[...].astype(F32)
    gain_sum[...] = jnp.sum(grad_f * normed, axis=0, keepdims=True)
    out_slope = normalize_back(grad_f * gain[...], normed, inverse).astype(BF)
    pre_slope = (dot_nt(out_slope, node_out[...]) * slope).astype(BF)
    agg_slope[...] = dot_nt(pre_slope, node_in[1]).astype(BF)
    direct[...] = grad_f + dot_nt(pre_slope, node_in[0])
    values = (dot_tn(nodes, pre_slope), dot_tn(summed, pre_slope), dot_tn(hidden, out_slope))
    for k, value in enumerate(values):
        squares[k * D : (k + 1) * D] = value.astype(squares.dtype)


def coarse_kernel(rows, summed, grad, node_in, node_out, gain, agg_slope):
    hidden, slope = swish(dot(rows[...], node_in[0]) + dot(summed[...], node_in[1]))
    normed, inverse = normalize(dot(hidden, node_out[...]))
    upstream = grad[...].astype(F32) * gain[...]
    out_slope = normalize_back(upstream, normed, inverse).astype(BF)
    pre_slope = (dot_nt(out_slope, node_out[...]) * slope).astype(BF)
    agg_slope[...] = dot_nt(pre_slope, node_in[1]).astype(BF)


def slope_kernel(
    live, me_ref, tiles, grads, edges, hidden, slope, normed, inverse,
    own_slope, coarse_slope, w_first, edge_out, gain, node_squares,
    edges_grad, pre_slope_o, gain_sum, send, keep, even,
    table, hot, hot_h, halo_total, out_sum, first_sum,
):
    step = pl.program_id(0)

    @pl.when(step == 0)
    def _():
        table[:OWN] = own_slope[...]
        table[OWN:FIRST_COARSE] = jnp.zeros((HALO, D), BF)
        table[FIRST_COARSE:] = coarse_slope[...]
        for ref in (out_sum, first_sum, gain_sum, halo_total):
            ref[...] = jnp.zeros_like(ref)

    for j in range(TB // LANES):
        at = slice(j * LANES, (j + 1) * LANES)
        hot[at, :] = onehot_wide(receiver_row(tiles[j, 1:2, :]), ROWS)
        hot_h[:, at] = onehot_tall(tiles[j, 0:1, :], HALO, OWN)
    grads_f = grads[...].astype(F32)
    normed_f = normed[...].astype(F32)
    message = (grads_f + dot(hot[...], table[...])) * alive_rows(live[0], step)
    gain_sum[...] += jnp.sum(message * normed_f, axis=0, keepdims=True)
    out_slope = normalize_back(message * gain[...], normed_f, inverse[...]).astype(BF)
    out_sum[...] += dot_tn(hidden[...], out_slope)
    pre_slope = (dot_nt(out_slope, edge_out[...]) * slope[...].astype(F32)).astype(BF)
    pre_slope_o[...] = pre_slope
    edges_grad[...] = (grads_f + dot_nt(pre_slope, w_first[...])).astype(BF)
    first_sum[...] += dot_tn(edges[...], pre_slope)
    halo_total[...] += dot(hot_h[...], pre_slope)

    @pl.when(step == pl.num_programs(0) - 1)
    def _():
        core = lax.rem(me_ref[0], 2)
        store_halves(core, send, keep, 0, first_sum[...])
        store_halves(core, send, keep, D, out_sum[...])
        store_halves(core, send, keep, 2 * D, node_squares[...])
        orders = piece_order(1)
        send[EARLY // 2 :] = pieces(halo_total[...], orders[0])
        even[...] = pieces(halo_total[...], orders[1])


def store_halves(core, send, keep, first, value):
    last = first + value.shape[0]
    for half in range(2):
        size = keep.shape[0]
        lo, hi = max(first, half * size), min(last, (half + 1) * size)
        if lo >= hi:
            continue
        rows = value[lo - first : hi - first].astype(BF)
        at = slice(lo - half * size, hi - half * size)

        @pl.when(core == half)
        def _():
            keep[at] = rows

        @pl.when(core != half)
        def _():
            send[at] = rows


def scatter_kernel(
    me_ref, tiles, pre_slope, own_direct, mesh_rows, halo, coarse, weights,
    gain_sum, node_gain_sum,
    send, keep, own_total,
    hot_s, hot_r, s_total, r_total, nodes,
):
    step = pl.program_id(0)

    @pl.when(step == 0)
    def _():
        s_total[...] = jnp.zeros_like(s_total)
        r_total[...] = jnp.zeros_like(r_total)

    for j in range(TB // LANES):
        at = slice(j * LANES, (j + 1) * LANES)
        hot_r[:, at] = onehot_tall(receiver_row(tiles[j, 1:2, :]), ROWS)
        hot_s[:, at] = onehot_tall(tiles[j, 0:1, :], ROWS)
    s_total[...] += dot(hot_s[...], pre_slope[...])
    r_total[...] += dot(hot_r[...], pre_slope[...])

    @pl.when(step == pl.num_programs(0) - 1)
    def _():
        core = lax.rem(me_ref[0], 2)
        nodes[:OWN] = mesh_rows[...]
        nodes[OWN:FIRST_COARSE] = halo[...]
        nodes[FIRST_COARSE:] = coarse[...]
        sent = s_total[...].astype(BF)
        got = r_total[...].astype(BF)
        store_halves(core, send, keep, 0, dot_tn(nodes[...], sent))
        store_halves(core, send, keep, D, dot_tn(nodes[...], got))
        term = dot_nt(sent, weights[1]) + dot_nt(got, weights[2])
        store_halves(core, send, keep, 2 * D, term[FIRST_COARSE:])
        for k, ref in enumerate((gain_sum, node_gain_sum)):
            wide = jnp.broadcast_to(ref[...], (LANES // 2, D))
            store_halves(core, send, keep, GAINS + k * LANES // 2, wide)
        own_total[...] = own_direct[...] + term[:OWN]


def found_rows(mine, other, core, first, count):
    pieces = (mine + other) if core == 0 else (other + mine)
    size = pieces[0].shape[0]
    for c, ref in enumerate(pieces):
        lo, hi = max(first, c * size), min(first + count, (c + 1) * size)
        if lo < hi:
            yield slice(lo - first, hi - first), ref[lo - c * size : hi - c * size].astype(F32)


def early_kernel(
    factor, me_ref, mine, other, extra, first_grad, out_grad, node_in_grad, node_out_grad
):
    def fill(core):
        early = functools.partial(found_rows, (mine,), (other,), core)
        for at, v in early(0, D):
            first_grad[at] = (v * factor).astype(BF)
        for at, v in early(D, D):
            out_grad[at] = (v * factor).astype(BF)
        for k in range(3):
            out = node_out_grad if k == 2 else node_in_grad.at[k]
            for at, v in early((2 + k) * D, D):
                more = extra[k * D + at.start : k * D + at.stop]
                out[at] = ((v + more) * factor).astype(BF)

    by_core(me_ref, fill)


def late_kernel(
    factor, me_ref, mine, other, first_grad, coarse_direct, extra_gain,
    coarse_grad, in_grad, gain_grad, node_gain_grad,
):
    in_grad[0] = first_grad[...]

    def fill(core):
        late = functools.partial(found_rows, (mine,), (other,), core)
        for k in range(2):
            for at, v in late(k * D, D):
                in_grad[k + 1, at] = (v * factor).astype(BF)
        for at, v in late(2 * D, COARSE):
            coarse_grad[at] = (coarse_direct[at] + v).astype(BF)
        for at, v in late(GAINS, 16):
            gain_grad[...] = v[:1] * factor
        for at, v in late(GAINS + LANES // 2, 16):
            node_gain_grad[...] = (v[:1] + extra_gain[...]) * factor

    by_core(me_ref, fill)


def by_core(me_ref, fill):
    for core in range(2):

        @pl.when(lax.rem(me_ref[0], 2) == core)
        def _():
            fill(core)


def piece_order(sign):
    odd = [MOVES.index(sign * offset) for offset in (-3, -1, 1, 3)]
    even = [MOVES.index(sign * offset) for offset in (-2, 2, sign * 32, sign * 64)]
    return odd, even


def pieces(value, order):
    return jnp.concatenate([value[k * 8 : (k + 1) * 8] for k in order]).astype(BF)


def onehot_lists(lists):
    lane = lax.broadcasted_iota(jnp.int32, (8, HALO), 1)
    entry = jnp.zeros((8, HALO), jnp.int32)
    for j in range(8):
        entry += jnp.where(lane % 8 == j, lists[0][:, j : j + 1], 0)
    mine = lax.broadcasted_iota(jnp.int32, (8, HALO), 0) == lane // 8
    row = jnp.sum(jnp.where(mine, entry, 0), axis=0, keepdims=True)
    ids = lax.broadcasted_iota(jnp.int32, (OWN, HALO), 0)
    return jnp.where(ids == row, 1.0, 0.0).astype(BF)


def finish_kernel(lists, returned, own_total, w_sender, out):
    gathered = dot(onehot_lists(lists[...]), returned[...]).astype(BF)
    out[...] = (own_total[...] + dot_nt(gathered, w_sender[...])).astype(BF)


def pick_kernel(lists, mesh_rows, odd, even):
    picked = dot_tn(onehot_lists(lists[...]), mesh_rows[...])
    orders = piece_order(-1)
    odd[...] = pieces(picked, orders[0])
    even[...] = pieces(picked, orders[1])


def whole(shape):
    return pl.BlockSpec(shape, lambda i: (0,) * len(shape))


def one_of(k):
    return pl.BlockSpec((None, D, D), lambda *_: (k, 0, 0))


def tiled(width):
    return pl.BlockSpec((TB, width), lambda i: (i, 0))


TILES = pl.BlockSpec((TB // LANES, 2, LANES), lambda i: (i, 0, 0))
SMEM = pl.BlockSpec(memory_space=pltpu.SMEM)
VM = pl.BlockSpec(memory_space=pltpu.VMEM)


def sds(shape, dtype):
    return jax.ShapeDtypeStruct(shape, dtype)


def far_out(shape, dtype):
    return pltpu.HBM(shape, dtype)


def params(mib):
    return pltpu.CompilerParams(vmem_limit_bytes=mib << 20)


def cost(gflop, mbytes):
    return pl.CostEstimate(
        flops=int(gflop * 1e9), bytes_accessed=int(mbytes * 1e6), transcendentals=0
    )


SHIFT = {"z": 1, "x": 3, "y": 5}


def ring_pairs(axis, offset):
    shift = SHIFT[axis]

    def target(i):
        p = (i >> shift) & 3
        return (i & ~(3 << shift)) | (((p + offset) % 4) << shift)

    return [(i, target(i)) for i in range(128)]


def position(me, axis):
    return (me >> SHIFT[axis]) & 3


def part(x, index, dim):
    size = x.shape[dim] // 4
    return lax.dynamic_slice_in_dim(x, index * size, size, dim)


def swap_core(x):
    return lax.ppermute(x, AXES, [(i, i ^ 1) for i in range(128)])


def double(x, me):
    other = swap_core(x)
    first = (me & 1) == 0
    return jnp.concatenate([jnp.where(first, x, other), jnp.where(first, other, x)])


def scatter_sum(x, me, axis, dim):
    p = position(me, axis)
    got = [
        lax.ppermute(part(x, (p + o) % 4, dim).astype(BF), AXES, ring_pairs(axis, o))
        for o in (2, 1, 3)
    ]
    total = part(x, p, dim).astype(F32)
    for g in got:
        total = total + g.astype(F32)
    return total


def exchange_sum(x, axis):
    x = x.astype(BF)
    far, one, three = [lax.ppermute(x, AXES, ring_pairs(axis, o)) for o in (2, 1, 3)]
    x, far, one, three = [v.astype(F32) for v in (x, far, one, three)]
    return (x + far) + (one + three)


def gather(x, me, axis, dim):
    p = position(me, axis)
    pieces = [x] * 4
    for o in (2, 1, 3):
        pieces[o] = lax.ppermute(x, AXES, ring_pairs(axis, o))
    return jnp.concatenate(
        [lax.select_n((p - j) % 4, *pieces) for j in range(4)], axis=dim
    )


def shift(x, offset):
    return lax.ppermute(x, AXES, [(i, (i + offset) % 128) for i in range(128)])


def far_route(even, sign):
    return tuple(shift(even[8 * k : 8 * k + 8], sign * far) for k, far in ((2, 32), (3, 64)))


def near_shifts(even, swapped, me):
    low = (me & 1) == 0
    minus2, plus2 = [even[8 * k : 8 * k + 8] for k in range(2)]
    minus3, minus1, plus1, plus3 = [swapped[8 * k : 8 * k + 8] for k in range(4)]
    up = shift(jnp.concatenate([plus2, jnp.where(low, plus1, plus3)]), 2)
    down = shift(jnp.concatenate([minus2, jnp.where(low, minus3, minus1)]), -2)
    return up, down


def near_route(even, swapped, up, down, far, me, sign):
    low = (me & 1) == 0
    minus3, minus1, plus1, plus3 = [swapped[8 * k : 8 * k + 8] for k in range(4)]
    pairs = [(i, (i + (4 if i % 2 == 0 else -4)) % 128) for i in range(128)]
    skip = lax.ppermute(jnp.where(low, plus3, minus3), AXES, pairs)
    here = jnp.where(low, minus1, plus1)
    got = {
        2: up[:8],
        -2: down[:8],
        1: jnp.where(low, up[8:], here),
        3: jnp.where(low, skip, up[8:]),
        -3: jnp.where(low, down[8:], skip),
        -1: jnp.where(low, here, down[8:]),
        sign * 32: far[0],
        sign * 64: far[1],
    }
    return jnp.concatenate([got[sign * move] for move in MOVES])


def node_call(rows, summed, grad, node_in, node_out, gain, name, kind):
    n = rows.shape[0]
    return pl.pallas_call(
        node_kernel,
        out_shape=(
            sds((n, D), BF), sds((n, D), F32), sds((n, D), BF), sds((1, D), F32),
            sds((3 * D, D), kind),
        ),
        in_specs=[VM] * 6,
        out_specs=(VM,) * 5,
        compiler_params=params(16),
        cost_estimate=cost(n * 512 * 512 * 2 * 9 / 1e9, 8),
        name=name,
    )(rows, summed, grad, node_in, node_out, gain)


def tie(*values):
    return lax.optimization_barrier(values)


def on_device(
    mesh_nodes, coarse_nodes, edge_latents, edge_tiles, send_lists, tiles_live,
    edge_in, edge_out, edge_gain, node_in, node_out, node_gain,
    grad_nodes, grad_coarse, grad_edges,
):
    me = lax.axis_index(AXES)
    edges = edge_latents.shape[0]
    grid = (edges // TB,)
    lists = send_lists
    gain_e = edge_gain.reshape(1, D)
    gain_n = node_gain.reshape(1, D)

    here = me.reshape(1)
    odd, even = pl.pallas_call(
        pick_kernel, out_shape=(sds((HALO // 2, D), BF),) * 2, in_specs=[VM, VM],
        out_specs=(VM, VM), name="pick",
    )(lists, mesh_nodes)
    far = far_route(even, -1)
    swapped, tiles_after = tie(swap_core(odd), edge_tiles)
    halo = near_route(even, swapped, *near_shifts(even, swapped, me), far, me, -1)

    pre = pl.pallas_call(
        pre_kernel,
        grid=grid,
        out_shape=sds((edges, D), F32),
        in_specs=[TILES, whole((OWN, D)), whole((COARSE, D)), tiled(D), whole((3, D, D))],
        out_specs=tiled(D),
        scratch_shapes=[pltpu.VMEM((2 * ROWS, D), BF), pltpu.VMEM((TB, 2 * ROWS), BF)],
        compiler_params=params(BIG),
        cost_estimate=cost(6.4, 8),
        name="pre",
    )(tiles_after, mesh_nodes, coarse_nodes, edge_latents, edge_in)

    half = COARSE // 2
    (new_edges, hidden, slope, normed, inverse, own_sum, c_send, c_keep) = pl.pallas_call(
        forward_kernel,
        grid=grid,
        out_shape=(
            far_out((edges, D), BF), far_out((edges, D), BF), far_out((edges, D), BF),
            far_out((edges, D), BF), far_out((edges, 1), F32), sds((OWN, D), F32), sds((half, D), BF), sds((half, D), F32),
        ),
        in_specs=[
            SMEM, SMEM, TILES, tiled(D), tiled(D), whole((HALO, D)), one_of(1),
            whole((D, D)), whole((1, D)),
        ],
        out_specs=(
            tiled(D), tiled(D), tiled(D), tiled(D), tiled(1), whole((OWN, D)), whole((half, D)),
            whole((half, D)),
        ),
        scratch_shapes=[
            pltpu.VMEM((HALO, D), BF), pltpu.VMEM((TB, HALO), BF),
            pltpu.VMEM((ROWS, TB), BF), pltpu.VMEM((ROWS, D), F32),
        ],
        compiler_params=params(BIG),
        cost_estimate=cost(4, 16),
        name="forward",
    )(tiles_live, here, edge_tiles, pre, edge_latents, halo, edge_in, edge_out, gain_e)

    new_nodes, own_direct, own_slope, own_gain, own_squares = node_call(
        mesh_nodes, own_sum, grad_nodes, node_in, node_out, gain_n, "own", BF
    )
    c = c_keep + swap_core(c_send).astype(F32)
    c, own_gain = tie(scatter_sum(c, me, "z", 0), own_gain)
    c = exchange_sum(c, "x")
    c = exchange_sum(c, "y").astype(BF)
    coarse_total = double(gather(c, me, "z", 0), me)
    coarse_slope = pl.pallas_call(
        coarse_kernel,
        out_shape=sds((COARSE, D), BF),
        in_specs=[VM] * 6,
        out_specs=VM,
        compiler_params=params(16),
        cost_estimate=cost(2, 6),
        name="coarse",
    )(coarse_nodes, coarse_total, grad_coarse, node_in, node_out, gain_n)

    edges_grad, pre_slope, gain_sum, e_send, e_keep, even = pl.pallas_call(
        slope_kernel,
        grid=grid,
        out_shape=(
            far_out((edges, D), BF), far_out((edges, D), BF), sds((1, D), F32),
            sds((EARLY // 2 + HALO // 2, D), BF), sds((EARLY // 2, D), BF),
            sds((HALO // 2, D), BF),
        ),
        in_specs=[
            SMEM, SMEM, TILES, tiled(D), tiled(D), tiled(D), tiled(D), tiled(D), tiled(1),
            whole((OWN, D)), whole((COARSE, D)), one_of(0), whole((D, D)), whole((1, D)),
            whole((3 * D, D)),
        ],
        out_specs=(
            tiled(D), tiled(D), whole((1, D)), whole((EARLY // 2 + HALO // 2, D)),
            whole((EARLY // 2, D)), whole((HALO // 2, D)),
        ),
        scratch_shapes=[
            pltpu.VMEM((ROWS, D), BF), pltpu.VMEM((TB, ROWS), BF), pltpu.VMEM((HALO, TB), BF),
            pltpu.VMEM((HALO, D), F32), pltpu.VMEM((D, D), F32), pltpu.VMEM((D, D), F32),
        ],
        compiler_params=params(54),
        cost_estimate=cost(7, 16),
        name="slope",
    )(
        tiles_live, here, edge_tiles, grad_edges, edge_latents, hidden, slope, normed, inverse,
        own_slope, coarse_slope, edge_in, edge_out, gain_e, own_squares,
    )
    swapped = swap_core(e_send)
    early = (e_keep.astype(F32) + swapped[: EARLY // 2].astype(F32)).astype(BF)
    pre_slope, early, back = tie(pre_slope, early, swapped[EARLY // 2 :])
    early = scatter_sum(early, me, "z", 0)
    far = far_route(even, 1)

    l_send, l_keep, own_total = pl.pallas_call(
        scatter_kernel,
        grid=grid,
        out_shape=(sds((LATE // 2, D), BF), sds((LATE // 2, D), BF), sds((OWN, D), F32)),
        in_specs=[
            SMEM, TILES, tiled(D), whole((OWN, D)), whole((OWN, D)), whole((HALO, D)),
            whole((COARSE, D)), whole((3, D, D)), whole((1, D)), whole((1, D)),
        ],
        out_specs=(whole((LATE // 2, D)), whole((LATE // 2, D)), whole((OWN, D))),
        scratch_shapes=[
            pltpu.VMEM((ROWS, TB), BF), pltpu.VMEM((ROWS, TB), BF), pltpu.VMEM((ROWS, D), F32),
            pltpu.VMEM((ROWS, D), F32), pltpu.VMEM((ROWS, D), BF),
        ],
        compiler_params=params(BIG + 8),
        cost_estimate=cost(7, 8),
        name="scatter",
    )(
        here, edge_tiles, pre_slope, own_direct, mesh_nodes, halo, coarse_nodes, edge_in,
        gain_sum, own_gain,
    )

    new_coarse, coarse_direct, _, extra_gain, extra_squares = node_call(
        coarse_nodes, tie(coarse_total, l_keep)[0], grad_coarse, node_in, node_out, gain_n,
        "rest", F32,
    )
    l_send, l_keep, back, far, early, coarse_direct = tie(
        l_send, l_keep, back, far, early, coarse_direct
    )
    late = (l_keep.astype(F32) + swap_core(l_send).astype(F32)).astype(BF)
    late, early = tie(late, early)
    returned = near_route(even, back, *near_shifts(even, back, me), far, me, 1)
    late, returned = tie(scatter_sum(late, me, "x", 0), returned)
    nodes_grad = pl.pallas_call(
        finish_kernel, grid=(1,), out_shape=sds((OWN, D), BF),
        in_specs=[whole((1, 8, 8)), whole((HALO, D)), whole((OWN, D)), one_of(1)],
        out_specs=whole((OWN, D)), name="finish",
    )(lists, returned, own_total, edge_in)
    early = exchange_sum(scatter_sum(early, me, "x", 1), "y").astype(BF)
    late = exchange_sum(scatter_sum(late, me, "y", 1), "z").astype(BF)
    late, nodes_grad = tie(late, nodes_grad)
    early = gather(gather(early, me, "x", 1), me, "z", 0)
    late = gather(gather(late, me, "y", 1), me, "x", 0)

    factor = float(edges * 128) ** (-0.5)
    square = sds((D, D), BF)
    first_grad, out_grad, node_in_grad, node_out_grad = pl.pallas_call(
        functools.partial(early_kernel, factor),
        out_shape=(square, square, sds((2, D, D), BF), square),
        in_specs=[SMEM] + [VM] * 3,
        out_specs=(VM,) * 4,
        compiler_params=params(BIG),
        name="early",
    )(here, early, swap_core(early), extra_squares)
    coarse_grad, in_grad, gain_grad, node_gain_grad = pl.pallas_call(
        functools.partial(late_kernel, factor),
        out_shape=(sds((COARSE, D), BF), sds((3, D, D), BF), sds((1, D), F32), sds((1, D), F32)),
        in_specs=[SMEM] + [VM] * 5,
        out_specs=(VM,) * 4,
        compiler_params=params(BIG),
        name="late",
    )(here, late, swap_core(late), first_grad, coarse_direct, extra_gain)
    return (
        new_nodes, new_coarse, new_edges, nodes_grad, coarse_grad, edges_grad, in_grad, out_grad,
        gain_grad.reshape(D), node_in_grad, node_out_grad, node_gain_grad.reshape(D),
    )


def solution(mesh):
    block = P(AXES, None)
    cube = P(AXES, None, None)
    in_specs = (
        block, P(), block, cube, cube, P(AXES), P(), P(), P(), P(), P(), P(), block, P(), block,
    )
    out_specs = (block, P(), block, block, P(), block, P(), P(), P(), P(), P(), P())
    return jax.shard_map(
        on_device, mesh=mesh, in_specs=in_specs, out_specs=out_specs, check_vma=False
    )
```
